128 devices in a mesh: span: 8 (over x_lo, z), tensor: 16 (over x_hi, y, core).
Axes of the slice: x: 4 (x_hi: 2, x_lo: 2; x = x_hi * 2 + x_lo), y: 4, z: 4, core: 2. Of those that a mesh axis runs over, the one named last changes fastest.
Arguments:
- inputs: bfloat16 [8192, 2048], P('span'), may hold values from -6 to 6
- out_grad: bfloat16 [8192, 2048], P('span'), may hold values from -6 to 6
- lengths: int32 [2, 3], replicated, may hold values from 1 to 2560, 4096 in all within a row
- span_order: int32 [64], replicated, may hold values from 0 to 63, as said below
- w_query: bfloat16 [2048, 2048], P('span', 'tensor'), may hold values from -0.125 to 0.125
- w_key: bfloat16 [2048, 1024], P('span', 'tensor'), may hold values from -0.125 to 0.125
- w_value: bfloat16 [2048, 1024], P('span', 'tensor'), may hold values from -0.125 to 0.125
- w_out: bfloat16 [2048, 2048], P('tensor', 'span'), may hold values from -4 to 4
- w_gate: bfloat16 [2048, 6144], P('span', 'tensor'), may hold values from -0.125 to 0.125
- w_up: bfloat16 [2048, 6144], P('span', 'tensor'), may hold values from -0.125 to 0.125
- w_down: bfloat16 [6144, 2048], P('tensor', 'span'), may hold values from -0.078125 to 0.078125
- norm_attn: bfloat16 [2048], P('span'), may hold values from 0.5 to 1.5
- norm_mlp: bfloat16 [2048], P('span'), may hold values from 0.5 to 1.5
- norm_query: bfloat16 [128], P('span'), may hold values from 0.5 to 1.5
- norm_key: bfloat16 [128], P('span'), may hold values from 0.5 to 1.5
Outputs:
- layer_out: float32 [8192, 2048], P('span', 'tensor')
- in_grad: float32 [8192, 2048], P('span', 'tensor')
- grad_query: float32 [2048, 2048], P('span', 'tensor')
- grad_key: float32 [2048, 1024], P('span', 'tensor')
- grad_value: float32 [2048, 1024], P('span', 'tensor')
- grad_out: float32 [2048, 2048], P('tensor', 'span')
- grad_gate: float32 [2048, 6144], P('span', 'tensor')
- grad_up: float32 [2048, 6144], P('span', 'tensor')
- grad_down: float32 [6144, 2048], P('tensor', 'span')
- grad_norm_attn: float32 [2048], P('span')
- grad_norm_mlp: float32 [2048], P('span')
- grad_norm_query: float32 [128], P('span')
- grad_norm_key: float32 [128], P('span')
The draws below stay inside these ranges and needn't reach their ends.
Inputs may be any that keep to these rules, and one draw needn't show every extreme that they name: Row m holds the lengths of the documents of micro-batch m, laid end to end from its first token; each row sums to 4096. `span_order`: every span number appears exactly once; slot s lies on index s // 8 of span.
All inputs are finite; a program needn't handle non-finite values.
Results may differ from the reference program's by a relative error of at most 0.035.
Values may be sent and summed in bfloat16 or wider, within the bound.
No kernel may reach another device: no remote copies, remote signals or barrier semaphores. Data moves between devices by JAX's collectives and lax.ppermute only.
A program may use at most 192 MiB of HBM per device.

```python
import math
import jax
import jax.numpy as jnp
import numpy as np
from jax import lax

D = 2048
HQ = 16
KV = 8
HD = 128
FF = 6144
SPAN = 128
MICRO = 2
DOCS = 3
NCHUNKS = 64
TOKENS = 8192
MB_TOK = 4096
MOST = 2560


def draw_span_order(key, part):
    key = jax.random.fold_in(key, 11)
    paired = jax.random.permutation(key, NCHUNKS // 2).astype(jnp.int32)
    return jnp.stack([paired, NCHUNKS - 1 - paired], axis=1).reshape(NCHUNKS).astype(jnp.int32)


def steps_of(stream_key, shape, shards, least, largest):
    loudness = 1.0
    for position, blocks in shards:
        heights = jax.random.uniform(jax.random.fold_in(jax.random.fold_in(stream_key, 6), position), (blocks,), jnp.float32, least / len(shards), largest / len(shards))
        loudness = loudness * jnp.repeat(jnp.exp(heights), shape[position] // blocks).reshape((-1,) + (1,) * (len(shape) - 1 - position))
    return loudness


def split_up(amount, total, most, slope):
    loads = [(1 << 20) // math.isqrt(grade ** slope) + 1 for grade in range(2, amount + 1)]
    surplus, holding = total - most - (amount - 1), [1] * (amount - 1)
    while surplus > 0:
        candidates = [i for i in range(amount - 1) if holding[i] < most]
        pool, remaining = sum([loads[i] for i in candidates]), surplus
        for i in candidates:
            extra = min(most - holding[i], max(1, remaining * loads[i] // pool), surplus)
            holding[i] = holding[i] + extra
            surplus = surplus - extra
    return np.array([most] + holding)


def ragged(stream_key, amount, total, bound, lean):
    if amount == 2:
        one = jax.random.randint(stream_key, (), max(1, total - bound), min(bound, total - 1) + 1)
        return jnp.stack([one, total - one])
    sizes = jnp.asarray(split_up(amount, total, bound, lean), jnp.int32)
    couples = (amount - 1) // 2
    giver, sink = sizes[1:1 + 2 * couples:2], sizes[2:2 + 2 * couples:2]
    margin = jnp.minimum(giver - 1, bound - sink)
    moved = jax.random.randint(jax.random.fold_in(stream_key, 1), (couples,), 0, 1 << 20) % (margin + 1)
    sizes = sizes.at[1:1 + 2 * couples:2].set(giver - moved).at[2:2 + 2 * couples:2].set(sink + moved)
    return sizes[jax.random.permutation(jax.random.fold_in(stream_key, 2), amount)]


def bell_draw(stream_key, shape, width, limit, cuts=(), kind=jnp.bfloat16):
    result = jax.random.normal(stream_key, shape, jnp.float32) * width
    if len(cuts) > 0:
        result = steps_of(stream_key, shape, cuts, -0.22, 0.18) * result
    return jnp.clip(result, min=-limit, max=limit).astype(kind)


def setup_inputs(seed: int = 0) -> dict:
    key_list = jax.random.split(jax.random.key(seed), 16)
    return {
        "inputs": bell_draw(key_list[0], (TOKENS, D), 1.0, 6.0, ((0, 8),)),
        "out_grad": bell_draw(key_list[1], (TOKENS, D), 1.0, 6.0, ((0, 8),)),
        "lengths": jax.vmap(lambda own: ragged(own, DOCS, MB_TOK, MOST, 0))(jax.random.split(key_list[2], MICRO)).reshape((MICRO, DOCS)).astype(jnp.int32),
        "span_order": draw_span_order(jax.random.fold_in(key_list[15], 71), 0),
        "w_query": bell_draw(key_list[4], (D, HQ * HD), D ** -0.5, 0.125, ((0, 8), (1, 16))),
        "w_key": bell_draw(key_list[5], (D, KV * HD), D ** -0.5, 0.125, ((0, 8), (1, 16))),
        "w_value": bell_draw(key_list[6], (D, KV * HD), D ** -0.5, 0.125, ((0, 8), (1, 16))),
        "w_out": bell_draw(key_list[7], (HQ * HD, D), (HQ * HD * 4 // MB_TOK) ** -0.5, 4.0, ((0, 16), (1, 8))),
        "w_gate": bell_draw(key_list[8], (D, FF), D ** -0.5, 0.125, ((0, 8), (1, 16))),
        "w_up": bell_draw(key_list[9], (D, FF), D ** -0.5, 0.125, ((0, 8), (1, 16))),
        "w_down": bell_draw(key_list[10], (FF, D), FF ** -0.5, 0.078125, ((0, 16), (1, 8))),
        "norm_attn": jnp.clip(1.0 + 0.1 * jax.random.normal(key_list[11], (D,), jnp.float32), 0.5, 1.5).astype(jnp.bfloat16),
        "norm_mlp": jnp.clip(1.0 + 0.1 * jax.random.normal(key_list[12], (D,), jnp.float32), 0.5, 1.5).astype(jnp.bfloat16),
        "norm_query": jnp.clip(1.0 + 0.1 * jax.random.normal(key_list[13], (HD,), jnp.float32), 0.5, 1.5).astype(jnp.bfloat16),
        "norm_key": jnp.clip(1.0 + 0.1 * jax.random.normal(key_list[14], (HD,), jnp.float32), 0.5, 1.5).astype(jnp.bfloat16),
    }


epsilon = 1e-06
rope_base = 1000000.0
neg_large = -1e+30
highest = lax.Precision.HIGHEST

@jax.custom_vjp
def low(v):
    return lax.optimization_barrier(v.astype(jnp.bfloat16)).astype(jnp.float32)

@jax.custom_vjp
def low_back(v):
    return v

def low_keep(v):
    return (low(v), None)

def low_pass(kept, grad):
    return (grad,)

def back_keep(v):
    return (v, None)

def back_low(kept, grad):
    return (low(grad),)
low.defvjp(low_keep, low_pass)
low_back.defvjp(back_keep, back_low)

def matmul(first_op, second_op):
    return jnp.dot(first_op, second_op, precision=highest, preferred_element_type=jnp.float32)

def rms_scale(values, gain_vector):
    return values * lax.rsqrt(lax.optimization_barrier(jnp.mean(values * values, axis=-1, keepdims=True)) + epsilon) * gain_vector

def rotate(values, cos_table, sin_table):
    middle = values.shape[-1] // 2
    former = values[..., :middle]
    latter = values[..., middle:]
    return jnp.concatenate([former * cos_table - latter * sin_table, latter * cos_table + former * sin_table], axis=-1)

def token_layout(lengths, tokens):
    batch_of = tokens // MB_TOK
    offset = tokens % MB_TOK
    doc_ends = jnp.cumsum(lengths, axis=1, dtype=jnp.int32)
    row_ends = jnp.take(doc_ends, batch_of, axis=0)
    row_lengths = jnp.take(lengths, batch_of, axis=0)
    document = lax.optimization_barrier(jnp.sum((offset[:, None] >= row_ends).astype(jnp.int32), axis=1, dtype=jnp.int32))
    picker = jnp.arange(DOCS, dtype=jnp.int32)[None, :] == document[:, None]
    doc_start = lax.optimization_barrier(jnp.sum(jnp.where(picker, row_ends - row_lengths, 0), axis=1, dtype=jnp.int32))
    return ((batch_of * DOCS + document).astype(jnp.int32), (offset - doc_start).astype(jnp.int32))

def rope_tables(positions, head_size):
    frequency = jnp.power(rope_base, -2.0 * jnp.arange(head_size // 2, dtype=jnp.float32) / head_size)
    angles = positions.astype(jnp.float32)[:, None] * frequency[None, :]
    return (jnp.cos(angles), jnp.sin(angles))

def attend(packed):
    query_heads, key_heads, value_heads, documents = packed
    scores = jnp.einsum('tkgd,skd->kgts', query_heads, key_heads, precision=highest) * HD ** (-0.5)
    scores = low_back(scores)
    places = jnp.arange(MB_TOK, dtype=jnp.int32)
    allowed = (places[:, None] >= places[None, :]) & (documents[:, None] == documents[None, :])
    scores = jnp.where(allowed[None, None], scores, neg_large)
    weights = jax.nn.softmax(scores, axis=-1)
    return low(low_back(jnp.einsum('kgts,skd->tkgd', low(weights), value_heads, precision=highest)))

def forward(inputs, w_query, w_key, w_value, w_out, w_gate, w_up, w_down, norm_attn, norm_mlp, norm_query, norm_key, cos_table, sin_table, documents, span_order):
    normed = low(rms_scale(inputs, norm_attn))
    query_heads = low_back(matmul(normed, w_query)).reshape(TOKENS, KV, HQ // KV, HD)
    key_heads = low_back(matmul(normed, w_key)).reshape(TOKENS, KV, HD)
    value_heads = low(low_back(matmul(normed, w_value))).reshape(TOKENS, KV, HD)
    query_heads = low(rotate(rms_scale(query_heads, norm_query), cos_table[:, None, None, :], sin_table[:, None, None, :]))
    key_heads = low(rotate(rms_scale(key_heads, norm_key), cos_table[:, None, :], sin_table[:, None, :]))
    attended = lax.map(jax.checkpoint(attend), (query_heads.reshape(MICRO, MB_TOK, KV, HQ // KV, HD), key_heads.reshape(MICRO, MB_TOK, KV, HD), value_heads.reshape(MICRO, MB_TOK, KV, HD), documents.reshape(MICRO, MB_TOK)))
    attn_branch = low_back(matmul(attended.reshape(TOKENS, HQ * HD), w_out))
    hidden = inputs + attn_branch
    normed_mlp = low(rms_scale(hidden, norm_mlp))
    gate_proj = low_back(matmul(normed_mlp, w_gate))
    upward = low_back(matmul(normed_mlp, w_up))
    activated = low(jax.nn.silu(gate_proj) * upward)
    block_out = hidden + low_back(matmul(activated, w_down))
    return jnp.take(block_out.reshape(NCHUNKS, SPAN, D), span_order, axis=0).reshape(TOKENS, D)

def reference(inputs, out_grad, lengths, span_order, w_query, w_key, w_value, w_out, w_gate, w_up, w_down, norm_attn, norm_mlp, norm_query, norm_key):
    documents, positions = token_layout(lengths, jnp.arange(TOKENS, dtype=jnp.int32))
    cos_table, sin_table = rope_tables(positions, HD)
    params = tuple((entry.astype(jnp.float32) for entry in (inputs, w_query, w_key, w_value, w_out, w_gate, w_up, w_down, norm_attn, norm_mlp, norm_query, norm_key)))

    def wrapped(*arrays):
        return forward(*arrays, cos_table, sin_table, documents, span_order)
    layer_out, pullback = jax.vjp(wrapped, *params)
    gradients = pullback(out_grad.astype(jnp.float32))
    return (layer_out, gradients[0], gradients[1], gradients[2], gradients[3], gradients[4], gradients[5], gradients[6], gradients[7], gradients[8], gradients[9], gradients[10], gradients[11])
```

```python
import jax
import jax.numpy as jnp
from jax import lax
from jax.experimental import pallas as pl
from jax.experimental.pallas import tpu as pltpu
from jax.sharding import Mesh, PartitionSpec as P

SPAN = 128
MICRO = 2
HD = 128
D = 2048
ROWS = 1024
KEYS = 4096
BLK = 256

epsilon = 1e-06
rope_base = 1000000.0
score_scale = HD ** (-0.5)
log2e = 1.4426950408889634
bf16 = jnp.bfloat16
f32 = jnp.float32
SPANS = ("xl", "z")
TENSOR = ("xh", "y", "c")
CHIPS = ("xh", "y")
VMEM_LIMIT = 48 * 1024 * 1024


def swap(block):
    return lax.ppermute(block, "c", [(0, 1), (1, 0)])


def cross(block):
    return lax.ppermute(block, "xh", [(0, 1), (1, 0)])


def shift(block, axis, by):
    return lax.ppermute(block, axis, [(i, (i + by) % 4) for i in range(4)])


def onward(block, by):
    return lax.ppermute(block, "z", [(i, i + by) for i in range(4) if i + by < 4])


def backward(block, by):
    return lax.ppermute(block, "z", [(i, i - by) for i in range(4) if i - by >= 0])


def exchange(block, axes):
    return lax.all_to_all(block, axes, 0, 0, tiled=True)


def spread(block, axes, count):
    return exchange(jnp.broadcast_to(block[None], (count,) + block.shape), axes)


def plain_dot(first_op, second_op):
    return jnp.dot(first_op, second_op, preferred_element_type=f32)


def left_dot(first_op, second_op):
    return lax.dot_general(
        first_op, second_op, (((0,), (0,)), ((), ())), preferred_element_type=f32
    )


def right_dot(first_op, second_op):
    return lax.dot_general(
        first_op, second_op, (((1,), (1,)), ((), ())), preferred_element_type=f32
    )


def inverse_rms(values):
    return lax.rsqrt(jnp.mean(values * values, axis=-1, keepdims=True) + epsilon)


def rotate(values, cos_table, sin_table):
    former, latter = values[..., :64], values[..., 64:]
    return jnp.concatenate(
        [former * cos_table - latter * sin_table, latter * cos_table + former * sin_table], axis=-1
    )


def rotate_back(values, cos_table, sin_table):
    former, latter = values[..., :64], values[..., 64:]
    return jnp.concatenate(
        [former * cos_table + latter * sin_table, latter * cos_table - former * sin_table], axis=-1
    )


def norm_back(incoming, normal, inverse):
    return inverse * (incoming - normal * jnp.mean(incoming * normal, axis=-1, keepdims=True))


def block_mask(block, key_block, starts):
    key_at = key_block * BLK + lax.broadcasted_iota(jnp.int32, (BLK, BLK), 0)
    query_at = (KEYS - ROWS) + block * BLK + lax.broadcasted_iota(jnp.int32, (BLK, BLK), 1)
    return (key_at >= starts) & (key_at <= query_at)


def attend_kernel(low_ref, start_ref, q_ref, k_ref, v_ref, out_ref, full_ref, total_ref):
    for block in range(ROWS // BLK):
        cols = pl.ds(block * BLK, BLK)
        queries = q_ref[cols, :]
        starts = start_ref[:, cols]

        def step(key_block, state):
            acc, total = state
            rows = pl.ds(pl.multiple_of(key_block * BLK, BLK), BLK)
            scores = right_dot(k_ref[rows, :], queries) * (score_scale * log2e)
            weights = jnp.where(block_mask(block, key_block, starts), jnp.exp2(scores), 0.0)
            total = total + jnp.sum(weights, axis=0, keepdims=True)
            acc = acc + left_dot(v_ref[rows, :], weights.astype(bf16))
            return acc, total

        acc, total = lax.fori_loop(
            low_ref[block],
            (KEYS - ROWS) // BLK + block + 1,
            step,
            (jnp.zeros((HD, BLK), f32), jnp.zeros((1, BLK), f32)),
        )
        full = acc / total
        full_ref[:, cols] = full
        total_ref[:, cols] = jnp.log2(total)
        out_ref[cols, :] = full.T.astype(bf16)


def attend(low, starts, queries, keys, values):
    vmem = pl.BlockSpec(memory_space=pltpu.VMEM)
    return pl.pallas_call(
        attend_kernel,
        out_shape=(
            jax.ShapeDtypeStruct((ROWS, HD), bf16),
            jax.ShapeDtypeStruct((HD, ROWS), f32),
            jax.ShapeDtypeStruct((1, ROWS), f32),
        ),
        in_specs=[pl.BlockSpec(memory_space=pltpu.SMEM)] + [vmem] * 4,
        out_specs=(vmem,) * 3,
        compiler_params=pltpu.CompilerParams(vmem_limit_bytes=VMEM_LIMIT),
        cost_estimate=pl.CostEstimate(
            flops=4 * ROWS * 2048 * HD, bytes_accessed=4 << 20, transcendentals=ROWS * 2048
        ),
        name="attend",
    )(low, starts, queries, keys, values)


def attend_back_kernel(
    low_ref,
    core_ref,
    start_ref,
    q_ref,
    k_ref,
    v_ref,
    do_ref,
    full_ref,
    total_ref,
    dq_ref,
    keep_ref,
    send_ref,
    dk_ref,
    dv_ref,
):
    dk_ref[...] = jnp.zeros_like(dk_ref)
    dv_ref[...] = jnp.zeros_like(dv_ref)
    for block in range(ROWS // BLK):
        cols = pl.ds(block * BLK, BLK)
        queries = q_ref[cols, :]
        starts = start_ref[:, cols]
        incoming = do_ref[cols, :]
        total = total_ref[:, cols]
        delta = jnp.sum(incoming.astype(f32).T * full_ref[:, cols], axis=0, keepdims=True)

        def step(key_block, acc):
            rows = pl.ds(pl.multiple_of(key_block * BLK, BLK), BLK)
            keys = k_ref[rows, :]
            scores = right_dot(keys, queries) * (score_scale * log2e)
            weights = jnp.where(
                block_mask(block, key_block, starts), jnp.exp2(scores - total), 0.0
            )
            grads = right_dot(v_ref[rows, :], incoming)
            grads = (weights * (grads - delta)).astype(bf16)
            dv_ref[rows, :] += plain_dot(weights.astype(bf16), incoming)
            dk_ref[rows, :] += plain_dot(grads, queries)
            return acc + left_dot(keys, grads)

        acc = lax.fori_loop(
            low_ref[block],
            (KEYS - ROWS) // BLK + block + 1,
            step,
            jnp.zeros((HD, BLK), f32),
        )
        dq_ref[cols, :] = acc.T * score_scale

    @pl.when(core_ref[0] == 0)
    def _():
        keep_ref[...] = dk_ref[...] * score_scale
        send_ref[...] = dv_ref[...].astype(bf16)

    @pl.when(core_ref[0] == 1)
    def _():
        keep_ref[...] = dv_ref[...]
        send_ref[...] = (dk_ref[...] * score_scale).astype(bf16)


def attend_back(low, core, starts, queries, keys, values, incoming, full, total):
    vmem = pl.BlockSpec(memory_space=pltpu.VMEM)
    smem = pl.BlockSpec(memory_space=pltpu.SMEM)
    return pl.pallas_call(
        attend_back_kernel,
        out_shape=(
            jax.ShapeDtypeStruct((ROWS, HD), f32),
            jax.ShapeDtypeStruct((KEYS, HD), f32),
            jax.ShapeDtypeStruct((KEYS, HD), bf16),
        ),
        in_specs=[smem, smem] + [vmem] * 7,
        out_specs=(vmem,) * 3,
        scratch_shapes=[pltpu.VMEM((KEYS, HD), f32), pltpu.VMEM((KEYS, HD), f32)],
        compiler_params=pltpu.CompilerParams(vmem_limit_bytes=VMEM_LIMIT),
        cost_estimate=pl.CostEstimate(
            flops=10 * ROWS * 2048 * HD, bytes_accessed=8 << 20, transcendentals=ROWS * 2048
        ),
        name="attend_back",
    )(low, core, starts, queries, keys, values, incoming, full, total)


def pick_kernel(index_ref, source_ref, out_ref):
    out_ref[...] = source_ref[...].astype(out_ref.dtype)


def pick(index, source):
    count, (rows, width) = index.shape[0], source.shape[1:]
    return pl.pallas_call(
        pick_kernel,
        out_shape=jax.ShapeDtypeStruct((count, rows, width), f32),
        grid_spec=pltpu.PrefetchScalarGridSpec(
            num_scalar_prefetch=1,
            grid=(count,),
            in_specs=[pl.BlockSpec((1, rows, width), lambda i, index_ref: (index_ref[i], 0, 0))],
            out_specs=pl.BlockSpec((1, rows, width), lambda i, index_ref: (i, 0, 0)),
        ),
        name="pick",
    )(index, source)


def body(
    inputs,
    out_grad,
    lengths,
    span_order,
    w_query,
    w_key,
    w_value,
    w_out,
    w_gate,
    w_up,
    w_down,
    norm_attn,
    norm_mlp,
    norm_query,
    norm_key,
):
    xl, z, xh, y, core = (lax.axis_index(name) for name in ("xl", "z", "xh", "y", "c"))
    span_place = xl * 4 + z
    tensor_place = (xh * 4 + y) * 2 + core
    first = core == 0

    def own_rows(block):
        wide = block.reshape(8, 16, 8, D)
        return lax.dynamic_index_in_dim(wide, tensor_place, 1, keepdims=False).reshape(64, D)

    other_half = swap(jnp.where(first, w_value, w_key))
    own_half = jnp.where(first, w_key, w_value)
    kv_shard = jnp.where(
        first,
        jnp.concatenate([own_half, other_half], 1),
        jnp.concatenate([other_half, own_half], 1),
    )
    gains = jnp.concatenate([norm_attn, norm_mlp, norm_query, norm_key])
    gains = jnp.pad(gains, (0, 16 * 384 - 544)).reshape(16, 384)
    shard = jnp.concatenate(
        [jnp.concatenate([w_query, kv_shard, w_out.T], axis=1), gains], axis=0
    )
    spread_weights = spread(shard, SPANS, 8)
    attn_weights = spread_weights[:, :256].reshape(D, 384)
    gains = spread_weights[:, 256:258].reshape(8, 768).astype(f32)
    gain_attn = gains[:, :256].reshape(D)
    gain_mlp = gains[:, 256:512].reshape(D)
    gain_query = gains[:, 512:528].reshape(HD)
    gain_key = gains[:, 528:544].reshape(HD)
    qkv_weights = attn_weights[:, :256]
    out_weights = attn_weights[:, 256:]

    slot_rows = lax.all_gather(own_rows(out_grad), SPANS, axis=0, tiled=True)
    mlp_weights = lax.all_gather(
        jnp.concatenate([w_gate, w_up, w_down.T], axis=1), SPANS, axis=0, tiled=True
    )
    gate_up_weights = mlp_weights[:, :768]
    down_weights = mlp_weights[:, 768:]

    ends = jnp.cumsum(lax.dynamic_index_in_dim(lengths, xl, 0, keepdims=False))
    offset = z * ROWS + jnp.arange(ROWS, dtype=jnp.int32)
    doc_start = jnp.where(offset >= ends[1], ends[1], jnp.where(offset >= ends[0], ends[0], 0))
    frequency = jnp.power(rope_base, -2.0 * jnp.arange(HD // 2, dtype=f32) / HD)
    angles = (offset - doc_start).astype(f32)[:, None] * frequency[None, :]
    cos_table, sin_table = jnp.cos(angles), jnp.sin(angles)
    starts = doc_start - (z - 3) * ROWS
    low = starts.reshape(ROWS // BLK, BLK)[:, 0] // BLK
    starts = starts.reshape(1, ROWS)

    rows_in = inputs.astype(f32)
    inverse_one = inverse_rms(rows_in)
    normal_one = rows_in * inverse_one
    normed = (normal_one * gain_attn).astype(bf16)
    proj = plain_dot(normed, qkv_weights)
    query_proj, kv_proj = proj[:, :HD], proj[:, HD:]
    query_inv = inverse_rms(query_proj)
    query_hat = query_proj * query_inv
    query_bf = rotate(query_hat * gain_query, cos_table, sin_table).astype(bf16)
    key_inv = inverse_rms(kv_proj)
    key_hat = kv_proj * key_inv
    key_rot = rotate(key_hat * gain_key, cos_table, sin_table)
    mine = jnp.where(first, key_rot, kv_proj).astype(bf16)
    mine = jnp.concatenate([onward(mine, 3), onward(mine, 2), onward(mine, 1), mine], axis=0)
    other = swap(mine)
    all_keys = jnp.where(first, mine, other)
    all_values = jnp.where(first, other, mine)

    out_mine = jnp.concatenate(
        [
            out_weights,
            shift(out_weights, "y", 1),
            shift(out_weights, "y", -1),
            shift(out_weights, "y", 2),
        ],
        axis=1,
    )
    out_wide = jnp.concatenate([out_mine, swap(out_mine)], axis=1)
    near = jnp.stack([y, y + 3, y + 1, y + 2]) % 4
    order = jnp.concatenate([near * 2 + core, near * 2 + (1 - core)])
    head = jnp.arange(8, dtype=jnp.int32)
    place = jnp.array([0, 2, 3, 1], jnp.int32)[(head // 2 - y) % 4]
    order_back = place + jnp.where(head % 2 == core, 0, 4)

    slots = span_place * 8 + jnp.arange(8, dtype=jnp.int32)
    hit = (slots[:, None] == span_order[None, :]).astype(bf16)
    own_grad = plain_dot(hit, slot_rows.reshape(64, 8 * D)).astype(bf16).reshape(64, D)

    def gather_rows(block):
        near_rows = spread(block, CHIPS, 8).reshape(512, D)
        return near_rows, swap(near_rows)

    grad_mine, grad_other = gather_rows(own_grad)

    attended, attended_full, total = attend(low, starts, query_bf, all_keys, all_values)
    by_rows = attended.reshape(8, 2, 4, 2, 8, HD).transpose(2, 3, 1, 0, 4, 5).reshape(8, 128, HD)
    by_rows = jnp.take(exchange(by_rows, ("y", "c")), order, axis=0)
    by_rows = by_rows.transpose(1, 0, 2).reshape(128, 8 * HD)
    branch = right_dot(by_rows, out_wide).reshape(2, 64, D)
    sent = lax.dynamic_index_in_dim(branch, 1 - xh, 0, keepdims=False).astype(bf16)
    kept = lax.dynamic_index_in_dim(branch, xh, 0, keepdims=False)
    hidden = own_rows(inputs).astype(f32) + (kept + cross(sent).astype(f32))
    inverse_two = inverse_rms(hidden)
    normal_two = hidden * inverse_two
    normed_mlp = (normal_two * gain_mlp).astype(bf16)
    normed_mine, normed_other = gather_rows(normed_mlp)

    def feed(normed_rows, grad_rows):
        wide = plain_dot(normed_rows, gate_up_weights)
        gate, up = wide[:, :384], wide[:, 384:]
        sigma = jax.nn.sigmoid(gate)
        silu = gate * sigma
        activated = (silu * up).astype(bf16)
        grad_act = plain_dot(grad_rows, down_weights)
        grad_gate = grad_act * up * sigma * (1.0 + gate * (1.0 - sigma))
        grad_up = grad_act * silu
        grad_wide = jnp.concatenate([grad_gate.astype(bf16), grad_up.astype(bf16)], axis=1)
        return activated, grad_wide

    act_mine, wide_mine = feed(normed_mine, grad_mine)
    act_other, wide_other = feed(normed_other, grad_other)
    part_other = right_dot(wide_other, gate_up_weights).astype(bf16)
    part_mine = right_dot(wide_mine, gate_up_weights)
    part = (part_mine + swap(part_other).astype(f32)).astype(bf16)
    grad_normed_mlp = jnp.sum(
        exchange(part.reshape(8, 64, D), CHIPS).astype(f32), axis=0
    )

    grad_mlp_weights = jnp.concatenate(
        [
            left_dot(normed_mine, wide_mine) + left_dot(normed_other, wide_other),
            left_dot(grad_mine, act_mine) + left_dot(grad_other, act_other),
        ],
        axis=1,
    ).astype(bf16)
    grad_mlp_weights = lax.psum_scatter(
        grad_mlp_weights, SPANS, scatter_dimension=0, tiled=True
    ).astype(f32)

    chip_place = xh * 4 + y
    out_mine_rows = right_dot(act_mine, down_weights)
    own_block = lax.dynamic_slice_in_dim(out_mine_rows, chip_place * 64, 64, 0) + hidden
    out_mine_rows = lax.dynamic_update_slice_in_dim(out_mine_rows, own_block, chip_place * 64, 0)
    out_other_rows = right_dot(act_other, down_weights)
    out_cols = jnp.stack([out_mine_rows.astype(bf16), out_other_rows.astype(bf16)])
    out_cols = out_cols.reshape(2, 512, 8, 2, 128)
    sent = lax.dynamic_index_in_dim(out_cols, 1 - core, 3, keepdims=False)
    kept = lax.dynamic_index_in_dim(out_cols, core, 3, keepdims=False)
    came = swap(sent)[::-1]
    out_cols = (kept.astype(f32) + came.astype(f32)).astype(bf16)
    out_cols = out_cols.reshape(1024, 8, 128).transpose(1, 0, 2)
    out_cols = jnp.sum(exchange(out_cols, CHIPS).astype(f32), axis=0).astype(bf16)
    out_cols = out_cols.reshape(2, 8, 8, 8, 128)
    out_cols = jnp.where(first, out_cols, out_cols[::-1])
    out_cols = out_cols.transpose(2, 1, 0, 3, 4).reshape(8, 128, 128)
    every_span = lax.all_gather(out_cols, SPANS, axis=0, tiled=True)
    own_spans = lax.dynamic_slice_in_dim(span_order, span_place * 8, 8, 0)
    layer_out = pick(own_spans, every_span).reshape(ROWS, 128)

    gain_mlp_part = jnp.sum(grad_normed_mlp * normal_two, axis=0)
    grad_hidden = own_grad.astype(f32) + norm_back(
        grad_normed_mlp * gain_mlp, normal_two, inverse_two
    )
    grad_branch = grad_hidden.astype(bf16)
    across = cross(grad_branch)
    both = jnp.where(
        xh == 0,
        jnp.concatenate([grad_branch, across], 0),
        jnp.concatenate([across, grad_branch], 0),
    )
    grad_att = plain_dot(both, out_wide).astype(bf16)
    grad_att = grad_att.reshape(128, 8, HD).transpose(1, 0, 2)
    grad_att = exchange(jnp.take(grad_att, order_back, axis=0), ("y", "c"))
    grad_att = (
        grad_att.reshape(4, 2, 2, 8, 8, HD).transpose(3, 2, 0, 1, 4, 5).reshape(ROWS, HD)
    )

    grad_query_rot, keep, send = attend_back(
        low,
        core.reshape(1),
        starts,
        query_bf,
        all_keys,
        all_values,
        grad_att,
        attended_full,
        total,
    )
    grad_kv = (keep + swap(send).astype(f32)).reshape(4, ROWS, HD)
    away = grad_kv.astype(bf16)
    grad_kv = (
        grad_kv[3]
        + backward(away[2], 1).astype(f32)
        + backward(away[1], 2).astype(f32)
        + backward(away[0], 3).astype(f32)
    )
    query_norm_grad = rotate_back(grad_query_rot, cos_table, sin_table)
    gain_query_part = jnp.sum(query_norm_grad * query_hat, axis=0)
    grad_query_proj = norm_back(query_norm_grad * gain_query, query_hat, query_inv)
    key_norm_grad = rotate_back(grad_kv, cos_table, sin_table)
    gain_key_part = jnp.where(first, jnp.sum(key_norm_grad * key_hat, axis=0), 0.0)
    grad_key_proj = norm_back(key_norm_grad * gain_key, key_hat, key_inv)
    grad_kv_proj = jnp.where(first, grad_key_proj, grad_kv)
    grad_proj = jnp.concatenate([grad_query_proj.astype(bf16), grad_kv_proj.astype(bf16)], axis=1)

    part = right_dot(grad_proj, qkv_weights)
    weighted = part * normal_one
    gain_attn_part = jnp.sum(weighted, axis=0)
    row_term = jnp.sum(weighted * gain_attn, axis=1) * (1.0 / D)
    by_cols = part.astype(bf16).reshape(ROWS, 8, 2, 128)
    sent = lax.dynamic_index_in_dim(by_cols, 1 - core, 2, keepdims=False)
    kept = lax.dynamic_index_in_dim(by_cols, core, 2, keepdims=False)
    by_cols = (kept.astype(f32) + swap(sent).astype(f32)).astype(bf16).transpose(1, 0, 2)
    row_term = row_term.reshape(8, 128)
    row_term = row_term + swap(row_term)
    coarse = row_term.astype(bf16)
    fine = (row_term - coarse.astype(f32)).astype(bf16)
    extra = jnp.concatenate([coarse, fine], axis=0)
    by_cols = jnp.concatenate([by_cols, jnp.broadcast_to(extra[None], (8, 16, 128))], axis=1)
    by_cols = jnp.sum(exchange(by_cols, CHIPS).astype(f32), axis=0)
    row_term = (by_cols[ROWS : ROWS + 8] + by_cols[ROWS + 8 :]).reshape(ROWS, 1)
    grad_normed = by_cols[:ROWS]
    own_cols = lax.dynamic_slice_in_dim(inputs, tensor_place * 128, 128, 1).astype(f32)
    own_gain = lax.dynamic_slice_in_dim(gain_attn, tensor_place * 128, 128, 0)
    hidden_cols = exchange(grad_branch.reshape(64, 16, 128).transpose(1, 0, 2), TENSOR)
    hidden_cols = hidden_cols.reshape(16, 8, 8, 128).transpose(1, 0, 2, 3).reshape(ROWS, 128)
    in_grad = hidden_cols.astype(f32) + inverse_one * (
        grad_normed * own_gain - own_cols * inverse_one * row_term
    )

    branch_mine, branch_other = gather_rows(grad_branch)
    att_rows = attended.reshape(8, 8, 2, 8, HD).transpose(2, 1, 0, 3, 4).reshape(2, 512, HD)
    att_mine = jnp.where(first, att_rows[0], att_rows[1])
    att_other = jnp.where(first, att_rows[1], att_rows[0])
    grad_out = left_dot(branch_mine, att_mine) + left_dot(branch_other, att_other)
    grad_attn = jnp.concatenate(
        [left_dot(normed, grad_proj).astype(bf16), grad_out.astype(bf16)], axis=1
    ).reshape(8, 256, 384)
    gain_parts = jnp.concatenate(
        [
            gain_attn_part.reshape(8, 256),
            gain_mlp_part.reshape(8, 256),
            gain_query_part.reshape(8, 16),
            gain_key_part.reshape(8, 16),
        ],
        axis=1,
    ).astype(bf16)
    gain_parts = jnp.pad(gain_parts, ((0, 0), (0, 16 * 384 - 544))).reshape(8, 16, 384)
    grad_attn = jnp.concatenate([grad_attn, gain_parts], axis=1)
    grad_attn = jnp.sum(exchange(grad_attn, SPANS).astype(f32), axis=0)
    gain_sums = grad_attn[256:259].reshape(9, 128)[:8]
    gain_sums = jnp.sum(spread(gain_sums, TENSOR, 16), axis=0).reshape(-1)
    grad_attn = grad_attn[:256]
    grad_kv_weight = grad_attn[:, 128:256]
    low_half, high_half = grad_kv_weight[:, :64], grad_kv_weight[:, 64:]
    came = swap(jnp.where(first, high_half, low_half))
    kept = jnp.where(first, low_half, high_half)

    return (
        layer_out,
        in_grad,
        grad_attn[:, :128],
        jnp.where(first, kept, came),
        jnp.where(first, came, kept),
        grad_attn[:, 256:].T,
        grad_mlp_weights[:, :384],
        grad_mlp_weights[:, 384:768],
        grad_mlp_weights[:, 768:].T,
        gain_sums[:256],
        gain_sums[256:512],
        gain_sums[512:528],
        gain_sums[528:544],
    )


def solution(mesh):
    fine = Mesh(mesh.devices.reshape(2, 4, 2, 4, 2), ("xl", "z", "xh", "y", "c"))
    rows = P(SPANS, None)
    by_both = P(SPANS, TENSOR)
    turned = P(TENSOR, SPANS)
    lone = P(SPANS)
    return jax.shard_map(
        body,
        mesh=fine,
        in_specs=(
            rows,
            rows,
            P(),
            P(),
            by_both,
            by_both,
            by_both,
            turned,
            by_both,
            by_both,
            turned,
            lone,
            lone,
            lone,
            lone,
        ),
        out_specs=(
            by_both,
            by_both,
            by_both,
            by_both,
            by_both,
            turned,
            by_both,
            by_both,
            turned,
            lone,
            lone,
            lone,
            lone,
        ),
        check_vma=False,
    )
```

```python
import jax
import jax.numpy as jnp
from jax import lax
from jax.experimental import pallas as pl
from jax.experimental.pallas import tpu as pltpu
from jax.sharding import Mesh, PartitionSpec as P

SPAN = 128
MICRO = 2
HD = 128
D = 2048
ROWS = 1024
KEYS = 4096
BLK = 256
KEY_BLK = 512

epsilon = 1e-06
rope_base = 1000000.0
score_scale = HD ** (-0.5)
log2e = 1.4426950408889634
bf16 = jnp.bfloat16
f32 = jnp.float32
SPANS = ("xl", "z")
TENSOR = ("xh", "y", "c")
CHIPS = ("xh", "y")
MIB = 1024 * 1024


def swap(block):
    return lax.ppermute(block, "c", [(0, 1), (1, 0)])


def far_span(block):
    return lax.ppermute(block, "xl", [(0, 1), (1, 0)])


def onward(block, by):
    return lax.ppermute(block, "z", [(i, i + by) for i in range(4) if i + by < 4])


def backward(block, by):
    return lax.ppermute(block, "z", [(i, i - by) for i in range(4) if i - by >= 0])


def exchange(block, axes):
    return lax.all_to_all(block, axes, 0, 0, tiled=True)


def spread(block, axes, count):
    return exchange(jnp.broadcast_to(block[None], (count,) + block.shape), axes)


def after(block, *earlier):
    return lax.optimization_barrier((block,) + earlier)[0]


def plain_dot(first_op, second_op):
    return jnp.dot(first_op, second_op, preferred_element_type=f32)


def left_dot(first_op, second_op):
    return lax.dot_general(
        first_op, second_op, (((0,), (0,)), ((), ())), preferred_element_type=f32
    )


def right_dot(first_op, second_op):
    return lax.dot_general(
        first_op, second_op, (((1,), (1,)), ((), ())), preferred_element_type=f32
    )


def inverse_rms(values):
    return lax.rsqrt(jnp.mean(values * values, axis=-1, keepdims=True) + epsilon)


def rotate_back(values, cos_table, sin_table):
    former, latter = values[..., :64], values[..., 64:]
    return jnp.concatenate(
        [former * cos_table + latter * sin_table, latter * cos_table - former * sin_table], axis=-1
    )


def norm_back(incoming, normal, inverse):
    return inverse * (incoming - normal * jnp.mean(incoming * normal, axis=-1, keepdims=True))


def block_mask(block, key_block, starts):
    key_at = key_block * KEY_BLK + lax.broadcasted_iota(jnp.int32, (KEY_BLK, BLK), 0)
    query_at = (KEYS - ROWS) + block * BLK + lax.broadcasted_iota(jnp.int32, (KEY_BLK, BLK), 1)
    return (key_at >= starts) & (key_at <= query_at)


def attend_kernel(low_ref, start_ref, q_ref, k_ref, v_ref, out_ref, full_ref, total_ref):
    for block in range(ROWS // BLK):
        cols = pl.ds(block * BLK, BLK)
        queries = q_ref[cols, :]
        starts = start_ref[:, cols]

        def step(key_block, state):
            acc, total = state
            rows = pl.ds(pl.multiple_of(key_block * KEY_BLK, KEY_BLK), KEY_BLK)
            scores = right_dot(k_ref[rows, :], queries) * (score_scale * log2e)
            weights = jnp.where(block_mask(block, key_block, starts), jnp.exp2(scores), 0.0)
            total = total + jnp.sum(weights, axis=0, keepdims=True)
            acc = acc + left_dot(v_ref[rows, :], weights.astype(bf16))
            return acc, total

        acc, total = lax.fori_loop(
            low_ref[block],
            (KEYS - ROWS + (block + 1) * BLK + KEY_BLK - 1) // KEY_BLK,
            step,
            (jnp.zeros((HD, BLK), f32), jnp.zeros((1, BLK), f32)),
        )
        full = acc / total
        full_ref[:, cols] = full
        total_ref[:, cols] = jnp.log2(total)
        out_ref[cols, :] = full.T.astype(bf16)


def attend(low, starts, queries, keys, values):
    vmem = pl.BlockSpec(memory_space=pltpu.VMEM)
    return pl.pallas_call(
        attend_kernel,
        out_shape=(
            jax.ShapeDtypeStruct((ROWS, HD), bf16),
            jax.ShapeDtypeStruct((HD, ROWS), f32),
            jax.ShapeDtypeStruct((1, ROWS), f32),
        ),
        in_specs=[pl.BlockSpec(memory_space=pltpu.SMEM)] + [vmem] * 4,
        out_specs=(vmem,) * 3,
        compiler_params=pltpu.CompilerParams(vmem_limit_bytes=16 * MIB),
        cost_estimate=pl.CostEstimate(
            flops=4 * ROWS * 2048 * HD, bytes_accessed=4 << 20, transcendentals=ROWS * 2048
        ),
        name="attend",
    )(low, starts, queries, keys, values)


def attend_back_kernel(
    low_ref,
    core_ref,
    start_ref,
    q_ref,
    k_ref,
    v_ref,
    do_ref,
    full_ref,
    total_ref,
    dq_ref,
    keep_ref,
    send_ref,
    dk_ref,
    dv_ref,
):
    dk_ref[...] = jnp.zeros_like(dk_ref)
    dv_ref[...] = jnp.zeros_like(dv_ref)
    for block in range(ROWS // BLK):
        cols = pl.ds(block * BLK, BLK)
        queries = q_ref[cols, :]
        starts = start_ref[:, cols]
        incoming = do_ref[cols, :]
        total = total_ref[:, cols]
        delta = jnp.sum(incoming.astype(f32).T * full_ref[:, cols], axis=0, keepdims=True)

        def step(key_block, acc):
            rows = pl.ds(pl.multiple_of(key_block * KEY_BLK, KEY_BLK), KEY_BLK)
            keys = k_ref[rows, :]
            scores = right_dot(keys, queries) * (score_scale * log2e)
            weights = jnp.where(
                block_mask(block, key_block, starts), jnp.exp2(scores - total), 0.0
            )
            grads = right_dot(v_ref[rows, :], incoming)
            grads = (weights * (grads - delta)).astype(bf16)
            dv_ref[rows, :] += plain_dot(weights.astype(bf16), incoming)
            dk_ref[rows, :] += plain_dot(grads, queries)
            return acc + left_dot(keys, grads)

        acc = lax.fori_loop(
            low_ref[block],
            (KEYS - ROWS + (block + 1) * BLK + KEY_BLK - 1) // KEY_BLK,
            step,
            jnp.zeros((HD, BLK), f32),
        )
        dq_ref[cols, :] = acc.T * score_scale

    @pl.when(core_ref[0] == 0)
    def _():
        keep_ref[...] = dk_ref[...] * score_scale
        send_ref[...] = dv_ref[...].astype(bf16)

    @pl.when(core_ref[0] == 1)
    def _():
        keep_ref[...] = dv_ref[...]
        send_ref[...] = (dk_ref[...] * score_scale).astype(bf16)


def attend_back(low, core, starts, queries, keys, values, incoming, full, total):
    vmem = pl.BlockSpec(memory_space=pltpu.VMEM)
    smem = pl.BlockSpec(memory_space=pltpu.SMEM)
    return pl.pallas_call(
        attend_back_kernel,
        out_shape=(
            jax.ShapeDtypeStruct((ROWS, HD), f32),
            jax.ShapeDtypeStruct((KEYS, HD), f32),
            jax.ShapeDtypeStruct((KEYS, HD), bf16),
        ),
        in_specs=[smem, smem] + [vmem] * 7,
        out_specs=(vmem,) * 3,
        scratch_shapes=[pltpu.VMEM((KEYS, HD), f32), pltpu.VMEM((KEYS, HD), f32)],
        compiler_params=pltpu.CompilerParams(vmem_limit_bytes=28 * MIB),
        cost_estimate=pl.CostEstimate(
            flops=10 * ROWS * 2048 * HD, bytes_accessed=8 << 20, transcendentals=ROWS * 2048
        ),
        name="attend_back",
    )(low, core, starts, queries, keys, values, incoming, full, total)


def colour_kernel(place_ref, column_ref, row_ref, out_ref):
    down_at = lax.broadcasted_iota(jnp.int32, (64, 64), 0)
    across_at = lax.broadcasted_iota(jnp.int32, (64, 64), 1)
    same_slots = (down_at >> 3) == (across_at >> 3)
    same_spans = (column_ref[...] >> 3) == (row_ref[...] >> 3)
    colour = jnp.zeros((64, 1), jnp.int32)
    for _ in range(3):
        colour_row = jnp.sum(
            jnp.where(down_at == across_at, colour, 0).astype(f32), axis=0, keepdims=True
        ).astype(jnp.int32)
        alike = colour == colour_row

        def partner(group):
            near = group & alike
            rank_down = jnp.sum(
                jnp.where(near & (across_at < down_at), 1.0, 0.0), axis=1, keepdims=True
            ).astype(jnp.int32)
            rank_across = jnp.sum(
                jnp.where(near & (down_at < across_at), 1.0, 0.0), axis=0, keepdims=True
            ).astype(jnp.int32)
            return jnp.where(near & ((rank_down ^ 1) == rank_across), 1.0, 0.0)

        by_slot = partner(same_slots)
        jump = plain_dot(by_slot, partner(same_spans))
        label = lax.broadcasted_iota(jnp.int32, (64, 128), 0).astype(f32)
        for turn in range(5):
            label = jnp.minimum(label, plain_dot(jump, label))
            if turn < 4:
                jump = plain_dot(jump, jump)
        bit = jnp.where(label > plain_dot(by_slot, label), 1, 0)
        colour = colour * 2 + bit[:, :1]
    colour_row = jnp.sum(
        jnp.where(down_at == across_at, colour, 0).astype(f32), axis=0, keepdims=True
    )
    own = place_ref[0]
    same_row = (down_at & 7) == (across_at & 7)
    slot_colour = jnp.sum(
        jnp.where(down_at == own * 8 + (across_at >> 3), colour, 0).astype(f32),
        axis=0,
        keepdims=True,
    ).astype(jnp.int32)
    owner = jnp.sum(
        jnp.where(same_slots & (colour == own), column_ref[...] >> 3, 0).astype(f32),
        axis=0,
        keepdims=True,
    ).astype(jnp.int32)
    span_colour = jnp.sum(
        jnp.where(row_ref[...] == own * 8 + (down_at >> 3), colour_row, 0.0),
        axis=1,
        keepdims=True,
    ).astype(jnp.int32)
    for index, match in enumerate(
        (
            slot_colour == (down_at >> 3),
            owner == (down_at >> 3),
            span_colour == (across_at >> 3),
        )
    ):
        out_ref[index] = jnp.where(match & same_row, 1.0, 0.0).astype(bf16)


def routes(place, span_order):
    vmem = pl.BlockSpec(memory_space=pltpu.VMEM)
    return pl.pallas_call(
        colour_kernel,
        out_shape=jax.ShapeDtypeStruct((3, 64, 64), bf16),
        in_specs=[pl.BlockSpec(memory_space=pltpu.SMEM), vmem, vmem],
        out_specs=vmem,
        name="routes",
    )(place.reshape(1), span_order.reshape(64, 1), span_order.reshape(1, 64))


def project_kernel(
    place_ref,
    rows_ref,
    gain_ref,
    query_ref,
    kv_ref,
    cos_ref,
    sin_ref,
    gain_query_ref,
    gain_key_ref,
    normed_ref,
    inverse_ref,
    query_out_ref,
    kv_out_ref,
    query_hat_ref,
    query_inv_ref,
    key_hat_ref,
    key_inv_ref,
):
    rows = rows_ref[...].astype(f32)
    inverse = inverse_rms(rows)
    normed = (rows * inverse * gain_ref[...]).astype(bf16)
    inverse_ref[...] = inverse
    normed_ref[...] = normed
    cos, sin = cos_ref[...], sin_ref[...]

    def turned(values):
        return values * cos + pltpu.roll(values, 64, 1) * sin

    kv = plain_dot(normed, kv_ref[...])
    inverse = inverse_rms(kv)
    hat = kv * inverse
    key_hat_ref[...] = hat
    key_inv_ref[...] = inverse
    key = turned(hat * gain_key_ref[...])
    kv_out_ref[...] = jnp.where(place_ref[0] == 0, key, kv).astype(bf16)
    query = plain_dot(normed, query_ref[...])
    inverse = inverse_rms(query)
    hat = query * inverse
    query_hat_ref[...] = hat
    query_inv_ref[...] = inverse
    query_out_ref[...] = turned(hat * gain_query_ref[...]).astype(bf16)


def project(core, rows, gain, query_weights, kv_weights, cos, sin, gain_query, gain_key):
    wide = pl.BlockSpec((256, D), lambda i: (i, 0))
    head = pl.BlockSpec((256, HD), lambda i: (i, 0))
    one = pl.BlockSpec((256, 1), lambda i: (i, 0))
    weight = pl.BlockSpec((D, HD), lambda i: (0, 0))
    small = pl.BlockSpec((1, HD), lambda i: (0, 0))
    column = pltpu.HBM((ROWS, 1), f32)
    return pl.pallas_call(
        project_kernel,
        grid=(4,),
        out_shape=(
            pltpu.HBM((ROWS, D), bf16),
            column,
            jax.ShapeDtypeStruct((ROWS, HD), bf16),
            jax.ShapeDtypeStruct((ROWS, HD), bf16),
            pltpu.HBM((ROWS, HD), f32),
            column,
            pltpu.HBM((ROWS, HD), f32),
            column,
        ),
        in_specs=[
            pl.BlockSpec(memory_space=pltpu.SMEM),
            wide,
            pl.BlockSpec((1, D), lambda i: (0, 0)),
            weight,
            weight,
            head,
            head,
            small,
            small,
        ],
        out_specs=(wide, one, head, head, head, one, head, one),
        compiler_params=pltpu.CompilerParams(vmem_limit_bytes=20 * MIB),
        cost_estimate=pl.CostEstimate(
            flops=4 * ROWS * D * HD, bytes_accessed=12 << 20, transcendentals=0
        ),
        name="project",
    )(core, rows, gain, query_weights, kv_weights, cos, sin, gain_query, gain_key)


def turned_columns(block):
    return jnp.concatenate(
        [block[:, at * 256 : at * 256 + 256] for at in (0, 4, 1, 5, 2, 6, 3, 7)], axis=1
    )


def turned_place(index):
    return (index % 2) * 4 + index // 2


def feed_kernel(normed_ref, grad_ref, near_ref, far_ref, act_ref, wide_ref, part_ref):
    normed, grad = turned_columns(normed_ref[...]), turned_columns(grad_ref[...])
    for index, weight_ref in enumerate((near_ref, far_ref)):
        gate = plain_dot(normed, weight_ref[:, :384])
        up = plain_dot(normed, weight_ref[:, 384:768])
        grad_act = plain_dot(grad, weight_ref[:, 768:])
        sigma = jax.nn.sigmoid(gate)
        silu = gate * sigma
        grad_gate = (grad_act * up * sigma * (1.0 + gate * (1.0 - sigma))).astype(bf16)
        grad_up = (grad_act * silu).astype(bf16)
        act_ref[:, index * 384 : index * 384 + 384] = (silu * up).astype(bf16)
        wide_ref[:, index * 768 : index * 768 + 384] = grad_gate
        wide_ref[:, index * 768 + 384 : index * 768 + 768] = grad_up
    part = right_dot(wide_ref[:, :768], near_ref[:, :768])
    part = part + right_dot(wide_ref[:, 768:], far_ref[:, :768])
    for index in range(8):
        at = turned_place(index) * 256
        part_ref[:, at : at + 256] = part[:, index * 256 : index * 256 + 256].astype(bf16)


def feed(normed, grad, near, far):
    tile = pl.BlockSpec((256, D), lambda i: (i, 0))
    weight = pl.BlockSpec((D, 1152), lambda i: (0, 0))
    return pl.pallas_call(
        feed_kernel,
        grid=(2,),
        out_shape=(
            jax.ShapeDtypeStruct((512, 768), bf16),
            jax.ShapeDtypeStruct((512, 1536), bf16),
            jax.ShapeDtypeStruct((512, D), bf16),
        ),
        in_specs=[tile, tile, weight, weight],
        out_specs=(
            pl.BlockSpec((256, 768), lambda i: (i, 0)),
            pl.BlockSpec((256, 1536), lambda i: (i, 0)),
            tile,
        ),
        compiler_params=pltpu.CompilerParams(vmem_limit_bytes=44 * MIB),
        cost_estimate=pl.CostEstimate(
            flops=2 * 512 * D * 3840, bytes_accessed=18 << 20, transcendentals=512 * 768
        ),
        name="feed",
    )(normed, grad, near, far)


def weights_grad_kernel(normed_ref, grad_ref, wide_ref, act_ref, *refs):
    came_ref, out_ref, wide_turned_ref, act_turned_ref = refs if len(refs) == 4 else (None, *refs)

    @pl.when(pl.program_id(0) == 0)
    def _():
        wide_turned_ref[...] = wide_ref[...].T
        act_turned_ref[...] = act_ref[...].T

    wide = plain_dot(wide_turned_ref[...], normed_ref[...])
    down = plain_dot(act_turned_ref[...], grad_ref[...])
    if came_ref is not None:
        wide = wide + came_ref[0, :768, :].astype(f32)
        down = down + came_ref[0, 768:, :].astype(f32)
    out_ref[0, :768, :] = wide.astype(bf16)
    out_ref[0, 768:, :] = down.astype(bf16)


def weights_grad(normed, grad, wide, act, half, came=None):
    tile = pl.BlockSpec((512, 256), lambda i: (0, i))
    out = pl.BlockSpec((1, 1152, 256), lambda i: (i % 4 * 2 + i // 4, 0, 0))
    return pl.pallas_call(
        weights_grad_kernel,
        grid=(8,),
        out_shape=jax.ShapeDtypeStruct((8, 1152, 256), bf16),
        in_specs=[
            tile,
            tile,
            pl.BlockSpec((512, 768), lambda i: (0, half)),
            pl.BlockSpec((512, 384), lambda i: (0, half)),
        ]
        + ([] if came is None else [out]),
        out_specs=out,
        scratch_shapes=[pltpu.VMEM((768, 512), bf16), pltpu.VMEM((384, 512), bf16)],
        compiler_params=pltpu.CompilerParams(vmem_limit_bytes=20 * MIB),
        cost_estimate=pl.CostEstimate(
            flops=2 * 512 * D * 1152, bytes_accessed=10 << 20, transcendentals=0
        ),
        name="weights_grad",
    )(normed, grad, wide, act, *(() if came is None else (came,)))


def down_kernel(place_ref, act_ref, near_ref, far_ref, hidden_ref, out_ref, total_ref):
    chip = place_ref[0]
    total = right_dot(act_ref[:, :384], near_ref[...])
    total_ref[...] = total + right_dot(act_ref[:, 384:], far_ref[...])

    @pl.when(pl.program_id(0) == chip // 4)
    def _():
        rows = pl.ds(pl.multiple_of((chip % 4) * 64, 64), 64)
        total_ref[rows, :] += turned_columns(hidden_ref[...])

    for index in range(8):
        cols = total_ref[:, index * 256 : index * 256 + 256]
        out_ref[turned_place(index)] = cols.astype(bf16)


def down(chip, act, near, far, hidden):
    weight = pl.BlockSpec((D, 384), lambda i: (0, 2))
    return pl.pallas_call(
        down_kernel,
        grid=(2,),
        out_shape=jax.ShapeDtypeStruct((8, 512, 256), bf16),
        in_specs=[
            pl.BlockSpec(memory_space=pltpu.SMEM),
            pl.BlockSpec((256, 768), lambda i: (i, 0)),
            weight,
            weight,
            pl.BlockSpec((64, D), lambda i: (0, 0)),
        ],
        out_specs=pl.BlockSpec((8, 256, 256), lambda i: (0, i, 0)),
        scratch_shapes=[pltpu.VMEM((256, D), f32)],
        compiler_params=pltpu.CompilerParams(vmem_limit_bytes=24 * MIB),
        cost_estimate=pl.CostEstimate(
            flops=2 * 512 * D * 768, bytes_accessed=8 << 20, transcendentals=0
        ),
        name="down",
    )(chip, act, near, far, hidden)


def input_part_kernel(
    place_ref,
    near_ref,
    far_ref,
    near_weight_ref,
    far_weight_ref,
    rows_ref,
    inverse_ref,
    gain_ref,
    hidden_ref,
    mlp_ref,
    head_ref,
    out_ref,
    total_ref,
    term_ref,
    sum_ref,
):
    step = pl.program_id(0)
    part = right_dot(near_ref[...], near_weight_ref[...])
    part = part + right_dot(far_ref[...], far_weight_ref[...])
    inverse = inverse_ref[...]
    gain = gain_ref[...]
    weighted = part * (rows_ref[...].astype(f32) * inverse)
    term = jnp.sum(weighted * gain, axis=1, keepdims=True) * (1.0 / D)
    term_ref[pl.ds(step, 1), :] = jnp.broadcast_to(term, (256, 128)).T[:1, :]
    sums = jnp.sum(weighted.reshape(32, 8, D), axis=0)

    @pl.when(step == 0)
    def _():
        sum_ref[...] = sums

    @pl.when(step > 0)
    def _():
        sum_ref[...] += sums

    total_ref[...] = part * (gain * inverse)
    hidden = hidden_ref[...]
    for span in range(2):
        own = pl.ds(pl.multiple_of(span * 128 + place_ref[0] * 16, 16), 16)
        total_ref[own, :] += hidden[span * 16 : span * 16 + 16, :]
    rows = pl.ds(pl.multiple_of(step * 256, 256), 256)
    for index in range(8):
        cols = total_ref[:, index * 256 : index * 256 + 256]
        out_ref[index, rows, :] = cols.astype(bf16)

    @pl.when(step == 1)
    def _():
        terms = term_ref[:2, :]
        coarse = terms.astype(bf16).astype(f32)
        totals = jnp.sum(sum_ref[...], axis=0, keepdims=True)
        extra = jnp.concatenate(
            [coarse, terms - coarse]
            + [totals[:, index * 256 : index * 256 + 256] for index in range(8)]
            + [mlp_ref[...], head_ref[...], jnp.zeros((11, 256), f32)],
            axis=0,
        ).astype(bf16)
        for index in range(8):
            out_ref[index, 512:, :] = extra


def input_part(place, near, far, near_weight, far_weight, rows, inverse, gain, hidden, mlp, head):
    def fixed(*shape):
        return pl.BlockSpec(shape, lambda i, place_ref: (0,) * len(shape))

    def tile(*shape):
        return pl.BlockSpec(shape, lambda i, place_ref: (i, 0))

    def own(*shape):
        return pl.BlockSpec(shape, lambda i, place_ref: (place_ref[1] * 2 + i, 0))

    return pl.pallas_call(
        input_part_kernel,
        out_shape=jax.ShapeDtypeStruct((8, 544, 256), bf16),
        grid_spec=pltpu.PrefetchScalarGridSpec(
            num_scalar_prefetch=1,
            grid=(2,),
            in_specs=[
                tile(256, 256),
                tile(256, 256),
                fixed(D, 256),
                fixed(D, 256),
                own(256, D),
                own(256, 1),
                fixed(1, D),
                tile(32, D),
                fixed(8, 256),
                fixed(1, 256),
            ],
            out_specs=fixed(8, 544, 256),
            scratch_shapes=[
                pltpu.VMEM((256, D), f32),
                pltpu.VMEM((8, 256), f32),
                pltpu.VMEM((8, D), f32),
            ],
        ),
        compiler_params=pltpu.CompilerParams(vmem_limit_bytes=28 * MIB),
        cost_estimate=pl.CostEstimate(
            flops=2 * ROWS * D * 256, bytes_accessed=8 << 20, transcendentals=0
        ),
        name="input_part",
    )(place, near, far, near_weight, far_weight, rows, inverse, gain, hidden, mlp, head)


def attention_grads_kernel(normed_ref, grad_ref, grad_out_ref, out_ref, turned_ref):
    @pl.when(pl.program_id(0) == 0)
    def _():
        turned_ref[...] = grad_ref[...].T

    out_ref[0, :256, :] = plain_dot(turned_ref[...], normed_ref[...]).astype(bf16)
    out_ref[0, 256:, :] = grad_out_ref[...]


def attention_grads(normed, grad_proj, grad_out):
    return pl.pallas_call(
        attention_grads_kernel,
        grid=(8,),
        out_shape=jax.ShapeDtypeStruct((8, 384, 256), bf16),
        in_specs=[
            pl.BlockSpec((ROWS, 256), lambda i: (0, i)),
            pl.BlockSpec((ROWS, 256), lambda i: (0, 0)),
            pl.BlockSpec((HD, 256), lambda i: (0, i)),
        ],
        out_specs=pl.BlockSpec((1, 384, 256), lambda i: (i % 4 * 2 + i // 4, 0, 0)),
        scratch_shapes=[pltpu.VMEM((256, ROWS), bf16)],
        compiler_params=pltpu.CompilerParams(vmem_limit_bytes=12 * MIB),
        cost_estimate=pl.CostEstimate(
            flops=2 * ROWS * D * 256, bytes_accessed=8 << 20, transcendentals=0
        ),
        name="attention_grads",
    )(normed, grad_proj, grad_out)


def body(
    inputs,
    out_grad,
    lengths,
    span_order,
    w_query,
    w_key,
    w_value,
    w_out,
    w_gate,
    w_up,
    w_down,
    norm_attn,
    norm_mlp,
    norm_query,
    norm_key,
):
    xl, z, xh, y, core = (lax.axis_index(name) for name in ("xl", "z", "xh", "y", "c"))
    span_place = xl * 4 + z
    chip = xh * 4 + y
    first = core == 0

    def by_core(near, far, axis=0):
        join = jnp.stack if axis is None else lambda parts: jnp.concatenate(parts, axis=axis)
        return jnp.where(first, join([near, far]), join([far, near]))

    def split(block):
        near = lax.dynamic_slice_in_dim(block, core * 512, 512, 0)
        far = lax.dynamic_slice_in_dim(block, (1 - core) * 512, 512, 0)
        return near, far

    def chip_major(block):
        return block.reshape(4, 8, 16, -1).transpose(1, 0, 2, 3).reshape(512, -1)

    def span_major(block):
        return block.reshape(8, 4, 16, -1).transpose(1, 0, 2, 3).reshape(512, -1)

    gains = jnp.concatenate([norm_attn, norm_mlp, norm_query, norm_key])
    gains = jnp.pad(gains, (0, 16 * 256 - 544)).reshape(16, 256)
    shard = jnp.concatenate(
        [jnp.concatenate([w_query, w_key, w_value], axis=1), gains], axis=0
    )
    spread_weights = spread(shard, SPANS, 8)
    qkv_weights = spread_weights[:, :256].reshape(D, 256)
    gains = spread_weights[:, 256:259].reshape(8, 768).astype(f32)
    gain_attn = gains[:, :256].reshape(1, D)
    gain_mlp = gains[:, 256:512].reshape(1, D)
    gain_query = gains[:, 512:528].reshape(1, HD)
    gain_key = gains[:, 528:544].reshape(1, HD)
    query_weights = qkv_weights[:, :128]
    key_half, value_half = qkv_weights[:, 128:192], qkv_weights[:, 192:256]
    other_half = swap(jnp.where(first, value_half, key_half))
    kv_weights = by_core(jnp.where(first, key_half, value_half), other_half, 1)

    route = routes(span_place, span_order)

    def reorder(index, rows):
        return plain_dot(route[index], rows).astype(bf16)

    moving = lax.dynamic_index_in_dim(
        out_grad.reshape(8, 16, 8, D), chip * 2 + core, 1, keepdims=False
    ).reshape(64, D)
    moving = reorder(0, moving).reshape(8, 8, D)
    spread_out = jnp.broadcast_to(w_out.reshape(1, 16, D), (8, 16, D))
    moving = jnp.concatenate([moving, spread_out], axis=1)
    moving = exchange(after(moving, qkv_weights), SPANS)
    gain_attn = after(gain_attn, moving)
    out_weights = moving[:, 8:].reshape(8, HD, 256)
    moving = moving[:, :8].reshape(64, D)

    ends = jnp.cumsum(lax.dynamic_index_in_dim(lengths, xl, 0, keepdims=False))
    offset = z * ROWS + jnp.arange(ROWS, dtype=jnp.int32)
    doc_start = jnp.where(offset >= ends[1], ends[1], jnp.where(offset >= ends[0], ends[0], 0))
    frequency = jnp.power(rope_base, -2.0 * jnp.arange(HD // 2, dtype=f32) / HD)
    angles = (offset - doc_start).astype(f32)[:, None] * frequency[None, :]
    cos_table, sin_table = jnp.cos(angles), jnp.sin(angles)
    starts = doc_start - (z - 3) * ROWS
    low = starts.reshape(ROWS // BLK, BLK)[:, 0] // KEY_BLK
    starts = starts.reshape(1, ROWS)

    normed, inverse_one, query_bf, own_kv, query_hat, query_inv, key_hat, key_inv = project(
        core.reshape(1),
        inputs,
        gain_attn,
        query_weights,
        kv_weights,
        jnp.concatenate([cos_table, cos_table], axis=1),
        jnp.concatenate([-sin_table, sin_table], axis=1),
        gain_query,
        gain_key,
    )
    moving = after(reorder(1, moving), own_kv)
    moving = exchange(moving.reshape(8, 8, D), SPANS).reshape(64, D)
    moving = reorder(2, moving).reshape(8, 8, D)
    near = lax.dynamic_slice_in_dim(moving, core * 4, 4, 0)
    far = lax.dynamic_slice_in_dim(moving, (1 - core) * 4, 4, 0)
    own_grad = by_core(near, swap(far), 1).reshape(64, D)
    grad_mine = spread(own_grad, CHIPS, 8).reshape(512, D)

    mine = jnp.concatenate(
        [onward(own_kv, 3), onward(own_kv, 2), onward(own_kv, 1), own_kv], axis=0
    )
    mine = after(mine, own_grad)
    other = swap(mine)
    all_keys = jnp.where(first, mine, other)
    all_values = jnp.where(first, other, mine)

    mlp_shard = after(jnp.concatenate([w_gate, w_up, w_down.T], axis=1), qkv_weights)
    far_shard = far_span(mlp_shard)
    mlp_shard = jnp.where(
        xl == 0,
        jnp.concatenate([mlp_shard, far_shard]),
        jnp.concatenate([far_shard, mlp_shard]),
    )
    near_weights = lax.all_gather(after(mlp_shard, mine), "z", axis=0, tiled=True)
    far_weights = swap(near_weights)

    out_weights = out_weights.transpose(1, 0, 2).reshape(HD, D)
    out_two = jnp.concatenate([out_weights, swap(out_weights)], axis=0)

    attended, attended_full, total = attend(low, starts, query_bf, all_keys, all_values)
    att_near, att_far = split(attended)
    att_two = jnp.concatenate(
        [chip_major(att_near), swap(chip_major(att_far))], axis=1
    )
    branch = plain_dot(att_two, out_two).astype(bf16)
    branch = after(branch, grad_mine).reshape(8, 64, D)
    branch = jnp.sum(exchange(branch, CHIPS).astype(f32), axis=0)
    own_rows = lax.dynamic_slice_in_dim(inputs, core * 512, 512, 0).reshape(4, 8, 16, D)
    own_rows = lax.dynamic_index_in_dim(own_rows, chip, 1, keepdims=False).reshape(64, D)
    hidden = own_rows.astype(f32) + branch
    inverse_two = inverse_rms(hidden)
    normal_two = hidden * inverse_two
    normed_mlp = (normal_two * gain_mlp).astype(bf16)
    normed_mine = spread(normed_mlp, CHIPS, 8).reshape(512, D)

    act, wide, part = feed(normed_mine, grad_mine, near_weights, far_weights)
    part = exchange(part.reshape(8, 64, D), CHIPS)
    came = swap(weights_grad(normed_mine, grad_mine, wide, act, 1))
    out_cols = down(chip.reshape(1), act, near_weights, far_weights, hidden)
    mlp_grads = weights_grad(normed_mine, grad_mine, wide, act, 0, came)
    part, mlp_grads, out_cols = lax.optimization_barrier((part, mlp_grads, out_cols))
    grad_normed_mlp = jnp.sum(part.astype(f32), axis=0)

    def scatter_weights(block):
        block = lax.psum_scatter(block, "z", scatter_dimension=0, tiled=True)
        sent = lax.dynamic_index_in_dim(block, 1 - xl, 0, keepdims=False)
        kept = lax.dynamic_index_in_dim(block, xl, 0, keepdims=False)
        return kept, sent

    mlp_grads, mlp_sent = scatter_weights(mlp_grads)

    gain_mlp_part = jnp.sum(grad_normed_mlp * normal_two, axis=0)
    grad_hidden = own_grad.astype(f32) + norm_back(
        grad_normed_mlp * gain_mlp, normal_two, inverse_two
    )
    branch_mine = spread(grad_hidden.astype(bf16), CHIPS, 8).reshape(512, D)
    grad_two = right_dot(branch_mine, out_two).astype(bf16)
    grad_att = by_core(span_major(grad_two[:, :HD]), span_major(swap(grad_two[:, HD:])))

    out_cols = exchange(after(out_cols, branch_mine), CHIPS)
    out_cols = jnp.sum(out_cols.astype(f32), axis=0).astype(bf16)
    near = jnp.where(first, out_cols[:, :128], out_cols[:, 128:])
    far = jnp.where(first, out_cols[:, 128:], out_cols[:, :128])
    out_cols = by_core(near, swap(far), None).reshape(2, 8, 4, 2, 8, 128)
    out_rows = jnp.concatenate(
        [out_cols[:, index // 2, :, index % 2].reshape(64, 128) for index in range(16)], axis=1
    )

    def unorder(index, rows):
        return left_dot(route[index], rows).astype(bf16)

    out_rows = exchange(unorder(2, out_rows).reshape(8, 8, D), SPANS).reshape(64, D)
    out_rows = unorder(1, out_rows).reshape(8, 8, D)

    grad_query_rot, keep, send = attend_back(
        low,
        core.reshape(1),
        starts,
        query_bf,
        all_keys,
        all_values,
        grad_att,
        attended_full,
        total,
    )
    grad_out = left_dot(att_two, branch_mine)
    grad_out = (grad_out[:HD] + swap(grad_out[HD:].astype(bf16)).astype(f32)).astype(bf16)
    grad_kv = (keep + swap(send).astype(f32)).reshape(4, ROWS, HD)
    away = grad_kv.astype(bf16)
    grad_kv = (
        grad_kv[3]
        + backward(away[2], 1).astype(f32)
        + backward(away[1], 2).astype(f32)
        + backward(away[0], 3).astype(f32)
    )
    grad_kv = after(grad_kv, mlp_sent)
    query_norm_grad = rotate_back(grad_query_rot, cos_table, sin_table)
    gain_query_part = jnp.sum(query_norm_grad * query_hat, axis=0)
    grad_query_proj = norm_back(query_norm_grad * gain_query, query_hat, query_inv)
    key_norm_grad = rotate_back(grad_kv, cos_table, sin_table)
    gain_key_part = jnp.where(first, jnp.sum(key_norm_grad * key_hat, axis=0), 0.0)
    grad_key_proj = norm_back(key_norm_grad * gain_key, key_hat, key_inv)
    grad_kv_proj = jnp.where(first, grad_key_proj, grad_kv)
    grad_proj = jnp.concatenate([grad_query_proj.astype(bf16), grad_kv_proj.astype(bf16)], axis=1)

    grad_near, grad_far = split(grad_proj)
    near_weight = jnp.concatenate([query_weights, kv_weights], axis=1)
    by_cols = input_part(
        jnp.stack([chip, core]),
        grad_near,
        swap(grad_far),
        near_weight,
        swap(near_weight),
        inputs,
        inverse_one,
        gain_attn,
        grad_hidden,
        gain_mlp_part.reshape(8, 256),
        jnp.concatenate([gain_query_part, gain_key_part]).reshape(1, 256),
    )
    grad_proj = after(grad_proj, by_cols)
    by_cols = jnp.sum(exchange(by_cols, CHIPS).astype(f32), axis=0)
    row_term = (by_cols[512:514] + by_cols[514:516]).reshape(512, 1)
    own_inverse = lax.dynamic_slice_in_dim(inverse_one, core * 512, 512, 0)
    own_cols = lax.dynamic_slice(inputs, (core * 512, chip * 256), (512, 256)).astype(f32)
    in_grad = by_cols[:512] - own_cols * (own_inverse * own_inverse * row_term)
    near = jnp.where(first, in_grad[:, :128], in_grad[:, 128:])
    far = jnp.where(first, in_grad[:, 128:], in_grad[:, :128])
    in_grad = by_core(near, swap(far))
    gain_sums = jnp.concatenate(
        [
            by_cols[516:524],
            by_cols[524:532],
            by_cols[532, :128].reshape(8, 16),
            by_cols[532, 128:].reshape(8, 16),
        ],
        axis=1,
    )
    gain_sums = gain_sums + swap(gain_sums)
    coarse = gain_sums.astype(bf16)
    extra = jnp.concatenate(
        [coarse, (gain_sums - coarse.astype(f32)).astype(bf16), jnp.zeros((8, 960), bf16)], axis=1
    )
    extra = jnp.pad(extra[:, None], ((0, 0), (0, 7), (0, 0)))
    out_rows = exchange(jnp.concatenate([out_rows, extra], axis=1), SPANS)
    gain_sums = jnp.sum(out_rows[:, 8].astype(f32), axis=0)
    gain_sums = gain_sums[:544] + gain_sums[544:1088]
    layer_out = unorder(0, out_rows[:, :8].reshape(64, D))
    layer_out = jnp.stack(
        [layer_out[:, at * 128 : at * 128 + 128].reshape(8, 8, 128) for at in range(16)],
        axis=1,
    )
    layer_out = layer_out.reshape(ROWS, 128).astype(f32)

    grad_attn = attention_grads(normed, grad_proj, grad_out)
    grad_attn, attn_sent = scatter_weights(grad_attn)
    grad_attn = grad_attn.astype(f32) + far_span(attn_sent).astype(f32)
    grad_kv_weight = grad_attn[128:256]
    low_half, high_half = grad_kv_weight[:64], grad_kv_weight[64:]
    came = swap(jnp.where(first, high_half, low_half))
    kept = jnp.where(first, low_half, high_half)
    mlp_grads = mlp_grads.astype(f32) + far_span(after(mlp_sent, by_cols)).astype(f32)

    return (
        layer_out,
        in_grad,
        grad_attn[:128].T,
        jnp.where(first, kept, came).T,
        jnp.where(first, came, kept).T,
        grad_attn[256:],
        mlp_grads[:384].T,
        mlp_grads[384:768].T,
        mlp_grads[768:],
        gain_sums[:256],
        gain_sums[256:512],
        gain_sums[512:528],
        gain_sums[528:544],
    )


def solution(mesh):
    fine = Mesh(mesh.devices.reshape(2, 4, 2, 4, 2), ("xl", "z", "xh", "y", "c"))
    rows = P(SPANS, None)
    by_both = P(SPANS, TENSOR)
    turned = P(TENSOR, SPANS)
    lone = P(SPANS)
    return jax.shard_map(
        body,
        mesh=fine,
        in_specs=(
            rows,
            rows,
            P(),
            P(),
            by_both,
            by_both,
            by_both,
            turned,
            by_both,
            by_both,
            turned,
            lone,
            lone,
            lone,
            lone,
        ),
        out_specs=(
            by_both,
            by_both,
            by_both,
            by_both,
            by_both,
            turned,
            by_both,
            by_both,
            turned,
            lone,
            lone,
            lone,
            lone,
        ),
        check_vma=False,
    )
```

```python
import jax
import jax.numpy as jnp
from jax import lax
from jax.experimental import pallas as pl
from jax.experimental.pallas import tpu as pltpu
from jax.sharding import Mesh, PartitionSpec as P

SPAN = 128
MICRO = 2
HD = 128
D = 2048
ROWS = 1024
KEYS = 4096
KEY_BLK = 512

epsilon = 1e-06
rope_base = 1000000.0
score_scale = HD ** (-0.5)
log2e = 1.4426950408889634
bf16 = jnp.bfloat16
f32 = jnp.float32
SPANS = ("xl", "z")
TENSOR = ("xh", "y", "c")
CHIPS = ("xh", "y")
MIB = 1024 * 1024
SMALL = pl.CostEstimate(flops=1024, bytes_accessed=1024, transcendentals=0)


def swap(block):
    return lax.ppermute(block, "c", [(0, 1), (1, 0)])


def far_span(block):
    return lax.ppermute(block, "xl", [(0, 1), (1, 0)])


def onward(block, by):
    return lax.ppermute(block, "z", [(i, i + by) for i in range(4) if i + by < 4])


def backward(block, by):
    return lax.ppermute(block, "z", [(i, i - by) for i in range(4) if i - by >= 0])


def exchange(block, axes):
    return lax.all_to_all(block, axes, 0, 0, tiled=True)


def spread(block, axes, count):
    return exchange(jnp.broadcast_to(block[None], (count,) + block.shape), axes)


def after(block, *earlier):
    return lax.optimization_barrier((block,) + earlier)[0]


def fence(block):
    return swap(block.reshape(-1, block.shape[-1])[:512, :256])


def ordered(kernel, inputs, earlier):
    return lambda *refs: kernel(*refs[:inputs], *refs[inputs + len(earlier) :])


def in_hbm(block):
    return pltpu.with_memory_space_constraint(block, pltpu.HBM)


def unread(earlier):
    return [pl.BlockSpec(memory_space=pl.ANY)] * len(earlier)


def plain_dot(first_op, second_op):
    return jnp.dot(first_op, second_op, preferred_element_type=f32)


def left_dot(first_op, second_op):
    return lax.dot_general(
        first_op, second_op, (((0,), (0,)), ((), ())), preferred_element_type=f32
    )


def right_dot(first_op, second_op):
    return lax.dot_general(
        first_op, second_op, (((1,), (1,)), ((), ())), preferred_element_type=f32
    )


def inverse_rms(values):
    return lax.rsqrt(jnp.mean(values * values, axis=-1, keepdims=True) + epsilon)


def norm_back(incoming, normal, inverse):
    return inverse * (incoming - normal * jnp.mean(incoming * normal, axis=-1, keepdims=True))


def block_mask(key_block, starts):
    key_at = key_block * KEY_BLK + lax.broadcasted_iota(jnp.int32, (KEY_BLK, ROWS), 0)
    query_at = (KEYS - ROWS) + lax.broadcasted_iota(jnp.int32, (KEY_BLK, ROWS), 1)
    return (key_at >= starts) & (key_at <= query_at)


def over_keys(range_ref, step, state):
    own = (KEYS - ROWS) // KEY_BLK
    seen = jnp.minimum(range_ref[1], own)
    state = lax.fori_loop(range_ref[0], seen, lambda at, state: step(at, state, True), state)
    state = lax.fori_loop(seen, own, lambda at, state: step(at, state, False), state)
    for at in range(own, KEYS // KEY_BLK):
        state = step(at, state, True)
    return state


def attend_kernel(range_ref, start_ref, q_ref, k_ref, v_ref, out_ref, full_ref, total_ref):
    queries = q_ref[...]
    starts = start_ref[...]

    def step(at, state, masked):
        acc, total = state
        rows = pl.ds(pl.multiple_of(at * KEY_BLK, KEY_BLK), KEY_BLK)
        weights = jnp.exp2(right_dot(k_ref[rows, :], queries) * (score_scale * log2e))
        if masked:
            weights = jnp.where(block_mask(at, starts), weights, 0.0)
        total = total + jnp.sum(weights, axis=0, keepdims=True)
        acc = acc + left_dot(v_ref[rows, :], weights.astype(bf16))
        return acc, total

    acc, total = over_keys(
        range_ref, step, (jnp.zeros((HD, ROWS), f32), jnp.zeros((1, ROWS), f32))
    )
    full = acc / total
    full_ref[...] = full
    total_ref[...] = jnp.log2(total)
    out_ref[...] = full.T.astype(bf16)


def attend(low, starts, queries, keys, values, earlier):
    vmem = pl.BlockSpec(memory_space=pltpu.VMEM)
    return pl.pallas_call(
        ordered(attend_kernel, 5, earlier),
        out_shape=(
            jax.ShapeDtypeStruct((ROWS, HD), bf16),
            pltpu.HBM((HD, ROWS), f32),
            jax.ShapeDtypeStruct((1, ROWS), f32),
        ),
        in_specs=[pl.BlockSpec(memory_space=pltpu.SMEM)] + [vmem] * 4 + unread(earlier),
        out_specs=(vmem,) * 3,
        compiler_params=pltpu.CompilerParams(vmem_limit_bytes=24 * MIB),
        cost_estimate=SMALL,
        name="attend",
    )(low, starts, queries, keys, values, *earlier)


def attend_back_kernel(
    range_ref,
    core_ref,
    start_ref,
    q_ref,
    k_ref,
    v_ref,
    do_ref,
    full_ref,
    total_ref,
    dq_ref,
    keep_ref,
    send_ref,
    dk_ref,
    dv_ref,
):
    dk_ref[...] = jnp.zeros_like(dk_ref)
    dv_ref[...] = jnp.zeros_like(dv_ref)
    queries = q_ref[...]
    starts = start_ref[...]
    incoming = do_ref[...]
    total = total_ref[...]
    delta = jnp.sum(incoming.astype(f32).T * full_ref[...], axis=0, keepdims=True)

    def step(at, acc, masked):
        rows = pl.ds(pl.multiple_of(at * KEY_BLK, KEY_BLK), KEY_BLK)
        keys = k_ref[rows, :]
        weights = jnp.exp2(right_dot(keys, queries) * (score_scale * log2e) - total)
        if masked:
            weights = jnp.where(block_mask(at, starts), weights, 0.0)
        grads = right_dot(v_ref[rows, :], incoming)
        grads = (weights * (grads - delta)).astype(bf16)
        dv_ref[rows, :] += plain_dot(weights.astype(bf16), incoming)
        dk_ref[rows, :] += plain_dot(grads, queries)
        return acc + left_dot(keys, grads)

    dq_ref[...] = over_keys(range_ref, step, jnp.zeros((HD, ROWS), f32)).T * score_scale

    @pl.when(core_ref[0] == 0)
    def _():
        keep_ref[...] = dk_ref[...] * score_scale
        send_ref[...] = dv_ref[...].astype(bf16)

    @pl.when(core_ref[0] == 1)
    def _():
        keep_ref[...] = dv_ref[...]
        send_ref[...] = (dk_ref[...] * score_scale).astype(bf16)


def attend_back(low, core, starts, queries, keys, values, incoming, full, total, earlier):
    vmem = pl.BlockSpec(memory_space=pltpu.VMEM)
    smem = pl.BlockSpec(memory_space=pltpu.SMEM)
    return pl.pallas_call(
        ordered(attend_back_kernel, 9, earlier),
        out_shape=(
            jax.ShapeDtypeStruct((ROWS, HD), f32),
            jax.ShapeDtypeStruct((KEYS, HD), f32),
            jax.ShapeDtypeStruct((KEYS, HD), bf16),
        ),
        in_specs=[smem, smem] + [vmem] * 7 + unread(earlier),
        out_specs=(vmem,) * 3,
        scratch_shapes=[pltpu.VMEM((KEYS, HD), f32), pltpu.VMEM((KEYS, HD), f32)],
        compiler_params=pltpu.CompilerParams(vmem_limit_bytes=32 * MIB),
        cost_estimate=SMALL,
        name="attend_back",
    )(low, core, starts, queries, keys, values, incoming, full, total, *earlier)


def colour_kernel(place_ref, lengths_ref, column_ref, row_ref, out_ref, start_ref, range_ref):
    micro, block = place_ref[1], place_ref[2]
    first_end = lengths_ref[micro, 0]
    second_end = first_end + lengths_ref[micro, 1]

    def begin(offset):
        begun = jnp.where(offset >= first_end, first_end, 0)
        begun = jnp.where(offset >= second_end, second_end, begun)
        return begun - (block - 3) * ROWS

    start_ref[...] = begin(block * ROWS + lax.broadcasted_iota(jnp.int32, (1, ROWS), 1))
    range_ref[0] = begin(block * ROWS) >> 9
    range_ref[1] = (begin(block * ROWS + ROWS - 1) + KEY_BLK - 1) >> 9
    down_at = lax.broadcasted_iota(jnp.int32, (64, 64), 0)
    across_at = lax.broadcasted_iota(jnp.int32, (64, 64), 1)
    same_slots = (down_at >> 3) == (across_at >> 3)
    same_spans = (column_ref[...] >> 3) == (row_ref[...] >> 3)
    colour = jnp.zeros((64, 1), jnp.int32)
    for _ in range(3):
        colour_row = jnp.sum(
            jnp.where(down_at == across_at, colour, 0).astype(f32), axis=0, keepdims=True
        ).astype(jnp.int32)
        alike = colour == colour_row

        def partner(group):
            near = group & alike
            rank_down = jnp.sum(
                jnp.where(near & (across_at < down_at), 1.0, 0.0), axis=1, keepdims=True
            ).astype(jnp.int32)
            rank_across = jnp.sum(
                jnp.where(near & (down_at < across_at), 1.0, 0.0), axis=0, keepdims=True
            ).astype(jnp.int32)
            return jnp.where(near & ((rank_down ^ 1) == rank_across), 1.0, 0.0)

        by_slot = partner(same_slots)
        jump = plain_dot(by_slot, partner(same_spans))
        label = lax.broadcasted_iota(jnp.int32, (64, 128), 0).astype(f32)
        for turn in range(5):
            label = jnp.minimum(label, plain_dot(jump, label))
            if turn < 4:
                jump = plain_dot(jump, jump)
        bit = jnp.where(label > plain_dot(by_slot, label), 1, 0)
        colour = colour * 2 + bit[:, :1]
    colour_row = jnp.sum(
        jnp.where(down_at == across_at, colour, 0).astype(f32), axis=0, keepdims=True
    )
    own = place_ref[0]
    same_row = (down_at & 7) == (across_at & 7)
    slot_colour = jnp.sum(
        jnp.where(down_at == own * 8 + (across_at >> 3), colour, 0).astype(f32),
        axis=0,
        keepdims=True,
    ).astype(jnp.int32)
    owner = jnp.sum(
        jnp.where(same_slots & (colour == own), column_ref[...] >> 3, 0).astype(f32),
        axis=0,
        keepdims=True,
    ).astype(jnp.int32)
    span_colour = jnp.sum(
        jnp.where(row_ref[...] == own * 8 + (down_at >> 3), colour_row, 0.0),
        axis=1,
        keepdims=True,
    ).astype(jnp.int32)
    for index, match in enumerate(
        (
            slot_colour == (down_at >> 3),
            owner == (down_at >> 3),
            span_colour == (across_at >> 3),
        )
    ):
        out_ref[index] = jnp.where(match & same_row, 1.0, 0.0).astype(bf16)


def routes(place, lengths, span_order):
    vmem = pl.BlockSpec(memory_space=pltpu.VMEM)
    smem = pl.BlockSpec(memory_space=pltpu.SMEM)
    return pl.pallas_call(
        colour_kernel,
        out_shape=(
            jax.ShapeDtypeStruct((3, 64, 64), bf16),
            jax.ShapeDtypeStruct((1, ROWS), jnp.int32),
            jax.ShapeDtypeStruct((2,), jnp.int32),
        ),
        in_specs=[smem, smem, vmem, vmem],
        out_specs=(vmem, vmem, smem),
        name="routes",
    )(place, lengths, span_order.reshape(64, 1), span_order.reshape(1, 64))


def project_kernel(
    place_ref,
    rows_ref,
    gain_ref,
    weight_ref,
    cos_ref,
    sin_ref,
    gain_query_ref,
    gain_key_ref,
    normed_ref,
    inverse_ref,
    query_out_ref,
    kv_out_ref,
    query_proj_ref,
    kv_proj_ref,
):
    rows = rows_ref[...].astype(f32)
    inverse = inverse_rms(rows)
    normed = (rows * inverse * gain_ref[...]).astype(bf16)
    inverse_ref[...] = inverse
    normed_ref[...] = normed
    cos, sin = cos_ref[...], sin_ref[...]

    def turned(values):
        return values * cos + pltpu.roll(values, 64, 1) * sin

    proj = plain_dot(normed, weight_ref[...])
    query, kv = proj[:, :HD], proj[:, HD:]
    kv_proj_ref[...] = kv
    key = turned(kv * inverse_rms(kv) * gain_key_ref[...])
    kv_out_ref[...] = jnp.where(place_ref[0] == 0, key, kv).astype(bf16)
    query_proj_ref[...] = query
    query = turned(query * inverse_rms(query) * gain_query_ref[...])
    query_out_ref[...] = query.astype(bf16)


def project(core, rows, gain, weights, cos, sin, gain_query, gain_key):
    wide = pl.BlockSpec((256, D), lambda i: (i, 0))
    head = pl.BlockSpec((256, HD), lambda i: (i, 0))
    one = pl.BlockSpec((256, 1), lambda i: (i, 0))
    weight = pl.BlockSpec((D, 256), lambda i: (0, 0))
    small = pl.BlockSpec((1, HD), lambda i: (0, 0))
    column = pltpu.HBM((ROWS, 1), f32)
    return pl.pallas_call(
        project_kernel,
        grid=(4,),
        out_shape=(
            pltpu.HBM((ROWS, D), bf16),
            column,
            jax.ShapeDtypeStruct((ROWS, HD), bf16),
            jax.ShapeDtypeStruct((ROWS, HD), bf16),
            pltpu.HBM((ROWS, HD), f32),
            pltpu.HBM((ROWS, HD), f32),
        ),
        in_specs=[
            pl.BlockSpec(memory_space=pltpu.SMEM),
            wide,
            pl.BlockSpec((1, D), lambda i: (0, 0)),
            weight,
            head,
            head,
            small,
            small,
        ],
        out_specs=(wide, one, head, head, head, head),
        compiler_params=pltpu.CompilerParams(vmem_limit_bytes=20 * MIB),
        cost_estimate=SMALL,
        name="project",
    )(core, rows, gain, weights, cos, sin, gain_query, gain_key)


def project_back_kernel(
    place_ref,
    query_grad_ref,
    own_ref,
    one_ref,
    two_ref,
    three_ref,
    cos_ref,
    sin_ref,
    query_proj_ref,
    kv_proj_ref,
    gain_query_ref,
    gain_key_ref,
    out_ref,
    sum_ref,
):
    cos, sin = cos_ref[...], sin_ref[...]

    def turned_back(values):
        return values * cos - pltpu.roll(values, 64, 1) * sin

    step = pl.program_id(0)
    grad = turned_back(query_grad_ref[...])
    query = query_proj_ref[...]
    inverse = inverse_rms(query)
    hat = query * inverse
    sums = jnp.sum(grad * hat, axis=0, keepdims=True)
    query = norm_back(grad * gain_query_ref[...], hat, inverse)
    out_ref[:, :HD] = query.astype(bf16)
    kv = own_ref[...] + one_ref[...].astype(f32)
    kv = kv + two_ref[...].astype(f32) + three_ref[...].astype(f32)
    grad = turned_back(kv)
    key = kv_proj_ref[...]
    inverse = inverse_rms(key)
    hat = key * inverse
    is_key = place_ref[0] == 0
    key_sums = jnp.where(is_key, jnp.sum(grad * hat, axis=0, keepdims=True), 0.0)
    key = norm_back(grad * gain_key_ref[...], hat, inverse)
    out_ref[:, HD:] = jnp.where(is_key, key, kv).astype(bf16)
    sums = jnp.concatenate([sums, key_sums], axis=1)

    @pl.when(step == 0)
    def _():
        sum_ref[...] = sums

    @pl.when(step > 0)
    def _():
        sum_ref[...] += sums


def project_back(core, query_grad, own, arrived, cos, sin, projections, gains, earlier):
    head = pl.BlockSpec((256, HD), lambda i: (i, 0))
    small = pl.BlockSpec((1, HD), lambda i: (0, 0))
    return pl.pallas_call(
        ordered(project_back_kernel, 12, earlier),
        grid=(4,),
        out_shape=(
            jax.ShapeDtypeStruct((ROWS, 256), bf16),
            jax.ShapeDtypeStruct((1, 256), f32),
        ),
        in_specs=[pl.BlockSpec(memory_space=pltpu.SMEM)]
        + [head] * 9
        + [small] * 2
        + unread(earlier),
        out_specs=(
            pl.BlockSpec((256, 256), lambda i: (i, 0)),
            pl.BlockSpec((1, 256), lambda i: (0, 0)),
        ),
        compiler_params=pltpu.CompilerParams(vmem_limit_bytes=12 * MIB),
        cost_estimate=SMALL,
        name="project_back",
    )(core, query_grad, own, *arrived, cos, sin, *projections, *gains, *earlier)


def merge_kernel(keep_ref, came_ref, own_ref, one_ref, two_ref, three_ref):
    for block, out_ref in enumerate((three_ref, two_ref, one_ref, own_ref)):
        rows = pl.ds(block * ROWS, ROWS)
        total = keep_ref[rows, :] + came_ref[rows, :].astype(f32)
        out_ref[...] = total.astype(out_ref.dtype)


def merge(keep, came):
    vmem = pl.BlockSpec(memory_space=pltpu.VMEM)
    away = jax.ShapeDtypeStruct((ROWS, HD), bf16)
    return pl.pallas_call(
        merge_kernel,
        out_shape=(jax.ShapeDtypeStruct((ROWS, HD), f32), away, away, away),
        in_specs=[vmem] * 2,
        out_specs=(vmem,) * 4,
        compiler_params=pltpu.CompilerParams(vmem_limit_bytes=12 * MIB),
        cost_estimate=SMALL,
        name="merge",
    )(keep, came)


def turned_columns(block):
    return jnp.concatenate(
        [block[:, at * 256 : at * 256 + 256] for at in (0, 4, 1, 5, 2, 6, 3, 7)], axis=1
    )


def turned_place(index):
    return (index % 2) * 4 + index // 2


def feed_kernel(normed_ref, grad_ref, near_ref, far_ref, near_out_ref, far_out_ref, part_ref):
    normed = turned_columns(normed_ref[...].reshape(256, D))
    grad = turned_columns(grad_ref[...].reshape(256, D))
    for weight_ref, out_ref in ((near_ref, near_out_ref), (far_ref, far_out_ref)):
        wide = plain_dot(normed, weight_ref[:, :768])
        gate, up = wide[:, :384], wide[:, 384:]
        grad_act = plain_dot(grad, weight_ref[:, 768:])
        sigma = jax.nn.sigmoid(gate)
        silu = gate * sigma
        grad_gate = grad_act * up * sigma * (1.0 + gate * (1.0 - sigma))
        out_ref[:, :384] = grad_gate.astype(bf16)
        out_ref[:, 384:768] = (grad_act * silu).astype(bf16)
        out_ref[:, 768:] = (silu * up).astype(bf16)
    part = right_dot(near_out_ref[:, :768], near_ref[:, :768])
    part = part + right_dot(far_out_ref[:, :768], far_ref[:, :768])
    for index in range(8):
        at = turned_place(index) * 256
        part_ref[:, at : at + 256] = part[:, index * 256 : index * 256 + 256].astype(bf16)


def feed(normed, grad, near, far):
    rows = pl.BlockSpec((4, 64, D), lambda i: (i, 0, 0))
    tile = pl.BlockSpec((256, D), lambda i: (i, 0))
    weight = pl.BlockSpec((D, 1152), lambda i: (0, 0))
    out = pl.BlockSpec((256, 1152), lambda i: (i, 0))
    return pl.pallas_call(
        feed_kernel,
        grid=(2,),
        out_shape=(
            pltpu.HBM((512, 1152), bf16),
            pltpu.HBM((512, 1152), bf16),
            pltpu.HBM((512, D), bf16),
        ),
        in_specs=[rows, rows, weight, weight],
        out_specs=(out, out, tile),
        compiler_params=pltpu.CompilerParams(vmem_limit_bytes=44 * MIB),
        cost_estimate=SMALL,
        name="feed",
    )(normed, grad, near, far)


def weights_grad_kernel(
    normed_near_ref,
    normed_far_ref,
    grad_near_ref,
    grad_far_ref,
    near_ref,
    far_ref,
    out_ref,
    near_turned_ref,
    far_turned_ref,
):
    @pl.when(pl.program_id(0) == 0)
    def _():
        near_turned_ref[...] = near_ref[...].T
        far_turned_ref[...] = far_ref[...].T

    wide = plain_dot(near_turned_ref[:768, :], normed_near_ref[...].reshape(512, 256))
    wide = wide + plain_dot(far_turned_ref[:768, :], normed_far_ref[...].reshape(512, 256))
    down = plain_dot(near_turned_ref[768:, :], grad_near_ref[...].reshape(512, 256))
    down = down + plain_dot(far_turned_ref[768:, :], grad_far_ref[...].reshape(512, 256))
    out_ref[0, :768, :] = wide.astype(bf16)
    out_ref[0, 768:, :] = down.astype(bf16)


def weights_grad(normed, grad, hidden, earlier):
    rows = pl.BlockSpec((8, 64, 256), lambda i: (0, 0, i))
    whole = pl.BlockSpec((512, 1152), lambda i: (0, 0))
    return pl.pallas_call(
        ordered(weights_grad_kernel, 6, earlier),
        grid=(8,),
        out_shape=pltpu.HBM((8, 1152, 256), bf16),
        in_specs=[rows] * 4 + [whole] * 2 + unread(earlier),
        out_specs=pl.BlockSpec((1, 1152, 256), lambda i: (i % 4 * 2 + i // 4, 0, 0)),
        scratch_shapes=[pltpu.VMEM((1152, 512), bf16)] * 2,
        compiler_params=pltpu.CompilerParams(vmem_limit_bytes=24 * MIB),
        cost_estimate=SMALL,
        name="weights_grad",
    )(*normed, *grad, *hidden, *earlier)


def down_kernel(
    place_ref, near_act_ref, far_act_ref, near_ref, far_ref, hidden_ref, out_ref, total_ref
):
    chip = place_ref[0]
    total = right_dot(near_act_ref[...], near_ref[...])
    total_ref[...] = total + right_dot(far_act_ref[...], far_ref[...])

    @pl.when(pl.program_id(0) == chip // 4)
    def _():
        rows = pl.ds(pl.multiple_of((chip % 4) * 64, 64), 64)
        total_ref[rows, :] += turned_columns(hidden_ref[...])

    for index in range(8):
        cols = total_ref[:, index * 256 : index * 256 + 256]
        out_ref[turned_place(index)] = cols.astype(bf16)


def down(chip, near_act, far_act, near, far, hidden, earlier):
    weight = pl.BlockSpec((D, 384), lambda i: (0, 2))
    return pl.pallas_call(
        ordered(down_kernel, 6, earlier),
        grid=(2,),
        out_shape=pltpu.HBM((8, 512, 256), bf16),
        in_specs=[
            pl.BlockSpec(memory_space=pltpu.SMEM),
            pl.BlockSpec((256, 384), lambda i: (i, 2)),
            pl.BlockSpec((256, 384), lambda i: (i, 2)),
            weight,
            weight,
            pl.BlockSpec((64, D), lambda i: (0, 0)),
            *unread(earlier),
        ],
        out_specs=pl.BlockSpec((8, 256, 256), lambda i: (0, i, 0)),
        scratch_shapes=[pltpu.VMEM((256, D), f32)],
        compiler_params=pltpu.CompilerParams(vmem_limit_bytes=24 * MIB),
        cost_estimate=SMALL,
        name="down",
    )(chip, near_act, far_act, near, far, hidden, *earlier)


def input_part_kernel(
    place_ref,
    near_ref,
    far_ref,
    near_weight_ref,
    far_weight_ref,
    rows_ref,
    gain_ref,
    hidden_ref,
    mlp_ref,
    head_ref,
    out_ref,
    total_ref,
    term_ref,
    sum_ref,
):
    step = pl.program_id(0)
    part = right_dot(near_ref[...], near_weight_ref[...])
    part = part + right_dot(far_ref[...], far_weight_ref[...])
    rows = rows_ref[...].astype(f32)
    inverse = inverse_rms(rows)
    gain = gain_ref[...]
    weighted = part * (rows * inverse)
    term = jnp.sum(weighted * gain, axis=1, keepdims=True) * (1.0 / D)
    term_ref[pl.ds(step, 1), :] = jnp.broadcast_to(term, (256, 128)).T[:1, :]
    sums = jnp.sum(weighted.reshape(32, 8, D), axis=0)

    @pl.when(step == 0)
    def _():
        sum_ref[...] = sums

    @pl.when(step > 0)
    def _():
        sum_ref[...] += sums

    total_ref[...] = part * (gain * inverse)
    hidden = hidden_ref[...]
    for span in range(2):
        own = pl.ds(pl.multiple_of(span * 128 + place_ref[0] * 16, 16), 16)
        total_ref[own, :] += hidden[span * 16 : span * 16 + 16, :]
    at = pl.ds(pl.multiple_of(step * 256, 256), 256)
    for index in range(8):
        cols = total_ref[:, index * 256 : index * 256 + 256]
        out_ref[index, at, :] = cols.astype(bf16)

    @pl.when(step == 1)
    def _():
        terms = term_ref[:2, :]
        coarse = terms.astype(bf16).astype(f32)
        totals = jnp.sum(sum_ref[...], axis=0, keepdims=True)
        extra = jnp.concatenate(
            [coarse, terms - coarse]
            + [totals[:, index * 256 : index * 256 + 256] for index in range(8)]
            + [mlp_ref[...], head_ref[...], jnp.zeros((11, 256), f32)],
            axis=0,
        ).astype(bf16)
        for index in range(8):
            out_ref[index, 512:, :] = extra


def input_part(
    place, near, far, near_weight, far_weight, rows, gain, hidden, mlp, head, earlier
):
    def fixed(*shape):
        return pl.BlockSpec(shape, lambda i, place_ref: (0,) * len(shape))

    def tile(*shape):
        return pl.BlockSpec(shape, lambda i, place_ref: (i, 0))

    def own(*shape):
        return pl.BlockSpec(shape, lambda i, place_ref: (place_ref[1] * 2 + i, 0))

    return pl.pallas_call(
        ordered(input_part_kernel, 10, earlier),
        out_shape=pltpu.HBM((8, 544, 256), bf16),
        grid_spec=pltpu.PrefetchScalarGridSpec(
            num_scalar_prefetch=1,
            grid=(2,),
            in_specs=[
                tile(256, 256),
                tile(256, 256),
                fixed(D, 256),
                fixed(D, 256),
                own(256, D),
                fixed(1, D),
                tile(32, D),
                fixed(8, 256),
                fixed(1, 256),
                *unread(earlier),
            ],
            out_specs=fixed(8, 544, 256),
            scratch_shapes=[
                pltpu.VMEM((256, D), f32),
                pltpu.VMEM((8, 256), f32),
                pltpu.VMEM((8, D), f32),
            ],
        ),
        compiler_params=pltpu.CompilerParams(vmem_limit_bytes=28 * MIB),
        cost_estimate=SMALL,
        name="input_part",
    )(place, near, far, near_weight, far_weight, rows, gain, hidden, mlp, head, *earlier)


def attention_grads_kernel(normed_ref, grad_ref, grad_out_ref, out_ref, turned_ref):
    @pl.when(pl.program_id(0) == 0)
    def _():
        turned_ref[...] = grad_ref[...].T

    out_ref[0, :256, :] = plain_dot(turned_ref[...], normed_ref[...]).astype(bf16)
    out_ref[0, 256:, :] = grad_out_ref[...]


def attention_grads(normed, grad_proj, grad_out, earlier):
    return pl.pallas_call(
        ordered(attention_grads_kernel, 3, earlier),
        grid=(8,),
        out_shape=jax.ShapeDtypeStruct((8, 384, 256), bf16),
        in_specs=[
            pl.BlockSpec((ROWS, 256), lambda i: (0, i)),
            pl.BlockSpec((ROWS, 256), lambda i: (0, 0)),
            pl.BlockSpec((HD, 256), lambda i: (0, i)),
            *unread(earlier),
        ],
        out_specs=pl.BlockSpec((1, 384, 256), lambda i: (i % 4 * 2 + i // 4, 0, 0)),
        scratch_shapes=[pltpu.VMEM((256, ROWS), bf16)],
        compiler_params=pltpu.CompilerParams(vmem_limit_bytes=12 * MIB),
        cost_estimate=SMALL,
        name="attention_grads",
    )(normed, grad_proj, grad_out, *earlier)


def body(
    inputs,
    out_grad,
    lengths,
    span_order,
    w_query,
    w_key,
    w_value,
    w_out,
    w_gate,
    w_up,
    w_down,
    norm_attn,
    norm_mlp,
    norm_query,
    norm_key,
):
    xl, z, xh, y, core = (lax.axis_index(name) for name in ("xl", "z", "xh", "y", "c"))
    span_place = xl * 4 + z
    chip = xh * 4 + y
    first = core == 0

    def by_core(near, far, axis=0):
        join = jnp.stack if axis is None else lambda parts: jnp.concatenate(parts, axis=axis)
        return jnp.where(first, join([near, far]), join([far, near]))

    def split(block):
        near = lax.dynamic_slice_in_dim(block, core * 512, 512, 0)
        far = lax.dynamic_slice_in_dim(block, (1 - core) * 512, 512, 0)
        return near, far

    def chip_major(block):
        return block.reshape(4, 8, 16, -1).transpose(1, 0, 2, 3).reshape(512, -1)

    def span_major(block):
        return block.reshape(8, 4, 16, -1).transpose(1, 0, 2, 3).reshape(512, -1)

    gains = jnp.concatenate([norm_attn, norm_mlp, norm_query, norm_key])
    gains = jnp.pad(gains, (0, 16 * 256 - 544)).reshape(16, 256)
    shard = jnp.concatenate(
        [jnp.concatenate([w_query, w_key, w_value], axis=1), gains], axis=0
    )
    spread_weights = spread(shard, SPANS, 8)
    qkv_weights = spread_weights[:, :256].reshape(D, 256)
    gains = spread_weights[:, 256:259].reshape(8, 768).astype(f32)
    gain_attn = gains[:, :256].reshape(1, D)
    gain_mlp = gains[:, 256:512].reshape(1, D)
    gain_query = gains[:, 512:528].reshape(1, HD)
    gain_key = gains[:, 528:544].reshape(1, HD)
    key_half, value_half = qkv_weights[:, 128:192], qkv_weights[:, 192:256]
    other_half = swap(jnp.where(first, value_half, key_half))
    near_weight = jnp.where(
        first,
        jnp.concatenate([qkv_weights[:, :192], other_half], 1),
        jnp.concatenate([qkv_weights[:, :128], other_half, value_half], 1),
    )

    route, starts, low = routes(jnp.stack([span_place, xl, z]), lengths, span_order)

    def reorder(index, rows):
        return plain_dot(route[index], rows).astype(bf16)

    moving = lax.dynamic_index_in_dim(
        out_grad.reshape(8, 16, 8, D), chip * 2 + core, 1, keepdims=False
    ).reshape(64, D)
    moving = reorder(0, moving).reshape(8, 8, D)
    spread_out = jnp.broadcast_to(w_out.reshape(1, 16, D), (8, 16, D))
    moving = jnp.concatenate([moving, spread_out], axis=1)
    arrived = exchange(after(moving, qkv_weights), SPANS)
    out_weights = arrived[:, 8:].reshape(8, HD, 256)
    moving = arrived[:, :8].reshape(64, D)

    ends = jnp.cumsum(lax.dynamic_index_in_dim(lengths, xl, 0, keepdims=False))
    offset = z * ROWS + jnp.arange(ROWS, dtype=jnp.int32)
    doc_start = jnp.where(offset >= ends[1], ends[1], jnp.where(offset >= ends[0], ends[0], 0))
    frequency = jnp.power(rope_base, -2.0 * jnp.arange(HD // 2, dtype=f32) / HD)
    angles = (offset - doc_start).astype(f32)[:, None] * frequency[None, :]
    cos_table, sin_table = jnp.cos(angles), jnp.sin(angles)
    cos_table = jnp.concatenate([cos_table, cos_table], axis=1)
    sin_table = jnp.concatenate([-sin_table, sin_table], axis=1)

    normed, inverse_one, query_bf, own_kv, query_proj, kv_proj = project(
        core.reshape(1),
        in_hbm(inputs),
        gain_attn,
        near_weight,
        cos_table,
        sin_table,
        gain_query,
        gain_key,
    )
    ready_kv = after(own_kv, arrived)
    moving = after(reorder(1, moving), own_kv)
    moving = exchange(moving.reshape(8, 8, D), SPANS).reshape(64, D)
    moving = reorder(2, moving).reshape(8, 8, D)
    near = lax.dynamic_slice_in_dim(moving, core * 4, 4, 0)
    far = lax.dynamic_slice_in_dim(moving, (1 - core) * 4, 4, 0)
    own_grad = by_core(near, swap(far), 1).reshape(64, D)
    spread_grad = jnp.broadcast_to(own_grad[None], (8, 64, D))
    grad_mine = exchange(spread_grad, CHIPS)

    mine = jnp.concatenate(
        [onward(ready_kv, 3), onward(ready_kv, 2), onward(ready_kv, 1), own_kv], axis=0
    )
    mine = after(mine, spread_grad)
    other = swap(mine)
    all_keys = jnp.where(first, mine, other)
    all_values = jnp.where(first, other, mine)

    out_weights = out_weights.transpose(1, 0, 2).reshape(HD, D)
    out_two = jnp.concatenate([out_weights, swap(out_weights)], axis=0)

    mlp_shard = after(jnp.concatenate([w_gate, w_up, w_down.T], axis=1), qkv_weights)
    far_shard = after(far_span(mlp_shard), mine)
    mlp_shard = jnp.where(
        xl == 0,
        jnp.concatenate([mlp_shard, far_shard]),
        jnp.concatenate([far_shard, mlp_shard]),
    )
    near_weights = lax.all_gather(mlp_shard, "z", axis=0, tiled=True)
    far_weights = swap(near_weights)

    attended, attended_full, total = attend(
        low,
        starts,
        in_hbm(query_bf),
        in_hbm(all_keys),
        in_hbm(all_values),
        [fence(spread_grad), out_two, mlp_shard],
    )

    att_near, att_far = split(attended)
    att_two = jnp.concatenate(
        [chip_major(att_near), swap(chip_major(after(att_far, grad_mine)))], axis=1
    )
    branch = plain_dot(att_two, out_two).astype(bf16)
    branch = branch.reshape(8, 64, D)
    branch = jnp.sum(exchange(branch, CHIPS).astype(f32), axis=0)
    own_rows = lax.dynamic_slice_in_dim(inputs, core * 512, 512, 0).reshape(4, 8, 16, D)
    own_rows = lax.dynamic_index_in_dim(own_rows, chip, 1, keepdims=False).reshape(64, D)
    hidden = own_rows.astype(f32) + branch
    inverse_two = inverse_rms(hidden)
    normal_two = hidden * inverse_two
    normed_mlp = (normal_two * gain_mlp).astype(bf16)
    normed_mine = spread(normed_mlp, CHIPS, 8)

    near_out, far_out, part = feed(normed_mine, grad_mine, near_weights, far_weights)
    mlp_grads = weights_grad(
        (normed_mine, swap(normed_mine)),
        (grad_mine, swap(grad_mine)),
        (near_out, swap(far_out)),
        [fence(part)],
    )
    part = exchange(part.reshape(8, 64, D), CHIPS)
    part, mlp_grads = lax.optimization_barrier((part, mlp_grads))
    grad_normed_mlp = jnp.sum(part.astype(f32), axis=0)

    def by_span(block):
        sent = lax.dynamic_index_in_dim(block, 1 - xl, 0, keepdims=False)
        return lax.dynamic_index_in_dim(block, xl, 0, keepdims=False), far_span(sent)

    mlp_grads = lax.psum_scatter(mlp_grads, "z", scatter_dimension=0, tiled=True)

    gain_mlp_part = jnp.sum(grad_normed_mlp * normal_two, axis=0)
    grad_hidden = own_grad.astype(f32) + norm_back(
        grad_normed_mlp * gain_mlp, normal_two, inverse_two
    )
    grad_branch = grad_hidden.astype(bf16)
    out_cols = down(
        chip.reshape(1),
        near_out,
        far_out,
        near_weights,
        far_weights,
        hidden,
        [fence(grad_branch)],
    )
    far_weight = swap(near_weight)
    branch_mine = spread(grad_branch, CHIPS, 8).reshape(512, D)
    branch_mine = after(branch_mine, out_cols, far_weight)
    out_cols = after(out_cols, branch_mine)
    out_fence = fence(out_cols)
    out_cols = exchange(out_cols, CHIPS)
    grad_two = right_dot(branch_mine, out_two).astype(bf16)
    grad_att = by_core(span_major(grad_two[:, :HD]), span_major(swap(grad_two[:, HD:])))

    grad_query_rot, keep, send = attend_back(
        low,
        core.reshape(1),
        starts,
        in_hbm(query_bf),
        in_hbm(all_keys),
        in_hbm(all_values),
        grad_att,
        in_hbm(attended_full),
        total,
        [out_fence],
    )
    came = swap(send)
    own_kv_grad, *away = merge(keep, came)
    received = [backward(block, by + 1) for by, block in enumerate(away)]

    def unorder(index, rows):
        return left_dot(route[index], rows).astype(bf16)

    grad_out = left_dot(att_two, after(branch_mine, received[2]))
    grad_out = (grad_out[:HD] + swap(grad_out[HD:].astype(bf16)).astype(f32)).astype(bf16)
    grad_proj, head_gains = project_back(
        core.reshape(1),
        in_hbm(grad_query_rot),
        own_kv_grad,
        received,
        in_hbm(cos_table),
        in_hbm(sin_table),
        (in_hbm(query_proj), in_hbm(kv_proj)),
        (gain_query, gain_key),
        [mlp_grads],
    )

    grad_near, grad_far = split(grad_proj)
    by_cols = input_part(
        jnp.stack([chip, core]),
        grad_near,
        swap(grad_far),
        in_hbm(near_weight),
        in_hbm(far_weight),
        in_hbm(inputs),
        gain_attn,
        in_hbm(grad_hidden),
        gain_mlp_part.reshape(8, 256),
        head_gains,
        [],
    )
    mlp_kept, mlp_came = by_span(after(mlp_grads, grad_proj))
    grad_attn = attention_grads(normed, grad_proj, grad_out, [fence(by_cols), mlp_came])
    out_cols = after(out_cols, grad_attn)
    grad_attn = grad_attn.reshape(4, 2, 384, 256)
    parts = [
        lax.dynamic_index_in_dim(grad_attn, (z + by) % 4, 0, keepdims=False) for by in range(4)
    ]
    parts = [parts[0]] + [
        lax.ppermute(parts[by], "z", [(i, (i + by) % 4) for i in range(4)]) for by in (1, 2, 3)
    ]
    out_cols = jnp.sum(out_cols.astype(f32), axis=0).astype(bf16)
    near = jnp.where(first, out_cols[:, :128], out_cols[:, 128:])
    far = jnp.where(first, out_cols[:, 128:], out_cols[:, :128])
    out_cols = by_core(near, swap(far), None).reshape(2, 8, 4, 2, 8, 128)
    out_rows = jnp.concatenate(
        [out_cols[:, index // 2, :, index % 2].reshape(64, 128) for index in range(16)], axis=1
    )

    by_cols = exchange(by_cols, CHIPS)

    out_rows = exchange(after(unorder(2, out_rows).reshape(8, 8, D), by_cols), SPANS)
    parts = lax.optimization_barrier((*parts, by_cols))[:4]
    grad_attn = sum(part.astype(f32) for part in parts)
    attn_kept, attn_came = by_span(grad_attn.astype(bf16))
    by_cols = jnp.sum(by_cols.astype(f32), axis=0)
    row_term = (by_cols[512:514] + by_cols[514:516]).reshape(512, 1)
    own_inverse = lax.dynamic_slice_in_dim(inverse_one, core * 512, 512, 0)
    own_cols = lax.dynamic_slice(inputs, (core * 512, chip * 256), (512, 256)).astype(f32)
    in_grad = by_cols[:512] - own_cols * (own_inverse * own_inverse * row_term)
    near = jnp.where(first, in_grad[:, :128], in_grad[:, 128:])
    far = jnp.where(first, in_grad[:, 128:], in_grad[:, :128])
    in_grad = by_core(near, swap(far))
    gain_sums = jnp.concatenate(
        [
            by_cols[516:524],
            by_cols[524:532],
            by_cols[532, :128].reshape(8, 16),
            by_cols[532, 128:].reshape(8, 16),
        ],
        axis=1,
    )
    gain_sums = gain_sums + swap(gain_sums)
    coarse = gain_sums.astype(bf16)
    extra = jnp.concatenate(
        [coarse, (gain_sums - coarse.astype(f32)).astype(bf16), jnp.zeros((8, 960), bf16)], axis=1
    )
    extra = jnp.pad(extra[:, None], ((0, 0), (0, 7), (0, 0)))
    out_rows = unorder(1, out_rows.reshape(64, D)).reshape(8, 8, D)
    out_rows = after(jnp.concatenate([out_rows, extra], axis=1), attn_came)
    out_rows = exchange(out_rows, SPANS)
    gain_sums = jnp.sum(out_rows[:, 8].astype(f32), axis=0)
    gain_sums = gain_sums[:544] + gain_sums[544:1088]
    layer_out = unorder(0, out_rows[:, :8].reshape(64, D))
    layer_out = jnp.stack(
        [layer_out[:, at * 128 : at * 128 + 128].reshape(8, 8, 128) for at in range(16)],
        axis=1,
    )
    layer_out = layer_out.reshape(ROWS, 128).astype(f32)

    grad_attn = attn_kept.astype(f32) + attn_came.astype(f32)
    grad_kv_weight = grad_attn[128:256]
    low_half, high_half = grad_kv_weight[:64], grad_kv_weight[64:]
    came = swap(jnp.where(first, high_half, low_half))
    kept = jnp.where(first, low_half, high_half)
    mlp_grads = mlp_kept.astype(f32) + mlp_came.astype(f32)

    return (
        layer_out,
        in_grad,
        grad_attn[:128].T,
        jnp.where(first, kept, came).T,
        jnp.where(first, came, kept).T,
        grad_attn[256:],
        mlp_grads[:384].T,
        mlp_grads[384:768].T,
        mlp_grads[768:],
        gain_sums[:256],
        gain_sums[256:512],
        gain_sums[512:528],
        gain_sums[528:544],
    )


def solution(mesh):
    fine = Mesh(mesh.devices.reshape(2, 4, 2, 4, 2), ("xl", "z", "xh", "y", "c"))
    rows = P(SPANS, None)
    by_both = P(SPANS, TENSOR)
    turned = P(TENSOR, SPANS)
    lone = P(SPANS)
    return jax.shard_map(
        body,
        mesh=fine,
        in_specs=(
            rows,
            rows,
            P(),
            P(),
            by_both,
            by_both,
            by_both,
            turned,
            by_both,
            by_both,
            turned,
            lone,
            lone,
            lone,
            lone,
        ),
        out_specs=(
            by_both,
            by_both,
            by_both,
            by_both,
            by_both,
            turned,
            by_both,
            by_both,
            turned,
            lone,
            lone,
            lone,
            lone,
        ),
        check_vma=False,
    )
```

```python
import jax
import jax.numpy as jnp
from jax import lax
from jax.experimental import pallas as pl
from jax.experimental.pallas import tpu as pltpu
from jax.sharding import Mesh, PartitionSpec as P

SPAN = 128
MICRO = 2
HD = 128
D = 2048
ROWS = 1024
KEYS = 4096
KEY_BLK = 512

epsilon = 1e-06
rope_base = 1000000.0
score_scale = HD ** (-0.5)
log2e = 1.4426950408889634
bf16 = jnp.bfloat16
f32 = jnp.float32
SPANS = ("xl", "z")
TENSOR = ("xh", "y", "c")
CHIPS = ("xh", "y")
MIB = 1024 * 1024
SMALL = pl.CostEstimate(flops=1024, bytes_accessed=1024, transcendentals=0)


def swap(block):
    return lax.ppermute(block, "c", [(0, 1), (1, 0)])


def far_span(block):
    return lax.ppermute(block, "xl", [(0, 1), (1, 0)])


def onward(block, by):
    return lax.ppermute(block, "z", [(i, i + by) for i in range(4) if i + by < 4])


def backward(block, by):
    return lax.ppermute(block, "z", [(i, i - by) for i in range(4) if i - by >= 0])


def exchange(block, axes):
    return lax.all_to_all(block, axes, 0, 0, tiled=True)


def spread(block, axes, count):
    return exchange(jnp.broadcast_to(block[None], (count,) + block.shape), axes)


def after(block, *earlier):
    return lax.optimization_barrier((block,) + earlier)[0]


def fence(block):
    return swap(block.reshape(-1, block.shape[-1])[:512, :256])


def ordered(kernel, inputs, earlier):
    return lambda *refs: kernel(*refs[:inputs], *refs[inputs + len(earlier) :])


def in_hbm(block):
    return pltpu.with_memory_space_constraint(block, pltpu.HBM)


def unread(earlier):
    return [pl.BlockSpec(memory_space=pl.ANY)] * len(earlier)


def plain_dot(first_op, second_op):
    return jnp.dot(first_op, second_op, preferred_element_type=f32)


def left_dot(first_op, second_op):
    return lax.dot_general(
        first_op, second_op, (((0,), (0,)), ((), ())), preferred_element_type=f32
    )


def right_dot(first_op, second_op):
    return lax.dot_general(
        first_op, second_op, (((1,), (1,)), ((), ())), preferred_element_type=f32
    )


def inverse_rms(values):
    return lax.rsqrt(jnp.mean(values * values, axis=-1, keepdims=True) + epsilon)


def norm_back(incoming, normal, inverse):
    return inverse * (incoming - normal * jnp.mean(incoming * normal, axis=-1, keepdims=True))


def block_mask(key_block, starts):
    key_at = key_block * KEY_BLK + lax.broadcasted_iota(jnp.int32, (KEY_BLK, ROWS), 0)
    query_at = (KEYS - ROWS) + lax.broadcasted_iota(jnp.int32, (KEY_BLK, ROWS), 1)
    return (key_at >= starts) & (key_at <= query_at)


def over_keys(range_ref, step, state):
    own = (KEYS - ROWS) // KEY_BLK
    seen = jnp.minimum(range_ref[1], own)
    state = lax.fori_loop(range_ref[0], seen, lambda at, state: step(at, state, True), state)
    state = lax.fori_loop(seen, own, lambda at, state: step(at, state, False), state)
    for at in range(own, KEYS // KEY_BLK):
        state = step(at, state, True)
    return state


def attend_kernel(range_ref, start_ref, q_ref, k_ref, v_ref, out_ref, full_ref, total_ref):
    queries = q_ref[...]
    starts = start_ref[...]

    def step(at, state, masked):
        acc, total = state
        rows = pl.ds(pl.multiple_of(at * KEY_BLK, KEY_BLK), KEY_BLK)
        weights = jnp.exp2(right_dot(k_ref[rows, :], queries) * (score_scale * log2e))
        if masked:
            weights = jnp.where(block_mask(at, starts), weights, 0.0)
        total = total + jnp.sum(weights, axis=0, keepdims=True)
        acc = acc + left_dot(v_ref[rows, :], weights.astype(bf16))
        return acc, total

    acc, total = over_keys(
        range_ref, step, (jnp.zeros((HD, ROWS), f32), jnp.zeros((1, ROWS), f32))
    )
    full = acc / total
    full_ref[...] = full
    total_ref[...] = jnp.log2(total)
    out_ref[...] = full.T.astype(bf16)


def attend(low, starts, queries, keys, values, earlier):
    vmem = pl.BlockSpec(memory_space=pltpu.VMEM)
    return pl.pallas_call(
        ordered(attend_kernel, 5, earlier),
        out_shape=(
            jax.ShapeDtypeStruct((ROWS, HD), bf16),
            pltpu.HBM((HD, ROWS), f32),
            jax.ShapeDtypeStruct((1, ROWS), f32),
        ),
        in_specs=[pl.BlockSpec(memory_space=pltpu.SMEM)] + [vmem] * 4 + unread(earlier),
        out_specs=(vmem,) * 3,
        compiler_params=pltpu.CompilerParams(vmem_limit_bytes=24 * MIB),
        cost_estimate=SMALL,
        name="attend",
    )(low, starts, queries, keys, values, *earlier)


def attend_back_kernel(
    range_ref,
    core_ref,
    start_ref,
    q_ref,
    k_ref,
    v_ref,
    do_ref,
    full_ref,
    total_ref,
    dq_ref,
    keep_ref,
    send_ref,
    dk_ref,
    dv_ref,
):
    dk_ref[...] = jnp.zeros_like(dk_ref)
    dv_ref[...] = jnp.zeros_like(dv_ref)
    queries = q_ref[...]
    starts = start_ref[...]
    incoming = do_ref[...]
    total = total_ref[...]
    delta = jnp.sum(incoming.astype(f32).T * full_ref[...], axis=0, keepdims=True)

    def step(at, acc, masked):
        rows = pl.ds(pl.multiple_of(at * KEY_BLK, KEY_BLK), KEY_BLK)
        keys = k_ref[rows, :]
        weights = jnp.exp2(right_dot(keys, queries) * (score_scale * log2e) - total)
        if masked:
            weights = jnp.where(block_mask(at, starts), weights, 0.0)
        grads = right_dot(v_ref[rows, :], incoming)
        grads = (weights * (grads - delta)).astype(bf16)
        dv_ref[rows, :] += plain_dot(weights.astype(bf16), incoming)
        dk_ref[rows, :] += plain_dot(grads, queries)
        return acc + left_dot(keys, grads)

    dq_ref[...] = over_keys(range_ref, step, jnp.zeros((HD, ROWS), f32)).T * score_scale

    @pl.when(core_ref[0] == 0)
    def _():
        keep_ref[...] = dk_ref[...] * score_scale
        send_ref[...] = dv_ref[...].astype(bf16)

    @pl.when(core_ref[0] == 1)
    def _():
        keep_ref[...] = dv_ref[...]
        send_ref[...] = (dk_ref[...] * score_scale).astype(bf16)


def attend_back(low, core, starts, queries, keys, values, incoming, full, total, earlier):
    vmem = pl.BlockSpec(memory_space=pltpu.VMEM)
    smem = pl.BlockSpec(memory_space=pltpu.SMEM)
    return pl.pallas_call(
        ordered(attend_back_kernel, 9, earlier),
        out_shape=(
            pltpu.HBM((ROWS, HD), f32),
            jax.ShapeDtypeStruct((KEYS, HD), f32),
            jax.ShapeDtypeStruct((KEYS, HD), bf16),
        ),
        in_specs=[smem, smem] + [vmem] * 7 + unread(earlier),
        out_specs=(vmem,) * 3,
        scratch_shapes=[pltpu.VMEM((KEYS, HD), f32), pltpu.VMEM((KEYS, HD), f32)],
        compiler_params=pltpu.CompilerParams(vmem_limit_bytes=32 * MIB),
        cost_estimate=SMALL,
        name="attend_back",
    )(low, core, starts, queries, keys, values, incoming, full, total, *earlier)


def colour_kernel(place_ref, lengths_ref, column_ref, row_ref, out_ref, start_ref, range_ref):
    micro, block = place_ref[1], place_ref[2]
    first_end = lengths_ref[micro, 0]
    second_end = first_end + lengths_ref[micro, 1]

    def begin(offset):
        begun = jnp.where(offset >= first_end, first_end, 0)
        begun = jnp.where(offset >= second_end, second_end, begun)
        return begun - (block - 3) * ROWS

    start_ref[...] = begin(block * ROWS + lax.broadcasted_iota(jnp.int32, (1, ROWS), 1))
    range_ref[0] = begin(block * ROWS) >> 9
    range_ref[1] = (begin(block * ROWS + ROWS - 1) + KEY_BLK - 1) >> 9
    down_at = lax.broadcasted_iota(jnp.int32, (64, 64), 0)
    across_at = lax.broadcasted_iota(jnp.int32, (64, 64), 1)
    same_slots = (down_at >> 3) == (across_at >> 3)
    same_spans = (column_ref[...] >> 3) == (row_ref[...] >> 3)
    colour = jnp.zeros((64, 1), jnp.int32)
    for _ in range(3):
        colour_row = jnp.sum(
            jnp.where(down_at == across_at, colour, 0).astype(f32), axis=0, keepdims=True
        ).astype(jnp.int32)
        alike = colour == colour_row

        def partner(group):
            near = group & alike
            rank_down = jnp.sum(
                jnp.where(near & (across_at < down_at), 1.0, 0.0), axis=1, keepdims=True
            ).astype(jnp.int32)
            rank_across = jnp.sum(
                jnp.where(near & (down_at < across_at), 1.0, 0.0), axis=0, keepdims=True
            ).astype(jnp.int32)
            return jnp.where(near & ((rank_down ^ 1) == rank_across), 1.0, 0.0)

        by_slot = partner(same_slots)
        jump = plain_dot(by_slot, partner(same_spans))
        label = lax.broadcasted_iota(jnp.int32, (64, 128), 0).astype(f32)
        for turn in range(5):
            label = jnp.minimum(label, plain_dot(jump, label))
            if turn < 4:
                jump = plain_dot(jump, jump)
        bit = jnp.where(label > plain_dot(by_slot, label), 1, 0)
        colour = colour * 2 + bit[:, :1]
    colour_row = jnp.sum(
        jnp.where(down_at == across_at, colour, 0).astype(f32), axis=0, keepdims=True
    )
    own = place_ref[0]
    same_row = (down_at & 7) == (across_at & 7)
    slot_colour = jnp.sum(
        jnp.where(down_at == own * 8 + (across_at >> 3), colour, 0).astype(f32),
        axis=0,
        keepdims=True,
    ).astype(jnp.int32)
    owner = jnp.sum(
        jnp.where(same_slots & (colour == own), column_ref[...] >> 3, 0).astype(f32),
        axis=0,
        keepdims=True,
    ).astype(jnp.int32)
    span_colour = jnp.sum(
        jnp.where(row_ref[...] == own * 8 + (down_at >> 3), colour_row, 0.0),
        axis=1,
        keepdims=True,
    ).astype(jnp.int32)
    for index, match in enumerate(
        (
            slot_colour == (down_at >> 3),
            owner == (down_at >> 3),
            span_colour == (across_at >> 3),
        )
    ):
        out_ref[index] = jnp.where(match & same_row, 1.0, 0.0).astype(bf16)


def routes(place, lengths, span_order):
    vmem = pl.BlockSpec(memory_space=pltpu.VMEM)
    smem = pl.BlockSpec(memory_space=pltpu.SMEM)
    return pl.pallas_call(
        colour_kernel,
        out_shape=(
            jax.ShapeDtypeStruct((3, 64, 64), bf16),
            jax.ShapeDtypeStruct((1, ROWS), jnp.int32),
            jax.ShapeDtypeStruct((2,), jnp.int32),
        ),
        in_specs=[smem, smem, vmem, vmem],
        out_specs=(vmem, vmem, smem),
        name="routes",
    )(place, lengths, span_order.reshape(64, 1), span_order.reshape(1, 64))


def project_kernel(
    place_ref,
    rows_ref,
    gain_ref,
    weight_ref,
    cos_ref,
    sin_ref,
    gain_query_ref,
    gain_key_ref,
    normed_ref,
    inverse_ref,
    query_out_ref,
    kv_out_ref,
    query_proj_ref,
    kv_proj_ref,
):
    rows = rows_ref[...].astype(f32)
    inverse = inverse_rms(rows)
    normed = (rows * inverse * gain_ref[...]).astype(bf16)
    inverse_ref[...] = inverse
    normed_ref[...] = normed
    cos, sin = cos_ref[...], sin_ref[...]

    def turned(values):
        return values * cos + pltpu.roll(values, 64, 1) * sin

    proj = plain_dot(normed, weight_ref[...])
    query, kv = proj[:, :HD], proj[:, HD:]
    kv_proj_ref[...] = kv
    key = turned(kv * inverse_rms(kv) * gain_key_ref[...])
    kv_out_ref[...] = jnp.where(place_ref[0] == 0, key, kv).astype(bf16)
    query_proj_ref[...] = query
    query = turned(query * inverse_rms(query) * gain_query_ref[...])
    query_out_ref[...] = query.astype(bf16)


def project(core, rows, gain, weights, cos, sin, gain_query, gain_key):
    wide = pl.BlockSpec((256, D), lambda i: (i, 0))
    head = pl.BlockSpec((256, HD), lambda i: (i, 0))
    one = pl.BlockSpec((256, 1), lambda i: (i, 0))
    weight = pl.BlockSpec((D, 256), lambda i: (0, 0))
    small = pl.BlockSpec((1, HD), lambda i: (0, 0))
    column = pltpu.HBM((ROWS, 1), f32)
    return pl.pallas_call(
        project_kernel,
        grid=(4,),
        out_shape=(
            pltpu.HBM((ROWS, D), bf16),
            column,
            jax.ShapeDtypeStruct((ROWS, HD), bf16),
            jax.ShapeDtypeStruct((ROWS, HD), bf16),
            pltpu.HBM((ROWS, HD), f32),
            pltpu.HBM((ROWS, HD), f32),
        ),
        in_specs=[
            pl.BlockSpec(memory_space=pltpu.SMEM),
            wide,
            pl.BlockSpec((1, D), lambda i: (0, 0)),
            weight,
            head,
            head,
            small,
            small,
        ],
        out_specs=(wide, one, head, head, head, head),
        compiler_params=pltpu.CompilerParams(vmem_limit_bytes=20 * MIB),
        cost_estimate=SMALL,
        name="project",
    )(core, rows, gain, weights, cos, sin, gain_query, gain_key)


def project_back_kernel(
    place_ref,
    query_grad_ref,
    own_ref,
    one_ref,
    two_ref,
    three_ref,
    cos_ref,
    sin_ref,
    query_proj_ref,
    kv_proj_ref,
    gain_query_ref,
    gain_key_ref,
    out_ref,
    sum_ref,
):
    cos, sin = cos_ref[...], sin_ref[...]

    def turned_back(values):
        return values * cos - pltpu.roll(values, 64, 1) * sin

    step = pl.program_id(0)
    grad = turned_back(query_grad_ref[...])
    query = query_proj_ref[...]
    inverse = inverse_rms(query)
    hat = query * inverse
    sums = jnp.sum(grad * hat, axis=0, keepdims=True)
    query = norm_back(grad * gain_query_ref[...], hat, inverse)
    out_ref[:, :HD] = query.astype(bf16)
    kv = own_ref[...] + one_ref[...].astype(f32)
    kv = kv + two_ref[...].astype(f32) + three_ref[...].astype(f32)
    grad = turned_back(kv)
    key = kv_proj_ref[...]
    inverse = inverse_rms(key)
    hat = key * inverse
    is_key = place_ref[0] == 0
    key_sums = jnp.where(is_key, jnp.sum(grad * hat, axis=0, keepdims=True), 0.0)
    key = norm_back(grad * gain_key_ref[...], hat, inverse)
    out_ref[:, HD:] = jnp.where(is_key, key, kv).astype(bf16)
    sums = jnp.concatenate([sums, key_sums], axis=1)

    @pl.when(step == 0)
    def _():
        sum_ref[...] = sums

    @pl.when(step > 0)
    def _():
        sum_ref[...] += sums


def project_back(core, query_grad, own, arrived, cos, sin, projections, gains, earlier):
    head = pl.BlockSpec((256, HD), lambda i: (i, 0))
    small = pl.BlockSpec((1, HD), lambda i: (0, 0))
    return pl.pallas_call(
        ordered(project_back_kernel, 12, earlier),
        grid=(4,),
        out_shape=(
            jax.ShapeDtypeStruct((ROWS, 256), bf16),
            jax.ShapeDtypeStruct((1, 256), f32),
        ),
        in_specs=[pl.BlockSpec(memory_space=pltpu.SMEM)]
        + [head] * 9
        + [small] * 2
        + unread(earlier),
        out_specs=(
            pl.BlockSpec((256, 256), lambda i: (i, 0)),
            pl.BlockSpec((1, 256), lambda i: (0, 0)),
        ),
        compiler_params=pltpu.CompilerParams(vmem_limit_bytes=12 * MIB),
        cost_estimate=SMALL,
        name="project_back",
    )(core, query_grad, own, *arrived, cos, sin, *projections, *gains, *earlier)


def merge_kernel(keep_ref, came_ref, own_ref, one_ref, two_ref, three_ref):
    for block, out_ref in enumerate((three_ref, two_ref, one_ref, own_ref)):
        rows = pl.ds(block * ROWS, ROWS)
        total = keep_ref[rows, :] + came_ref[rows, :].astype(f32)
        out_ref[...] = total.astype(out_ref.dtype)


def merge(keep, came):
    vmem = pl.BlockSpec(memory_space=pltpu.VMEM)
    away = jax.ShapeDtypeStruct((ROWS, HD), bf16)
    return pl.pallas_call(
        merge_kernel,
        out_shape=(jax.ShapeDtypeStruct((ROWS, HD), f32), away, away, away),
        in_specs=[vmem] * 2,
        out_specs=(vmem,) * 4,
        compiler_params=pltpu.CompilerParams(vmem_limit_bytes=12 * MIB),
        cost_estimate=SMALL,
        name="merge",
    )(keep, came)


def norm_kernel(parts_ref, rows_ref, gain_ref, hidden_ref, out_ref):
    hidden = rows_ref[...].astype(f32)
    hidden = hidden + sum(parts_ref[index].astype(f32) for index in range(8))
    hidden_ref[...] = hidden
    normed = (hidden * inverse_rms(hidden) * gain_ref[...]).astype(bf16)
    for index in range(8):
        out_ref[index] = normed


def norm(parts, rows, gain):
    vmem = pl.BlockSpec(memory_space=pltpu.VMEM)
    return pl.pallas_call(
        norm_kernel,
        out_shape=(
            pltpu.HBM((64, D), f32),
            pltpu.HBM((8, 64, D), bf16),
        ),
        in_specs=[vmem] * 3,
        out_specs=(vmem, vmem),
        compiler_params=pltpu.CompilerParams(vmem_limit_bytes=12 * MIB),
        cost_estimate=SMALL,
        name="norm",
    )(in_hbm(parts), rows, gain)


def norm_grad_kernel(
    parts_ref, hidden_ref, gain_ref, grad_ref, hidden_grad_ref, gain_grad_ref, out_ref
):
    grad = sum(parts_ref[index].astype(f32) for index in range(8))
    hidden = hidden_ref[...]
    inverse = inverse_rms(hidden)
    normal = hidden * inverse
    gain_grad_ref[...] = jnp.sum(grad * normal, axis=0, keepdims=True)
    grad = grad_ref[...].astype(f32) + norm_back(grad * gain_ref[...], normal, inverse)
    hidden_grad_ref[...] = grad
    for index in range(8):
        out_ref[index] = grad.astype(bf16)


def norm_grad(parts, hidden, gain, grad):
    vmem = pl.BlockSpec(memory_space=pltpu.VMEM)
    return pl.pallas_call(
        norm_grad_kernel,
        out_shape=(
            pltpu.HBM((64, D), f32),
            jax.ShapeDtypeStruct((1, D), f32),
            pltpu.HBM((8, 64, D), bf16),
        ),
        in_specs=[vmem] * 4,
        out_specs=(vmem,) * 3,
        compiler_params=pltpu.CompilerParams(vmem_limit_bytes=12 * MIB),
        cost_estimate=SMALL,
        name="norm_grad",
    )(in_hbm(parts), hidden, gain, grad)


def turned_columns(block):
    return jnp.concatenate(
        [block[:, at * 256 : at * 256 + 256] for at in (0, 4, 1, 5, 2, 6, 3, 7)], axis=1
    )


def turned_place(index):
    return (index % 2) * 4 + index // 2


def feed_kernel(
    normed_ref,
    grad_ref,
    near_source_ref,
    far_source_ref,
    near_out_ref,
    far_out_ref,
    part_ref,
    near_ref,
    far_ref,
    sems,
):
    copies = [
        pltpu.make_async_copy(near_source_ref, near_ref, sems.at[0]),
        pltpu.make_async_copy(far_source_ref, far_ref, sems.at[1]),
    ]
    first = pl.program_id(0) == 0

    @pl.when(first)
    def _():
        for copy in copies:
            copy.start()

    def arrived(index):
        @pl.when(first)
        def _():
            copies[index].wait()

    normed = turned_columns(normed_ref[...].reshape(256, D))
    grad = turned_columns(grad_ref[...].reshape(256, D))
    for index, (weight_ref, out_ref) in enumerate(
        ((near_ref, near_out_ref), (far_ref, far_out_ref))
    ):
        arrived(index)
        wide = plain_dot(normed, weight_ref[:, :768])
        gate, up = wide[:, :384], wide[:, 384:]
        grad_act = plain_dot(grad, weight_ref[:, 768:])
        sigma = jax.nn.sigmoid(gate)
        silu = gate * sigma
        grad_gate = grad_act * up * sigma * (1.0 + gate * (1.0 - sigma))
        out_ref[:, :384] = grad_gate.astype(bf16)
        out_ref[:, 384:768] = (grad_act * silu).astype(bf16)
        out_ref[:, 768:] = (silu * up).astype(bf16)
    part = right_dot(near_out_ref[:, :768], near_ref[:, :768])
    part = part + right_dot(far_out_ref[:, :768], far_ref[:, :768])
    for index in range(8):
        at = turned_place(index) * 256
        part_ref[:, at : at + 256] = part[:, index * 256 : index * 256 + 256].astype(bf16)


def feed(normed, grad, near, far):
    rows = pl.BlockSpec((4, 64, D), lambda i: (i, 0, 0))
    tile = pl.BlockSpec((256, D), lambda i: (i, 0))
    weight = pl.BlockSpec(memory_space=pl.ANY)
    out = pl.BlockSpec((256, 1152), lambda i: (i, 0))
    return pl.pallas_call(
        feed_kernel,
        grid=(2,),
        out_shape=(
            pltpu.HBM((512, 1152), bf16),
            pltpu.HBM((512, 1152), bf16),
            pltpu.HBM((512, D), bf16),
        ),
        in_specs=[rows, rows, weight, weight],
        out_specs=(out, out, tile),
        scratch_shapes=[
            pltpu.VMEM((D, 1152), bf16),
            pltpu.VMEM((D, 1152), bf16),
            pltpu.SemaphoreType.DMA((2,)),
        ],
        compiler_params=pltpu.CompilerParams(vmem_limit_bytes=36 * MIB),
        cost_estimate=SMALL,
        name="feed",
    )(normed, grad, in_hbm(near), in_hbm(far))


def weights_grad_kernel(
    normed_near_ref,
    normed_far_ref,
    grad_near_ref,
    grad_far_ref,
    near_ref,
    far_ref,
    out_ref,
    near_turned_ref,
    far_turned_ref,
):
    @pl.when(pl.program_id(0) == 0)
    def _():
        near_turned_ref[...] = near_ref[...].T
        far_turned_ref[...] = far_ref[...].T

    wide = plain_dot(near_turned_ref[:768, :], normed_near_ref[...].reshape(512, 256))
    wide = wide + plain_dot(far_turned_ref[:768, :], normed_far_ref[...].reshape(512, 256))
    down = plain_dot(near_turned_ref[768:, :], grad_near_ref[...].reshape(512, 256))
    down = down + plain_dot(far_turned_ref[768:, :], grad_far_ref[...].reshape(512, 256))
    out_ref[0, :768, :] = wide.astype(bf16)
    out_ref[0, 768:, :] = down.astype(bf16)


def weights_grad(normed, grad, hidden, earlier):
    rows = pl.BlockSpec((8, 64, 256), lambda i: (0, 0, i))
    whole = pl.BlockSpec((512, 1152), lambda i: (0, 0))
    return pl.pallas_call(
        ordered(weights_grad_kernel, 6, earlier),
        grid=(8,),
        out_shape=pltpu.HBM((8, 1152, 256), bf16),
        in_specs=[rows] * 4 + [whole] * 2 + unread(earlier),
        out_specs=pl.BlockSpec((1, 1152, 256), lambda i: (i % 4 * 2 + i // 4, 0, 0)),
        scratch_shapes=[pltpu.VMEM((1152, 512), bf16)] * 2,
        compiler_params=pltpu.CompilerParams(vmem_limit_bytes=24 * MIB),
        cost_estimate=SMALL,
        name="weights_grad",
    )(*normed, *grad, *hidden, *earlier)


def down_kernel(
    place_ref,
    near_act_ref,
    far_act_ref,
    near_ref,
    far_ref,
    hidden_ref,
    out_ref,
    mark_ref,
    total_ref,
):
    chip = place_ref[0]
    total = right_dot(near_act_ref[...], near_ref[...])
    total_ref[...] = total + right_dot(far_act_ref[...], far_ref[...])

    @pl.when(pl.program_id(0) == chip // 4)
    def _():
        rows = pl.ds(pl.multiple_of((chip % 4) * 64, 64), 64)
        total_ref[rows, :] += turned_columns(hidden_ref[...])

    for index in range(8):
        cols = total_ref[:, index * 256 : index * 256 + 256]
        out_ref[turned_place(index)] = cols.astype(bf16)
    mark_ref[...] = total_ref[:, :256].astype(bf16)


def down(chip, near_act, far_act, near, far, hidden, earlier):
    weight = pl.BlockSpec((D, 384), lambda i: (0, 2))
    return pl.pallas_call(
        ordered(down_kernel, 6, earlier),
        grid=(2,),
        out_shape=(
            pltpu.HBM((8, 512, 256), bf16),
            jax.ShapeDtypeStruct((512, 256), bf16),
        ),
        in_specs=[
            pl.BlockSpec(memory_space=pltpu.SMEM),
            pl.BlockSpec((256, 384), lambda i: (i, 2)),
            pl.BlockSpec((256, 384), lambda i: (i, 2)),
            weight,
            weight,
            pl.BlockSpec((64, D), lambda i: (0, 0)),
            *unread(earlier),
        ],
        out_specs=(
            pl.BlockSpec((8, 256, 256), lambda i: (0, i, 0)),
            pl.BlockSpec((256, 256), lambda i: (i, 0)),
        ),
        scratch_shapes=[pltpu.VMEM((256, D), f32)],
        compiler_params=pltpu.CompilerParams(vmem_limit_bytes=24 * MIB),
        cost_estimate=SMALL,
        name="down",
    )(chip, near_act, far_act, near, far, hidden, *earlier)


def input_part_kernel(
    place_ref,
    near_ref,
    far_ref,
    near_weight_ref,
    far_weight_ref,
    rows_ref,
    gain_ref,
    hidden_ref,
    mlp_ref,
    head_ref,
    out_ref,
    mark_ref,
    total_ref,
    term_ref,
    sum_ref,
):
    step = pl.program_id(0)
    part = right_dot(near_ref[...], near_weight_ref[...])
    part = part + right_dot(far_ref[...], far_weight_ref[...])
    rows = rows_ref[...].astype(f32)
    inverse = inverse_rms(rows)
    gain = gain_ref[...]
    weighted = part * (rows * inverse)
    term = jnp.sum(weighted * gain, axis=1, keepdims=True) * (1.0 / D)
    term_ref[pl.ds(step, 1), :] = jnp.broadcast_to(term, (256, 128)).T[:1, :]
    sums = jnp.sum(weighted.reshape(32, 8, D), axis=0)

    @pl.when(step == 0)
    def _():
        sum_ref[...] = sums

    @pl.when(step > 0)
    def _():
        sum_ref[...] += sums

    total_ref[...] = part * (gain * inverse)
    hidden = hidden_ref[...]
    for span in range(2):
        own = pl.ds(pl.multiple_of(span * 128 + place_ref[0] * 16, 16), 16)
        total_ref[own, :] += hidden[span * 16 : span * 16 + 16, :]
    at = pl.ds(pl.multiple_of(step * 256, 256), 256)
    for index in range(8):
        cols = total_ref[:, index * 256 : index * 256 + 256]
        out_ref[index, at, :] = cols.astype(bf16)
    mark_ref[...] = total_ref[:, :256].astype(bf16)

    @pl.when(step == 1)
    def _():
        terms = term_ref[:2, :]
        coarse = terms.astype(bf16).astype(f32)
        totals = jnp.sum(sum_ref[...], axis=0, keepdims=True)
        extra = jnp.concatenate(
            [coarse, terms - coarse]
            + [totals[:, index * 256 : index * 256 + 256] for index in range(8)]
            + [mlp_ref[:, index * 256 : index * 256 + 256] for index in range(8)]
            + [head_ref[...], jnp.zeros((11, 256), f32)],
            axis=0,
        ).astype(bf16)
        for index in range(8):
            out_ref[index, 512:, :] = extra


def input_part(
    place, near, far, near_weight, far_weight, rows, gain, hidden, mlp, head, earlier
):
    def fixed(*shape):
        return pl.BlockSpec(shape, lambda i, place_ref: (0,) * len(shape))

    def tile(*shape):
        return pl.BlockSpec(shape, lambda i, place_ref: (i, 0))

    def own(*shape):
        return pl.BlockSpec(shape, lambda i, place_ref: (place_ref[1] * 2 + i, 0))

    return pl.pallas_call(
        ordered(input_part_kernel, 10, earlier),
        out_shape=(
            pltpu.HBM((8, 544, 256), bf16),
            jax.ShapeDtypeStruct((512, 256), bf16),
        ),
        grid_spec=pltpu.PrefetchScalarGridSpec(
            num_scalar_prefetch=1,
            grid=(2,),
            in_specs=[
                tile(256, 256),
                tile(256, 256),
                fixed(D, 256),
                fixed(D, 256),
                own(256, D),
                fixed(1, D),
                tile(32, D),
                fixed(1, D),
                fixed(1, 256),
                *unread(earlier),
            ],
            out_specs=(fixed(8, 544, 256), tile(256, 256)),
            scratch_shapes=[
                pltpu.VMEM((256, D), f32),
                pltpu.VMEM((8, 256), f32),
                pltpu.VMEM((8, D), f32),
            ],
        ),
        compiler_params=pltpu.CompilerParams(vmem_limit_bytes=28 * MIB),
        cost_estimate=SMALL,
        name="input_part",
    )(place, near, far, near_weight, far_weight, rows, gain, hidden, mlp, head, *earlier)


def attention_grads_kernel(normed_ref, grad_ref, grad_out_ref, out_ref, turned_ref):
    @pl.when(pl.program_id(0) == 0)
    def _():
        turned_ref[...] = grad_ref[...].T

    out_ref[0, :256, :] = plain_dot(turned_ref[...], normed_ref[...]).astype(bf16)
    out_ref[0, 256:, :] = grad_out_ref[...]


def attention_grads(normed, grad_proj, grad_out, earlier):
    return pl.pallas_call(
        ordered(attention_grads_kernel, 3, earlier),
        grid=(8,),
        out_shape=jax.ShapeDtypeStruct((8, 384, 256), bf16),
        in_specs=[
            pl.BlockSpec((ROWS, 256), lambda i: (0, i)),
            pl.BlockSpec((ROWS, 256), lambda i: (0, 0)),
            pl.BlockSpec((HD, 256), lambda i: (0, i)),
            *unread(earlier),
        ],
        out_specs=pl.BlockSpec((1, 384, 256), lambda i: (i % 4 * 2 + i // 4, 0, 0)),
        scratch_shapes=[pltpu.VMEM((256, ROWS), bf16)],
        compiler_params=pltpu.CompilerParams(vmem_limit_bytes=12 * MIB),
        cost_estimate=SMALL,
        name="attention_grads",
    )(normed, grad_proj, grad_out, *earlier)


def body(
    inputs,
    out_grad,
    lengths,
    span_order,
    w_query,
    w_key,
    w_value,
    w_out,
    w_gate,
    w_up,
    w_down,
    norm_attn,
    norm_mlp,
    norm_query,
    norm_key,
):
    xl, z, xh, y, core = (lax.axis_index(name) for name in ("xl", "z", "xh", "y", "c"))
    span_place = xl * 4 + z
    chip = xh * 4 + y
    first = core == 0

    def by_core(near, far, axis=0):
        join = jnp.stack if axis is None else lambda parts: jnp.concatenate(parts, axis=axis)
        return jnp.where(first, join([near, far]), join([far, near]))

    def split(block):
        near = lax.dynamic_slice_in_dim(block, core * 512, 512, 0)
        far = lax.dynamic_slice_in_dim(block, (1 - core) * 512, 512, 0)
        return near, far

    def chip_major(block):
        return block.reshape(4, 8, 16, -1).transpose(1, 0, 2, 3).reshape(512, -1)

    def span_major(block):
        return block.reshape(8, 4, 16, -1).transpose(1, 0, 2, 3).reshape(512, -1)

    gains = jnp.concatenate([norm_attn, norm_mlp, norm_query, norm_key])
    gains = jnp.pad(gains, (0, 16 * 256 - 544)).reshape(16, 256)
    shard = jnp.concatenate(
        [jnp.concatenate([w_query, w_key, w_value], axis=1), gains], axis=0
    )
    spread_weights = spread(shard, SPANS, 8)
    qkv_weights = spread_weights[:, :256].reshape(D, 256)
    gains = spread_weights[:, 256:259].reshape(8, 768).astype(f32)
    gain_attn = gains[:, :256].reshape(1, D)
    gain_mlp = gains[:, 256:512].reshape(1, D)
    gain_query = gains[:, 512:528].reshape(1, HD)
    gain_key = gains[:, 528:544].reshape(1, HD)
    key_half, value_half = qkv_weights[:, 128:192], qkv_weights[:, 192:256]
    other_half = swap(jnp.where(first, value_half, key_half))
    near_weight = jnp.where(
        first,
        jnp.concatenate([qkv_weights[:, :192], other_half], 1),
        jnp.concatenate([qkv_weights[:, :128], other_half, value_half], 1),
    )

    route, starts, low = routes(jnp.stack([span_place, xl, z]), lengths, span_order)

    def reorder(index, rows):
        return plain_dot(route[index], rows).astype(bf16)

    moving = lax.dynamic_index_in_dim(
        out_grad.reshape(8, 16, 8, D), chip * 2 + core, 1, keepdims=False
    ).reshape(64, D)
    moving = reorder(0, moving).reshape(8, 8, D)
    spread_out = jnp.broadcast_to(w_out.reshape(1, 16, D), (8, 16, D))
    moving = jnp.concatenate([moving, spread_out], axis=1)
    arrived = exchange(after(moving, qkv_weights), SPANS)
    out_weights = arrived[:, 8:].reshape(8, HD, 256)
    moving = arrived[:, :8].reshape(64, D)

    ends = jnp.cumsum(lax.dynamic_index_in_dim(lengths, xl, 0, keepdims=False))
    offset = z * ROWS + jnp.arange(ROWS, dtype=jnp.int32)
    doc_start = jnp.where(offset >= ends[1], ends[1], jnp.where(offset >= ends[0], ends[0], 0))
    frequency = jnp.power(rope_base, -2.0 * jnp.arange(HD // 2, dtype=f32) / HD)
    angles = (offset - doc_start).astype(f32)[:, None] * frequency[None, :]
    cos_table, sin_table = jnp.cos(angles), jnp.sin(angles)
    cos_table = jnp.concatenate([cos_table, cos_table], axis=1)
    sin_table = jnp.concatenate([-sin_table, sin_table], axis=1)

    normed, inverse_one, query_bf, own_kv, query_proj, kv_proj = project(
        core.reshape(1),
        in_hbm(inputs),
        gain_attn,
        near_weight,
        cos_table,
        sin_table,
        gain_query,
        gain_key,
    )
    ready_kv = after(own_kv, arrived)
    moving = after(reorder(1, moving), own_kv)
    moving = exchange(moving.reshape(8, 8, D), SPANS).reshape(64, D)
    moving = reorder(2, moving).reshape(8, 8, D)
    near = lax.dynamic_slice_in_dim(moving, core * 4, 4, 0)
    far = lax.dynamic_slice_in_dim(moving, (1 - core) * 4, 4, 0)
    own_grad = by_core(near, swap(far), 1).reshape(64, D)
    spread_grad = jnp.broadcast_to(own_grad[None], (8, 64, D))
    grad_mine = exchange(spread_grad, CHIPS)

    mine = jnp.concatenate(
        [onward(ready_kv, 3), onward(ready_kv, 2), onward(ready_kv, 1), own_kv], axis=0
    )
    mine = after(mine, spread_grad)
    other = swap(mine)
    all_keys = jnp.where(first, mine, other)
    all_values = jnp.where(first, other, mine)

    out_weights = out_weights.transpose(1, 0, 2).reshape(HD, D)
    out_two = jnp.concatenate([out_weights, swap(out_weights)], axis=0)

    mlp_shard = after(jnp.concatenate([w_gate, w_up, w_down.T], axis=1), qkv_weights)
    far_shard = after(far_span(mlp_shard), mine)
    mlp_shard = jnp.where(
        xl == 0,
        jnp.concatenate([mlp_shard, far_shard]),
        jnp.concatenate([far_shard, mlp_shard]),
    )
    near_weights = lax.all_gather(mlp_shard, "z", axis=0, tiled=True)

    own_rows = lax.dynamic_slice_in_dim(inputs, core * 512, 512, 0).reshape(4, 8, 16, D)
    own_rows = lax.dynamic_index_in_dim(own_rows, chip, 1, keepdims=False).reshape(64, D)

    attended, attended_full, total = attend(
        low,
        starts,
        in_hbm(query_bf),
        in_hbm(all_keys),
        in_hbm(all_values),
        [fence(spread_grad), out_two, mlp_shard, own_rows],
    )

    att_near, att_far = split(attended)
    att_two = jnp.concatenate(
        [chip_major(att_near), swap(after(chip_major(att_far), grad_mine))], axis=1
    )
    branch = plain_dot(att_two, out_two).astype(bf16)
    branch = branch.reshape(8, 64, D)
    branch = exchange(branch, CHIPS)
    far_weights = swap(after(near_weights, branch))
    hidden, spread_normed = norm(branch, own_rows, gain_mlp)
    normed_mine = exchange(spread_normed, CHIPS)

    near_out, far_out, part = feed(normed_mine, grad_mine, near_weights, far_weights)
    mlp_grads = weights_grad(
        (normed_mine, swap(normed_mine)),
        (grad_mine, swap(grad_mine)),
        (near_out, swap(far_out)),
        [fence(part)],
    )
    part = exchange(part.reshape(8, 64, D), CHIPS)
    part, mlp_grads = lax.optimization_barrier((part, mlp_grads))
    def by_span(block):
        sent = lax.dynamic_index_in_dim(block, 1 - xl, 0, keepdims=False)
        return lax.dynamic_index_in_dim(block, xl, 0, keepdims=False), far_span(sent)

    mlp_grads = lax.psum_scatter(mlp_grads, "z", scatter_dimension=0, tiled=True)

    grad_hidden, gain_mlp_part, spread_branch = norm_grad(part, hidden, gain_mlp, own_grad)
    out_cols, out_mark = down(
        chip.reshape(1),
        near_out,
        far_out,
        near_weights,
        far_weights,
        hidden,
        [fence(spread_branch)],
    )
    far_weight = swap(near_weight)
    branch_mine = exchange(spread_branch, CHIPS).reshape(512, D)
    branch_mine = after(branch_mine, out_cols, far_weight)
    out_cols, out_mark = after(out_cols, branch_mine), after(out_mark, branch_mine)
    out_fence = swap(out_mark)
    out_cols = exchange(out_cols, CHIPS)
    grad_two = right_dot(branch_mine, out_two).astype(bf16)
    grad_att = by_core(span_major(grad_two[:, :HD]), span_major(swap(grad_two[:, HD:])))

    grad_query_rot, keep, send = attend_back(
        low,
        core.reshape(1),
        starts,
        in_hbm(query_bf),
        in_hbm(all_keys),
        in_hbm(all_values),
        grad_att,
        in_hbm(attended_full),
        total,
        [out_fence],
    )
    came = swap(send)
    own_kv_grad, *away = merge(keep, came)
    received = [backward(block, by + 1) for by, block in enumerate(away)]

    def unorder(index, rows):
        return left_dot(route[index], rows).astype(bf16)

    grad_out = left_dot(att_two, after(branch_mine, received[2]))
    grad_out = (grad_out[:HD] + swap(grad_out[HD:].astype(bf16)).astype(f32)).astype(bf16)
    grad_proj, head_gains = project_back(
        core.reshape(1),
        in_hbm(grad_query_rot),
        own_kv_grad,
        [in_hbm(block) for block in received],
        in_hbm(cos_table),
        in_hbm(sin_table),
        (in_hbm(query_proj), in_hbm(kv_proj)),
        (gain_query, gain_key),
        [in_hbm(mlp_grads), out_cols],
    )

    grad_near, grad_far = split(grad_proj)
    by_cols, mark = input_part(
        jnp.stack([chip, core]),
        grad_near,
        swap(grad_far),
        in_hbm(near_weight),
        in_hbm(far_weight),
        in_hbm(inputs),
        gain_attn,
        in_hbm(grad_hidden),
        gain_mlp_part,
        head_gains,
        [],
    )
    mlp_kept, mlp_came = by_span(after(mlp_grads, grad_proj))
    grad_attn = attention_grads(normed, grad_proj, grad_out, [swap(mark), mlp_came])
    out_cols = after(out_cols, grad_attn)
    grad_attn = grad_attn.reshape(4, 2, 384, 256)
    parts = [
        lax.dynamic_index_in_dim(grad_attn, (z + by) % 4, 0, keepdims=False) for by in range(4)
    ]
    parts = [parts[0]] + [
        lax.ppermute(parts[by], "z", [(i, (i + by) % 4) for i in range(4)]) for by in (1, 2, 3)
    ]
    out_cols = jnp.sum(out_cols.astype(f32), axis=0).astype(bf16)
    near = jnp.where(first, out_cols[:, :128], out_cols[:, 128:])
    far = jnp.where(first, out_cols[:, 128:], out_cols[:, :128])
    out_cols = by_core(near, swap(far), None).reshape(2, 8, 4, 2, 8, 128)
    out_rows = jnp.concatenate(
        [out_cols[:, index // 2, :, index % 2].reshape(64, 128) for index in range(16)], axis=1
    )

    by_cols = exchange(by_cols, CHIPS)

    class_rows = exchange(after(unorder(2, out_rows).reshape(8, 8, D), by_cols), SPANS)
    out_rows = class_rows
    parts = lax.optimization_barrier((*parts, by_cols))[:4]
    grad_attn = sum(part.astype(f32) for part in parts)
    attn_kept, attn_came = by_span(grad_attn.astype(bf16))
    by_cols = jnp.sum(by_cols.astype(f32), axis=0)
    row_term = (by_cols[512:514] + by_cols[514:516]).reshape(512, 1)
    own_inverse = lax.dynamic_slice_in_dim(inverse_one, core * 512, 512, 0)
    own_cols = lax.dynamic_slice(inputs, (core * 512, chip * 256), (512, 256)).astype(f32)
    in_grad = by_cols[:512] - own_cols * (own_inverse * own_inverse * row_term)
    near = jnp.where(first, in_grad[:, :128], in_grad[:, 128:])
    far = jnp.where(first, in_grad[:, 128:], in_grad[:, :128])
    in_grad = by_core(near, swap(far))
    gain_sums = jnp.concatenate(
        [
            by_cols[516:524],
            by_cols[524:532],
            by_cols[532, :128].reshape(8, 16),
            by_cols[532, 128:].reshape(8, 16),
        ],
        axis=1,
    )
    gain_sums = gain_sums + swap(gain_sums)
    coarse = gain_sums.astype(bf16)
    extra = jnp.concatenate(
        [coarse, (gain_sums - coarse.astype(f32)).astype(bf16), jnp.zeros((8, 960), bf16)], axis=1
    )
    extra = jnp.pad(extra[:, None], ((0, 0), (0, 7), (0, 0)))
    out_rows = unorder(1, out_rows.reshape(64, D)).reshape(8, 8, D)
    out_rows = after(jnp.concatenate([out_rows, extra], axis=1), attn_came)
    out_rows = exchange(out_rows, SPANS)
    gain_sums = jnp.sum(out_rows[:, 8].astype(f32), axis=0)
    gain_sums = gain_sums[:544] + gain_sums[544:1088]
    layer_out = unorder(0, out_rows[:, :8].reshape(64, D))
    layer_out = jnp.stack(
        [layer_out[:, at * 128 : at * 128 + 128].reshape(8, 8, 128) for at in range(16)],
        axis=1,
    )
    layer_out = layer_out.reshape(ROWS, 128).astype(f32)

    grad_attn = attn_kept.astype(f32) + attn_came.astype(f32)
    grad_kv_weight = grad_attn[128:256]
    low_half, high_half = grad_kv_weight[:64], grad_kv_weight[64:]
    came = swap(jnp.where(first, high_half, low_half))
    kept = jnp.where(first, low_half, high_half)
    mlp_kept, mlp_came = after(mlp_kept, class_rows), after(mlp_came, class_rows)
    mlp_grads = mlp_kept.astype(f32) + mlp_came.astype(f32)

    return (
        layer_out,
        in_grad,
        grad_attn[:128].T,
        jnp.where(first, kept, came).T,
        jnp.where(first, came, kept).T,
        grad_attn[256:],
        mlp_grads[:384].T,
        mlp_grads[384:768].T,
        mlp_grads[768:],
        gain_sums[:256],
        gain_sums[256:512],
        gain_sums[512:528],
        gain_sums[528:544],
    )


def solution(mesh):
    fine = Mesh(mesh.devices.reshape(2, 4, 2, 4, 2), ("xl", "z", "xh", "y", "c"))
    rows = P(SPANS, None)
    by_both = P(SPANS, TENSOR)
    turned = P(TENSOR, SPANS)
    lone = P(SPANS)
    return jax.shard_map(
        body,
        mesh=fine,
        in_specs=(
            rows,
            rows,
            P(),
            P(),
            by_both,
            by_both,
            by_both,
            turned,
            by_both,
            by_both,
            turned,
            lone,
            lone,
            lone,
            lone,
        ),
        out_specs=(
            by_both,
            by_both,
            by_both,
            by_both,
            by_both,
            turned,
            by_both,
            by_both,
            turned,
            lone,
            lone,
            lone,
            lone,
        ),
        check_vma=False,
    )
```

```python
import jax
import jax.numpy as jnp
from jax import lax
from jax.experimental import pallas as pl
from jax.experimental.pallas import tpu as pltpu
from jax.sharding import Mesh, PartitionSpec as P

SPAN = 128
MICRO = 2
HD = 128
D = 2048
ROWS = 1024
KEYS = 4096
KEY_BLK = 512

epsilon = 1e-06
rope_base = 1000000.0
score_scale = HD ** (-0.5)
log2e = 1.4426950408889634
bf16 = jnp.bfloat16
f32 = jnp.float32
SPANS = ("xl", "z")
TENSOR = ("xh", "y", "c")
CHIPS = ("xh", "y")
MIB = 1024 * 1024
SMALL = pl.CostEstimate(flops=1024, bytes_accessed=1024, transcendentals=0)


def swap(block):
    return lax.ppermute(block, "c", [(0, 1), (1, 0)])


def far_span(block):
    return lax.ppermute(block, "xl", [(0, 1), (1, 0)])


def onward(block, by):
    return lax.ppermute(block, "z", [(i, i + by) for i in range(4) if i + by < 4])


def backward(block, by):
    return lax.ppermute(block, "z", [(i, i - by) for i in range(4) if i - by >= 0])


def exchange(block, axes):
    return lax.all_to_all(block, axes, 0, 0, tiled=True)


def spread(block, axes, count):
    return exchange(jnp.broadcast_to(block[None], (count,) + block.shape), axes)


def after(block, *earlier):
    return lax.optimization_barrier((block,) + earlier)[0]


def fence(block):
    return swap(block.reshape(-1, block.shape[-1])[:512, :256])


def ordered(kernel, inputs, earlier):
    return lambda *refs: kernel(*refs[:inputs], *refs[inputs + len(earlier) :])


def in_hbm(block):
    return pltpu.with_memory_space_constraint(block, pltpu.HBM)


def unread(earlier):
    return [pl.BlockSpec(memory_space=pl.ANY)] * len(earlier)


def plain_dot(first_op, second_op):
    return jnp.dot(first_op, second_op, preferred_element_type=f32)


def left_dot(first_op, second_op):
    return lax.dot_general(
        first_op, second_op, (((0,), (0,)), ((), ())), preferred_element_type=f32
    )


def right_dot(first_op, second_op):
    return lax.dot_general(
        first_op, second_op, (((1,), (1,)), ((), ())), preferred_element_type=f32
    )


def inverse_rms(values):
    return lax.rsqrt(jnp.mean(values * values, axis=-1, keepdims=True) + epsilon)


def norm_back(incoming, normal, inverse):
    return inverse * (incoming - normal * jnp.mean(incoming * normal, axis=-1, keepdims=True))


def block_mask(key_block, starts):
    key_at = key_block * KEY_BLK + lax.broadcasted_iota(jnp.int32, (KEY_BLK, ROWS), 0)
    query_at = (KEYS - ROWS) + lax.broadcasted_iota(jnp.int32, (KEY_BLK, ROWS), 1)
    return (key_at >= starts) & (key_at <= query_at)


def over_keys(range_ref, step, state):
    own = (KEYS - ROWS) // KEY_BLK
    seen = jnp.minimum(range_ref[1], own)
    state = lax.fori_loop(range_ref[0], seen, lambda at, state: step(at, state, True), state)
    state = lax.fori_loop(seen, own, lambda at, state: step(at, state, False), state)
    for at in range(own, KEYS // KEY_BLK):
        state = step(at, state, True)
    return state


def attend_kernel(range_ref, start_ref, q_ref, k_ref, v_ref, out_ref, full_ref, total_ref):
    queries = q_ref[...]
    starts = start_ref[...]

    def step(at, state, masked):
        acc, total = state
        rows = pl.ds(pl.multiple_of(at * KEY_BLK, KEY_BLK), KEY_BLK)
        weights = jnp.exp2(right_dot(k_ref[rows, :], queries) * (score_scale * log2e))
        if masked:
            weights = jnp.where(block_mask(at, starts), weights, 0.0)
        total = total + jnp.sum(weights, axis=0, keepdims=True)
        acc = acc + left_dot(v_ref[rows, :], weights.astype(bf16))
        return acc, total

    acc, total = over_keys(
        range_ref, step, (jnp.zeros((HD, ROWS), f32), jnp.zeros((1, ROWS), f32))
    )
    full = acc / total
    full_ref[...] = full
    total_ref[...] = jnp.log2(total)
    out_ref[...] = full.T.astype(bf16)


def attend(low, starts, queries, keys, values, earlier):
    vmem = pl.BlockSpec(memory_space=pltpu.VMEM)
    return pl.pallas_call(
        ordered(attend_kernel, 5, earlier),
        out_shape=(
            jax.ShapeDtypeStruct((ROWS, HD), bf16),
            pltpu.HBM((HD, ROWS), f32),
            jax.ShapeDtypeStruct((1, ROWS), f32),
        ),
        in_specs=[pl.BlockSpec(memory_space=pltpu.SMEM)] + [vmem] * 4 + unread(earlier),
        out_specs=(vmem,) * 3,
        compiler_params=pltpu.CompilerParams(vmem_limit_bytes=24 * MIB),
        cost_estimate=SMALL,
        name="attend",
    )(low, starts, queries, keys, values, *earlier)


def attend_back_kernel(
    range_ref,
    core_ref,
    start_ref,
    q_ref,
    k_ref,
    v_ref,
    do_ref,
    full_ref,
    total_ref,
    dq_ref,
    keep_ref,
    send_ref,
    dk_ref,
    dv_ref,
):
    dk_ref[...] = jnp.zeros_like(dk_ref)
    dv_ref[...] = jnp.zeros_like(dv_ref)
    queries = q_ref[...]
    starts = start_ref[...]
    incoming = do_ref[...]
    total = total_ref[...]
    delta = jnp.sum(incoming.astype(f32).T * full_ref[...], axis=0, keepdims=True)

    def step(at, acc, masked):
        rows = pl.ds(pl.multiple_of(at * KEY_BLK, KEY_BLK), KEY_BLK)
        keys = k_ref[rows, :]
        weights = jnp.exp2(right_dot(keys, queries) * (score_scale * log2e) - total)
        if masked:
            weights = jnp.where(block_mask(at, starts), weights, 0.0)
        grads = right_dot(v_ref[rows, :], incoming)
        grads = (weights * (grads - delta)).astype(bf16)
        dv_ref[rows, :] += plain_dot(weights.astype(bf16), incoming)
        dk_ref[rows, :] += plain_dot(grads, queries)
        return acc + left_dot(keys, grads)

    dq_ref[...] = over_keys(range_ref, step, jnp.zeros((HD, ROWS), f32)).T * score_scale

    @pl.when(core_ref[0] == 0)
    def _():
        keep_ref[...] = dk_ref[...] * score_scale
        send_ref[...] = dv_ref[...].astype(bf16)

    @pl.when(core_ref[0] == 1)
    def _():
        keep_ref[...] = dv_ref[...]
        send_ref[...] = (dk_ref[...] * score_scale).astype(bf16)


def attend_back(low, core, starts, queries, keys, values, incoming, full, total, earlier):
    vmem = pl.BlockSpec(memory_space=pltpu.VMEM)
    smem = pl.BlockSpec(memory_space=pltpu.SMEM)
    return pl.pallas_call(
        ordered(attend_back_kernel, 9, earlier),
        out_shape=(
            pltpu.HBM((ROWS, HD), f32),
            jax.ShapeDtypeStruct((KEYS, HD), f32),
            jax.ShapeDtypeStruct((KEYS, HD), bf16),
        ),
        in_specs=[smem, smem] + [vmem] * 7 + unread(earlier),
        out_specs=(vmem,) * 3,
        scratch_shapes=[pltpu.VMEM((KEYS, HD), f32), pltpu.VMEM((KEYS, HD), f32)],
        compiler_params=pltpu.CompilerParams(vmem_limit_bytes=32 * MIB),
        cost_estimate=SMALL,
        name="attend_back",
    )(low, core, starts, queries, keys, values, incoming, full, total, *earlier)


def colour_kernel(place_ref, lengths_ref, column_ref, row_ref, out_ref, start_ref, range_ref):
    micro, block = place_ref[1], place_ref[2]
    first_end = lengths_ref[micro, 0]
    second_end = first_end + lengths_ref[micro, 1]

    def begin(offset):
        begun = jnp.where(offset >= first_end, first_end, 0)
        begun = jnp.where(offset >= second_end, second_end, begun)
        return begun - (block - 3) * ROWS

    start_ref[...] = begin(block * ROWS + lax.broadcasted_iota(jnp.int32, (1, ROWS), 1))
    range_ref[0] = begin(block * ROWS) >> 9
    range_ref[1] = (begin(block * ROWS + ROWS - 1) + KEY_BLK - 1) >> 9
    down_at = lax.broadcasted_iota(jnp.int32, (64, 64), 0)
    across_at = lax.broadcasted_iota(jnp.int32, (64, 64), 1)
    same_slots = (down_at >> 3) == (across_at >> 3)
    same_spans = (column_ref[...] >> 3) == (row_ref[...] >> 3)
    colour = jnp.zeros((64, 1), jnp.int32)
    for _ in range(3):
        colour_row = jnp.sum(
            jnp.where(down_at == across_at, colour, 0).astype(f32), axis=0, keepdims=True
        ).astype(jnp.int32)
        alike = colour == colour_row

        def partner(group):
            near = group & alike
            rank_down = jnp.sum(
                jnp.where(near & (across_at < down_at), 1.0, 0.0), axis=1, keepdims=True
            ).astype(jnp.int32)
            rank_across = jnp.sum(
                jnp.where(near & (down_at < across_at), 1.0, 0.0), axis=0, keepdims=True
            ).astype(jnp.int32)
            return jnp.where(near & ((rank_down ^ 1) == rank_across), 1.0, 0.0)

        by_slot = partner(same_slots)
        jump = plain_dot(by_slot, partner(same_spans))
        label = lax.broadcasted_iota(jnp.int32, (64, 128), 0).astype(f32)
        for turn in range(5):
            label = jnp.minimum(label, plain_dot(jump, label))
            if turn < 4:
                jump = plain_dot(jump, jump)
        bit = jnp.where(label > plain_dot(by_slot, label), 1, 0)
        colour = colour * 2 + bit[:, :1]
    colour_row = jnp.sum(
        jnp.where(down_at == across_at, colour, 0).astype(f32), axis=0, keepdims=True
    )
    own = place_ref[0]
    same_row = (down_at & 7) == (across_at & 7)
    slot_colour = jnp.sum(
        jnp.where(down_at == own * 8 + (across_at >> 3), colour, 0).astype(f32),
        axis=0,
        keepdims=True,
    ).astype(jnp.int32)
    owner = jnp.sum(
        jnp.where(same_slots & (colour == own), column_ref[...] >> 3, 0).astype(f32),
        axis=0,
        keepdims=True,
    ).astype(jnp.int32)
    span_colour = jnp.sum(
        jnp.where(row_ref[...] == own * 8 + (down_at >> 3), colour_row, 0.0),
        axis=1,
        keepdims=True,
    ).astype(jnp.int32)
    for index, match in enumerate(
        (
            slot_colour == (down_at >> 3),
            owner == (down_at >> 3),
            span_colour == (across_at >> 3),
        )
    ):
        out_ref[index] = jnp.where(match & same_row, 1.0, 0.0).astype(bf16)


def routes(place, lengths, span_order):
    vmem = pl.BlockSpec(memory_space=pltpu.VMEM)
    smem = pl.BlockSpec(memory_space=pltpu.SMEM)
    return pl.pallas_call(
        colour_kernel,
        out_shape=(
            jax.ShapeDtypeStruct((3, 64, 64), bf16),
            jax.ShapeDtypeStruct((1, ROWS), jnp.int32),
            jax.ShapeDtypeStruct((2,), jnp.int32),
        ),
        in_specs=[smem, smem, vmem, vmem],
        out_specs=(vmem, vmem, smem),
        name="routes",
    )(place, lengths, span_order.reshape(64, 1), span_order.reshape(1, 64))


def project_kernel(
    place_ref,
    rows_ref,
    gain_ref,
    weight_ref,
    cos_ref,
    sin_ref,
    gain_query_ref,
    gain_key_ref,
    normed_ref,
    inverse_ref,
    query_out_ref,
    kv_out_ref,
    query_proj_ref,
    kv_proj_ref,
):
    rows = rows_ref[...].astype(f32)
    inverse = inverse_rms(rows)
    normed = (rows * inverse * gain_ref[...]).astype(bf16)
    inverse_ref[...] = inverse
    normed_ref[...] = normed
    cos, sin = cos_ref[...], sin_ref[...]

    def turned(values):
        return values * cos + pltpu.roll(values, 64, 1) * sin

    proj = plain_dot(normed, weight_ref[...])
    query, kv = proj[:, :HD], proj[:, HD:]
    kv_proj_ref[...] = kv
    key = turned(kv * inverse_rms(kv) * gain_key_ref[...])
    kv_out_ref[...] = jnp.where(place_ref[0] == 0, key, kv).astype(bf16)
    query_proj_ref[...] = query
    query = turned(query * inverse_rms(query) * gain_query_ref[...])
    query_out_ref[...] = query.astype(bf16)


def project(core, rows, gain, weights, cos, sin, gain_query, gain_key):
    wide = pl.BlockSpec((256, D), lambda i: (i, 0))
    head = pl.BlockSpec((256, HD), lambda i: (i, 0))
    one = pl.BlockSpec((256, 1), lambda i: (i, 0))
    weight = pl.BlockSpec((D, 256), lambda i: (0, 0))
    small = pl.BlockSpec((1, HD), lambda i: (0, 0))
    column = pltpu.HBM((ROWS, 1), f32)
    return pl.pallas_call(
        project_kernel,
        grid=(4,),
        out_shape=(
            pltpu.HBM((ROWS, D), bf16),
            column,
            jax.ShapeDtypeStruct((ROWS, HD), bf16),
            jax.ShapeDtypeStruct((ROWS, HD), bf16),
            pltpu.HBM((ROWS, HD), f32),
            pltpu.HBM((ROWS, HD), f32),
        ),
        in_specs=[
            pl.BlockSpec(memory_space=pltpu.SMEM),
            wide,
            pl.BlockSpec((1, D), lambda i: (0, 0)),
            weight,
            head,
            head,
            small,
            small,
        ],
        out_specs=(wide, one, head, head, head, head),
        compiler_params=pltpu.CompilerParams(vmem_limit_bytes=20 * MIB),
        cost_estimate=SMALL,
        name="project",
    )(core, rows, gain, weights, cos, sin, gain_query, gain_key)


def project_back_kernel(
    place_ref,
    query_grad_ref,
    own_ref,
    one_ref,
    two_ref,
    three_ref,
    cos_ref,
    sin_ref,
    query_proj_ref,
    kv_proj_ref,
    gain_query_ref,
    gain_key_ref,
    out_ref,
    sum_ref,
):
    cos, sin = cos_ref[...], sin_ref[...]

    def turned_back(values):
        return values * cos - pltpu.roll(values, 64, 1) * sin

    step = pl.program_id(0)
    grad = turned_back(query_grad_ref[...])
    query = query_proj_ref[...]
    inverse = inverse_rms(query)
    hat = query * inverse
    sums = jnp.sum(grad * hat, axis=0, keepdims=True)
    query = norm_back(grad * gain_query_ref[...], hat, inverse)
    out_ref[:, :HD] = query.astype(bf16)
    kv = own_ref[...] + one_ref[...].astype(f32)
    kv = kv + two_ref[...].astype(f32) + three_ref[...].astype(f32)
    grad = turned_back(kv)
    key = kv_proj_ref[...]
    inverse = inverse_rms(key)
    hat = key * inverse
    is_key = place_ref[0] == 0
    key_sums = jnp.where(is_key, jnp.sum(grad * hat, axis=0, keepdims=True), 0.0)
    key = norm_back(grad * gain_key_ref[...], hat, inverse)
    out_ref[:, HD:] = jnp.where(is_key, key, kv).astype(bf16)
    sums = jnp.concatenate([sums, key_sums], axis=1)

    @pl.when(step == 0)
    def _():
        sum_ref[...] = sums

    @pl.when(step > 0)
    def _():
        sum_ref[...] += sums


def project_back(core, query_grad, own, arrived, cos, sin, projections, gains, earlier):
    head = pl.BlockSpec((256, HD), lambda i: (i, 0))
    small = pl.BlockSpec((1, HD), lambda i: (0, 0))
    return pl.pallas_call(
        ordered(project_back_kernel, 12, earlier),
        grid=(4,),
        out_shape=(
            jax.ShapeDtypeStruct((ROWS, 256), bf16),
            jax.ShapeDtypeStruct((1, 256), f32),
        ),
        in_specs=[pl.BlockSpec(memory_space=pltpu.SMEM)]
        + [head] * 9
        + [small] * 2
        + unread(earlier),
        out_specs=(
            pl.BlockSpec((256, 256), lambda i: (i, 0)),
            pl.BlockSpec((1, 256), lambda i: (0, 0)),
        ),
        compiler_params=pltpu.CompilerParams(vmem_limit_bytes=12 * MIB),
        cost_estimate=SMALL,
        name="project_back",
    )(core, query_grad, own, *arrived, cos, sin, *projections, *gains, *earlier)


def pack_kernel(query_ref, key_ref, value_ref, gains_ref, out_ref):
    half = jnp.concatenate([key_ref[...], value_ref[...]], axis=0).T
    query = query_ref[...]
    gains = gains_ref[...]
    for index in range(8):
        out_ref[index, :256, :HD] = query
        out_ref[index, :256, HD:] = half
        out_ref[index, 256:, :] = gains


def pack(query, key, value, gains):
    vmem = pl.BlockSpec(memory_space=pltpu.VMEM)
    return pl.pallas_call(
        pack_kernel,
        out_shape=jax.ShapeDtypeStruct((8, 272, 256), bf16),
        in_specs=[vmem] * 4,
        out_specs=vmem,
        compiler_params=pltpu.CompilerParams(vmem_limit_bytes=8 * MIB),
        cost_estimate=SMALL,
        name="pack",
    )(query, key.T, value.T, gains)


def merge_kernel(keep_ref, came_ref, own_ref, one_ref, two_ref, three_ref):
    for block, out_ref in enumerate((three_ref, two_ref, one_ref, own_ref)):
        rows = pl.ds(block * ROWS, ROWS)
        total = keep_ref[rows, :] + came_ref[rows, :].astype(f32)
        out_ref[...] = total.astype(out_ref.dtype)


def merge(keep, came):
    vmem = pl.BlockSpec(memory_space=pltpu.VMEM)
    away = jax.ShapeDtypeStruct((ROWS, HD), bf16)
    return pl.pallas_call(
        merge_kernel,
        out_shape=(jax.ShapeDtypeStruct((ROWS, HD), f32), away, away, away),
        in_specs=[vmem] * 2,
        out_specs=(vmem,) * 4,
        compiler_params=pltpu.CompilerParams(vmem_limit_bytes=12 * MIB),
        cost_estimate=SMALL,
        name="merge",
    )(keep, came)


def norm_kernel(parts_ref, rows_ref, gain_ref, hidden_ref, out_ref):
    hidden = rows_ref[...].astype(f32)
    hidden = hidden + sum(parts_ref[index].astype(f32) for index in range(8))
    hidden_ref[...] = hidden
    normed = (hidden * inverse_rms(hidden) * gain_ref[...]).astype(bf16)
    for index in range(8):
        out_ref[index] = normed


def norm(parts, rows, gain):
    vmem = pl.BlockSpec(memory_space=pltpu.VMEM)
    return pl.pallas_call(
        norm_kernel,
        out_shape=(
            pltpu.HBM((64, D), f32),
            pltpu.HBM((8, 64, D), bf16),
        ),
        in_specs=[vmem] * 3,
        out_specs=(vmem, vmem),
        compiler_params=pltpu.CompilerParams(vmem_limit_bytes=12 * MIB),
        cost_estimate=SMALL,
        name="norm",
    )(in_hbm(parts), rows, gain)


def norm_grad_kernel(
    parts_ref, hidden_ref, gain_ref, grad_ref, hidden_grad_ref, gain_grad_ref, out_ref
):
    grad = sum(parts_ref[index].astype(f32) for index in range(8))
    hidden = hidden_ref[...]
    inverse = inverse_rms(hidden)
    normal = hidden * inverse
    gain_grad_ref[...] = jnp.sum(grad * normal, axis=0, keepdims=True)
    grad = grad_ref[...].astype(f32) + norm_back(grad * gain_ref[...], normal, inverse)
    hidden_grad_ref[...] = grad
    for index in range(8):
        out_ref[index] = grad.astype(bf16)


def norm_grad(parts, hidden, gain, grad):
    vmem = pl.BlockSpec(memory_space=pltpu.VMEM)
    return pl.pallas_call(
        norm_grad_kernel,
        out_shape=(
            pltpu.HBM((64, D), f32),
            jax.ShapeDtypeStruct((1, D), f32),
            pltpu.HBM((8, 64, D), bf16),
        ),
        in_specs=[vmem] * 4,
        out_specs=(vmem,) * 3,
        compiler_params=pltpu.CompilerParams(vmem_limit_bytes=12 * MIB),
        cost_estimate=SMALL,
        name="norm_grad",
    )(in_hbm(parts), hidden, gain, grad)


def turned_columns(block):
    return jnp.concatenate(
        [block[:, at * 256 : at * 256 + 256] for at in (0, 4, 1, 5, 2, 6, 3, 7)], axis=1
    )


def turned_place(index):
    return (index % 2) * 4 + index // 2


def feed_kernel(
    normed_ref,
    grad_ref,
    near_source_ref,
    far_source_ref,
    near_out_ref,
    far_out_ref,
    part_ref,
    near_ref,
    far_ref,
    sems,
):
    copies = [
        pltpu.make_async_copy(near_source_ref, near_ref, sems.at[0]),
        pltpu.make_async_copy(far_source_ref, far_ref, sems.at[1]),
    ]
    first = pl.program_id(0) == 0

    @pl.when(first)
    def _():
        for copy in copies:
            copy.start()

    def arrived(index):
        @pl.when(first)
        def _():
            copies[index].wait()

    normed = turned_columns(normed_ref[...].reshape(256, D))
    grad = turned_columns(grad_ref[...].reshape(256, D))
    for index, (weight_ref, out_ref) in enumerate(
        ((near_ref, near_out_ref), (far_ref, far_out_ref))
    ):
        arrived(index)
        wide = plain_dot(normed, weight_ref[:, :768])
        gate, up = wide[:, :384], wide[:, 384:]
        grad_act = plain_dot(grad, weight_ref[:, 768:])
        sigma = jax.nn.sigmoid(gate)
        silu = gate * sigma
        grad_gate = grad_act * up * sigma * (1.0 + gate * (1.0 - sigma))
        out_ref[:, :384] = grad_gate.astype(bf16)
        out_ref[:, 384:768] = (grad_act * silu).astype(bf16)
        out_ref[:, 768:] = (silu * up).astype(bf16)
    part = right_dot(near_out_ref[:, :768], near_ref[:, :768])
    part = part + right_dot(far_out_ref[:, :768], far_ref[:, :768])
    for index in range(8):
        at = turned_place(index) * 256
        part_ref[:, at : at + 256] = part[:, index * 256 : index * 256 + 256].astype(bf16)


def feed(normed, grad, near, far):
    rows = pl.BlockSpec((4, 64, D), lambda i: (i, 0, 0))
    tile = pl.BlockSpec((256, D), lambda i: (i, 0))
    weight = pl.BlockSpec(memory_space=pl.ANY)
    out = pl.BlockSpec((256, 1152), lambda i: (i, 0))
    return pl.pallas_call(
        feed_kernel,
        grid=(2,),
        out_shape=(
            pltpu.HBM((512, 1152), bf16),
            pltpu.HBM((512, 1152), bf16),
            pltpu.HBM((512, D), bf16),
        ),
        in_specs=[rows, rows, weight, weight],
        out_specs=(out, out, tile),
        scratch_shapes=[
            pltpu.VMEM((D, 1152), bf16),
            pltpu.VMEM((D, 1152), bf16),
            pltpu.SemaphoreType.DMA((2,)),
        ],
        compiler_params=pltpu.CompilerParams(vmem_limit_bytes=36 * MIB),
        cost_estimate=SMALL,
        name="feed",
    )(normed, grad, in_hbm(near), in_hbm(far))


def weights_grad_kernel(
    normed_near_ref,
    normed_far_ref,
    grad_near_ref,
    grad_far_ref,
    near_ref,
    far_ref,
    out_ref,
    near_turned_ref,
    far_turned_ref,
):
    @pl.when(pl.program_id(0) == 0)
    def _():
        near_turned_ref[...] = near_ref[...].T
        far_turned_ref[...] = far_ref[...].T

    wide = plain_dot(near_turned_ref[:768, :], normed_near_ref[...].reshape(512, 256))
    wide = wide + plain_dot(far_turned_ref[:768, :], normed_far_ref[...].reshape(512, 256))
    down = plain_dot(near_turned_ref[768:, :], grad_near_ref[...].reshape(512, 256))
    down = down + plain_dot(far_turned_ref[768:, :], grad_far_ref[...].reshape(512, 256))
    out_ref[0, :768, :] = wide.astype(bf16)
    out_ref[0, 768:, :] = down.astype(bf16)


def weights_grad(normed, grad, hidden, earlier):
    rows = pl.BlockSpec((8, 64, 256), lambda i: (0, 0, i))
    whole = pl.BlockSpec((512, 1152), lambda i: (0, 0))
    return pl.pallas_call(
        ordered(weights_grad_kernel, 6, earlier),
        grid=(8,),
        out_shape=pltpu.HBM((8, 1152, 256), bf16),
        in_specs=[rows] * 4 + [whole] * 2 + unread(earlier),
        out_specs=pl.BlockSpec((1, 1152, 256), lambda i: (i % 4 * 2 + i // 4, 0, 0)),
        scratch_shapes=[pltpu.VMEM((1152, 512), bf16)] * 2,
        compiler_params=pltpu.CompilerParams(vmem_limit_bytes=24 * MIB),
        cost_estimate=SMALL,
        name="weights_grad",
    )(*normed, *grad, *hidden, *earlier)


def down_kernel(
    place_ref,
    near_act_ref,
    far_act_ref,
    near_ref,
    far_ref,
    hidden_ref,
    out_ref,
    mark_ref,
    total_ref,
):
    chip = place_ref[0]
    total = right_dot(near_act_ref[...], near_ref[...])
    total_ref[...] = total + right_dot(far_act_ref[...], far_ref[...])

    @pl.when(pl.program_id(0) == chip // 4)
    def _():
        rows = pl.ds(pl.multiple_of((chip % 4) * 64, 64), 64)
        total_ref[rows, :] += turned_columns(hidden_ref[...])

    for index in range(8):
        cols = total_ref[:, index * 256 : index * 256 + 256]
        out_ref[turned_place(index)] = cols.astype(bf16)
    mark_ref[...] = total_ref[:, :256].astype(bf16)


def down(chip, near_act, far_act, near, far, hidden, earlier):
    weight = pl.BlockSpec((D, 384), lambda i: (0, 2))
    return pl.pallas_call(
        ordered(down_kernel, 6, earlier),
        grid=(2,),
        out_shape=(
            pltpu.HBM((8, 512, 256), bf16),
            jax.ShapeDtypeStruct((512, 256), bf16),
        ),
        in_specs=[
            pl.BlockSpec(memory_space=pltpu.SMEM),
            pl.BlockSpec((256, 384), lambda i: (i, 2)),
            pl.BlockSpec((256, 384), lambda i: (i, 2)),
            weight,
            weight,
            pl.BlockSpec((64, D), lambda i: (0, 0)),
            *unread(earlier),
        ],
        out_specs=(
            pl.BlockSpec((8, 256, 256), lambda i: (0, i, 0)),
            pl.BlockSpec((256, 256), lambda i: (i, 0)),
        ),
        scratch_shapes=[pltpu.VMEM((256, D), f32)],
        compiler_params=pltpu.CompilerParams(vmem_limit_bytes=24 * MIB),
        cost_estimate=SMALL,
        name="down",
    )(chip, near_act, far_act, near, far, hidden, *earlier)


def input_part_kernel(
    place_ref,
    near_ref,
    far_ref,
    near_weight_ref,
    far_weight_ref,
    rows_ref,
    gain_ref,
    hidden_ref,
    mlp_ref,
    head_ref,
    out_ref,
    mark_ref,
    total_ref,
    term_ref,
    sum_ref,
):
    step = pl.program_id(0)
    part = right_dot(near_ref[...], near_weight_ref[...])
    part = part + right_dot(far_ref[...], far_weight_ref[...])
    rows = rows_ref[...].astype(f32)
    inverse = inverse_rms(rows)
    gain = gain_ref[...]
    weighted = part * (rows * inverse)
    term = jnp.sum(weighted * gain, axis=1, keepdims=True) * (1.0 / D)
    term_ref[pl.ds(step, 1), :] = jnp.broadcast_to(term, (256, 128)).T[:1, :]
    sums = jnp.sum(weighted.reshape(32, 8, D), axis=0)

    @pl.when(step == 0)
    def _():
        sum_ref[...] = sums

    @pl.when(step > 0)
    def _():
        sum_ref[...] += sums

    total_ref[...] = part * (gain * inverse)
    hidden = hidden_ref[...]
    for span in range(2):
        own = pl.ds(pl.multiple_of(span * 128 + place_ref[0] * 16, 16), 16)
        total_ref[own, :] += hidden[span * 16 : span * 16 + 16, :]
    at = pl.ds(pl.multiple_of(step * 256, 256), 256)
    for index in range(8):
        cols = total_ref[:, index * 256 : index * 256 + 256]
        out_ref[index, at, :] = cols.astype(bf16)
    mark_ref[...] = total_ref[:, :256].astype(bf16)

    @pl.when(step == 1)
    def _():
        terms = term_ref[:2, :]
        coarse = terms.astype(bf16).astype(f32)
        totals = jnp.sum(sum_ref[...], axis=0, keepdims=True)
        extra = jnp.concatenate(
            [coarse, terms - coarse]
            + [totals[:, index * 256 : index * 256 + 256] for index in range(8)]
            + [mlp_ref[:, index * 256 : index * 256 + 256] for index in range(8)]
            + [head_ref[...], jnp.zeros((11, 256), f32)],
            axis=0,
        ).astype(bf16)
        for index in range(8):
            out_ref[index, 512:, :] = extra


def input_part(
    place, near, far, near_weight, far_weight, rows, gain, hidden, mlp, head, earlier
):
    def fixed(*shape):
        return pl.BlockSpec(shape, lambda i, place_ref: (0,) * len(shape))

    def tile(*shape):
        return pl.BlockSpec(shape, lambda i, place_ref: (i, 0))

    def own(*shape):
        return pl.BlockSpec(shape, lambda i, place_ref: (place_ref[1] * 2 + i, 0))

    return pl.pallas_call(
        ordered(input_part_kernel, 10, earlier),
        out_shape=(
            pltpu.HBM((8, 544, 256), bf16),
            jax.ShapeDtypeStruct((512, 256), bf16),
        ),
        grid_spec=pltpu.PrefetchScalarGridSpec(
            num_scalar_prefetch=1,
            grid=(2,),
            in_specs=[
                tile(256, 256),
                tile(256, 256),
                fixed(D, 256),
                fixed(D, 256),
                own(256, D),
                fixed(1, D),
                tile(32, D),
                fixed(1, D),
                fixed(1, 256),
                *unread(earlier),
            ],
            out_specs=(fixed(8, 544, 256), tile(256, 256)),
            scratch_shapes=[
                pltpu.VMEM((256, D), f32),
                pltpu.VMEM((8, 256), f32),
                pltpu.VMEM((8, D), f32),
            ],
        ),
        compiler_params=pltpu.CompilerParams(vmem_limit_bytes=28 * MIB),
        cost_estimate=SMALL,
        name="input_part",
    )(place, near, far, near_weight, far_weight, rows, gain, hidden, mlp, head, *earlier)


def attention_grads_kernel(normed_ref, grad_ref, grad_out_ref, out_ref, turned_ref):
    @pl.when(pl.program_id(0) == 0)
    def _():
        turned_ref[...] = grad_ref[...].T

    out_ref[0, :256, :] = plain_dot(turned_ref[...], normed_ref[...]).astype(bf16)
    out_ref[0, 256:, :] = grad_out_ref[...]


def attention_grads(normed, grad_proj, grad_out, earlier):
    return pl.pallas_call(
        ordered(attention_grads_kernel, 3, earlier),
        grid=(8,),
        out_shape=jax.ShapeDtypeStruct((8, 384, 256), bf16),
        in_specs=[
            pl.BlockSpec((ROWS, 256), lambda i: (0, i)),
            pl.BlockSpec((ROWS, 256), lambda i: (0, 0)),
            pl.BlockSpec((HD, 256), lambda i: (0, i)),
            *unread(earlier),
        ],
        out_specs=pl.BlockSpec((1, 384, 256), lambda i: (i % 4 * 2 + i // 4, 0, 0)),
        scratch_shapes=[pltpu.VMEM((256, ROWS), bf16)],
        compiler_params=pltpu.CompilerParams(vmem_limit_bytes=12 * MIB),
        cost_estimate=SMALL,
        name="attention_grads",
    )(normed, grad_proj, grad_out, *earlier)


def body(
    inputs,
    out_grad,
    lengths,
    span_order,
    w_query,
    w_key,
    w_value,
    w_out,
    w_gate,
    w_up,
    w_down,
    norm_attn,
    norm_mlp,
    norm_query,
    norm_key,
):
    xl, z, xh, y, core = (lax.axis_index(name) for name in ("xl", "z", "xh", "y", "c"))
    span_place = xl * 4 + z
    chip = xh * 4 + y
    first = core == 0

    def by_core(near, far, axis=0):
        join = jnp.stack if axis is None else lambda parts: jnp.concatenate(parts, axis=axis)
        return jnp.where(first, join([near, far]), join([far, near]))

    def split(block):
        near = lax.dynamic_slice_in_dim(block, core * 512, 512, 0)
        far = lax.dynamic_slice_in_dim(block, (1 - core) * 512, 512, 0)
        return near, far

    def chip_major(block):
        return block.reshape(4, 8, 16, -1).transpose(1, 0, 2, 3).reshape(512, -1)

    def span_major(block):
        return block.reshape(8, 4, 16, -1).transpose(1, 0, 2, 3).reshape(512, -1)

    gains = jnp.concatenate([norm_attn, norm_mlp, norm_query, norm_key])
    gains = jnp.pad(gains, (0, 16 * 256 - 544)).reshape(16, 256)
    spread_weights = exchange(pack(w_query, w_key, w_value, gains), SPANS)
    qkv_weights = spread_weights[:, :256].reshape(D, 256)
    gains = spread_weights[:, 256:259].reshape(8, 768).astype(f32)
    gain_attn = gains[:, :256].reshape(1, D)
    gain_mlp = gains[:, 256:512].reshape(1, D)
    gain_query = gains[:, 512:528].reshape(1, HD)
    gain_key = gains[:, 528:544].reshape(1, HD)
    key_half, value_half = qkv_weights[:, 128:192], qkv_weights[:, 192:256]
    other_half = swap(jnp.where(first, value_half, key_half))
    near_weight = jnp.where(
        first,
        jnp.concatenate([qkv_weights[:, :192], other_half], 1),
        jnp.concatenate([qkv_weights[:, :128], other_half, value_half], 1),
    )

    route, starts, low = routes(jnp.stack([span_place, xl, z]), lengths, span_order)

    def reorder(index, rows):
        return plain_dot(route[index], rows).astype(bf16)

    moving = lax.dynamic_index_in_dim(
        out_grad.reshape(8, 16, 8, D), chip * 2 + core, 1, keepdims=False
    ).reshape(64, D)
    moving = reorder(0, moving).reshape(8, 8, D)
    spread_out = jnp.broadcast_to(w_out.reshape(1, 16, D), (8, 16, D))
    moving = jnp.concatenate([moving, spread_out], axis=1)
    arrived = exchange(after(moving, qkv_weights), SPANS)
    out_weights = arrived[:, 8:].reshape(8, HD, 256)
    moving = arrived[:, :8].reshape(64, D)

    ends = jnp.cumsum(lax.dynamic_index_in_dim(lengths, xl, 0, keepdims=False))
    offset = z * ROWS + jnp.arange(ROWS, dtype=jnp.int32)
    doc_start = jnp.where(offset >= ends[1], ends[1], jnp.where(offset >= ends[0], ends[0], 0))
    frequency = jnp.power(rope_base, -2.0 * jnp.arange(HD // 2, dtype=f32) / HD)
    angles = (offset - doc_start).astype(f32)[:, None] * frequency[None, :]
    cos_table, sin_table = jnp.cos(angles), jnp.sin(angles)
    cos_table = jnp.concatenate([cos_table, cos_table], axis=1)
    sin_table = jnp.concatenate([-sin_table, sin_table], axis=1)

    normed, inverse_one, query_bf, own_kv, query_proj, kv_proj = project(
        core.reshape(1),
        in_hbm(inputs),
        gain_attn,
        near_weight,
        cos_table,
        sin_table,
        gain_query,
        gain_key,
    )
    ready_kv = after(own_kv, arrived)
    moving = after(reorder(1, moving), own_kv)
    moving = exchange(moving.reshape(8, 8, D), SPANS).reshape(64, D)
    moving = reorder(2, moving).reshape(8, 8, D)
    near = lax.dynamic_slice_in_dim(moving, core * 4, 4, 0)
    far = lax.dynamic_slice_in_dim(moving, (1 - core) * 4, 4, 0)
    own_grad = by_core(near, swap(far), 1).reshape(64, D)
    spread_grad = jnp.broadcast_to(own_grad[None], (8, 64, D))
    grad_mine = exchange(spread_grad, CHIPS)

    mine = jnp.concatenate(
        [onward(ready_kv, 3), onward(ready_kv, 2), onward(ready_kv, 1), own_kv], axis=0
    )
    mine = after(mine, spread_grad)
    other = swap(mine)
    all_keys = jnp.where(first, mine, other)
    all_values = jnp.where(first, other, mine)

    out_weights = out_weights.transpose(1, 0, 2).reshape(HD, D)
    out_two = jnp.concatenate([out_weights, swap(out_weights)], axis=0)

    mlp_shard = after(jnp.concatenate([w_gate, w_up, w_down.T], axis=1), qkv_weights)
    grad_fence = fence(spread_grad)
    far_shard = after(far_span(mlp_shard), mine, grad_fence)
    mlp_shard = jnp.where(
        xl == 0,
        jnp.concatenate([mlp_shard, far_shard]),
        jnp.concatenate([far_shard, mlp_shard]),
    )
    near_weights = lax.all_gather(mlp_shard, "z", axis=0, tiled=True)

    own_rows = lax.dynamic_slice_in_dim(inputs, core * 512, 512, 0).reshape(4, 8, 16, D)
    own_rows = lax.dynamic_index_in_dim(own_rows, chip, 1, keepdims=False).reshape(64, D)

    attended, attended_full, total = attend(
        low,
        starts,
        in_hbm(query_bf),
        in_hbm(all_keys),
        in_hbm(all_values),
        [grad_fence, out_two, mlp_shard, own_rows],
    )

    att_near, att_far = split(attended)
    att_near, att_far = after(chip_major(att_near), grad_mine), after(chip_major(att_far), grad_mine)
    att_two = jnp.concatenate([att_near, swap(att_far)], axis=1)
    branch = plain_dot(att_two, out_two).astype(bf16)
    branch = branch.reshape(8, 64, D)
    branch = exchange(branch, CHIPS)
    far_weights = swap(after(near_weights, branch))
    hidden, spread_normed = norm(branch, own_rows, gain_mlp)
    normed_mine = exchange(spread_normed, CHIPS)

    near_out, far_out, part = feed(normed_mine, grad_mine, near_weights, far_weights)
    mlp_grads = weights_grad(
        (normed_mine, swap(normed_mine)),
        (grad_mine, swap(grad_mine)),
        (near_out, swap(far_out)),
        [fence(part)],
    )
    part = exchange(part.reshape(8, 64, D), CHIPS)
    part, mlp_grads = lax.optimization_barrier((part, mlp_grads))
    def by_span(block):
        sent = lax.dynamic_index_in_dim(block, 1 - xl, 0, keepdims=False)
        return lax.dynamic_index_in_dim(block, xl, 0, keepdims=False), far_span(sent)

    mlp_grads = lax.psum_scatter(mlp_grads, "z", scatter_dimension=0, tiled=True)

    grad_hidden, gain_mlp_part, spread_branch = norm_grad(part, hidden, gain_mlp, own_grad)
    out_cols, out_mark = down(
        chip.reshape(1),
        near_out,
        far_out,
        near_weights,
        far_weights,
        hidden,
        [fence(spread_branch)],
    )
    far_weight = swap(near_weight)
    branch_mine = exchange(spread_branch, CHIPS).reshape(512, D)
    branch_mine = after(branch_mine, out_cols, far_weight)
    out_cols, out_mark = after(out_cols, branch_mine), after(out_mark, branch_mine)
    out_fence = swap(out_mark)
    out_cols = exchange(out_cols, CHIPS)
    grad_two = right_dot(branch_mine, out_two).astype(bf16)
    grad_att = by_core(span_major(grad_two[:, :HD]), span_major(swap(grad_two[:, HD:])))

    grad_query_rot, keep, send = attend_back(
        low,
        core.reshape(1),
        starts,
        in_hbm(query_bf),
        in_hbm(all_keys),
        in_hbm(all_values),
        grad_att,
        in_hbm(attended_full),
        total,
        [out_fence],
    )
    came = swap(send)
    own_kv_grad, *away = merge(keep, came)
    received = [backward(block, by + 1) for by, block in enumerate(away)]

    def unorder(index, rows):
        return left_dot(route[index], rows).astype(bf16)

    grad_out = left_dot(att_two, after(branch_mine, received[2]))
    grad_out = (grad_out[:HD] + swap(grad_out[HD:].astype(bf16)).astype(f32)).astype(bf16)
    grad_proj, head_gains = project_back(
        core.reshape(1),
        in_hbm(grad_query_rot),
        own_kv_grad,
        [in_hbm(block) for block in received],
        in_hbm(cos_table),
        in_hbm(sin_table),
        (in_hbm(query_proj), in_hbm(kv_proj)),
        (gain_query, gain_key),
        [in_hbm(mlp_grads), out_cols],
    )

    grad_near, grad_far = split(grad_proj)
    by_cols, mark = input_part(
        jnp.stack([chip, core]),
        grad_near,
        swap(grad_far),
        in_hbm(near_weight),
        in_hbm(far_weight),
        in_hbm(inputs),
        gain_attn,
        in_hbm(grad_hidden),
        gain_mlp_part,
        head_gains,
        [],
    )
    mlp_kept, mlp_came = by_span(after(mlp_grads, grad_proj))
    grad_attn = attention_grads(normed, grad_proj, grad_out, [swap(mark), mlp_came])
    out_cols = after(out_cols, grad_attn)
    grad_attn = grad_attn.reshape(4, 2, 384, 256)
    parts = [
        lax.dynamic_index_in_dim(grad_attn, (z + by) % 4, 0, keepdims=False) for by in range(4)
    ]
    parts = [parts[0]] + [
        lax.ppermute(parts[by], "z", [(i, (i + by) % 4) for i in range(4)]) for by in (1, 2, 3)
    ]
    out_cols = jnp.sum(out_cols.astype(f32), axis=0).astype(bf16)
    near = jnp.where(first, out_cols[:, :128], out_cols[:, 128:])
    far = jnp.where(first, out_cols[:, 128:], out_cols[:, :128])
    out_cols = by_core(near, swap(far), None).reshape(2, 8, 4, 2, 8, 128)
    out_rows = jnp.concatenate(
        [out_cols[:, index // 2, :, index % 2].reshape(64, 128) for index in range(16)], axis=1
    )

    by_cols = exchange(by_cols, CHIPS)

    class_rows = exchange(after(unorder(2, out_rows).reshape(8, 8, D), by_cols), SPANS)
    out_rows = class_rows
    parts = lax.optimization_barrier((*parts, by_cols))[:4]
    grad_attn = sum(part.astype(f32) for part in parts)
    attn_kept, attn_came = by_span(grad_attn.astype(bf16))
    by_cols = jnp.sum(by_cols.astype(f32), axis=0)
    row_term = (by_cols[512:514] + by_cols[514:516]).reshape(512, 1)
    own_inverse = lax.dynamic_slice_in_dim(inverse_one, core * 512, 512, 0)
    own_cols = lax.dynamic_slice(inputs, (core * 512, chip * 256), (512, 256)).astype(f32)
    in_grad = by_cols[:512] - own_cols * (own_inverse * own_inverse * row_term)
    near = jnp.where(first, in_grad[:, :128], in_grad[:, 128:])
    far = jnp.where(first, in_grad[:, 128:], in_grad[:, :128])
    in_grad = by_core(near, swap(far))
    gain_sums = jnp.concatenate(
        [
            by_cols[516:524],
            by_cols[524:532],
            by_cols[532, :128].reshape(8, 16),
            by_cols[532, 128:].reshape(8, 16),
        ],
        axis=1,
    )
    gain_sums = gain_sums + swap(gain_sums)
    coarse = gain_sums.astype(bf16)
    extra = jnp.concatenate(
        [coarse, (gain_sums - coarse.astype(f32)).astype(bf16), jnp.zeros((8, 960), bf16)], axis=1
    )
    extra = jnp.pad(extra[:, None], ((0, 0), (0, 7), (0, 0)))
    out_rows = unorder(1, out_rows.reshape(64, D)).reshape(8, 8, D)
    out_rows = after(jnp.concatenate([out_rows, extra], axis=1), attn_came)
    out_rows = exchange(out_rows, SPANS)
    gain_sums = jnp.sum(out_rows[:, 8].astype(f32), axis=0)
    gain_sums = gain_sums[:544] + gain_sums[544:1088]
    layer_out = unorder(0, out_rows[:, :8].reshape(64, D))
    layer_out = jnp.stack(
        [layer_out[:, at * 128 : at * 128 + 128].reshape(8, 8, 128) for at in range(16)],
        axis=1,
    )
    layer_out = layer_out.reshape(ROWS, 128).astype(f32)

    grad_attn = attn_kept.astype(f32) + attn_came.astype(f32)
    grad_kv_weight = grad_attn[128:256]
    low_half, high_half = grad_kv_weight[:64], grad_kv_weight[64:]
    came = swap(jnp.where(first, high_half, low_half))
    kept = jnp.where(first, low_half, high_half)
    mlp_kept, mlp_came = after(mlp_kept, class_rows), after(mlp_came, class_rows)
    mlp_grads = mlp_kept.astype(f32) + mlp_came.astype(f32)

    return (
        layer_out,
        in_grad,
        grad_attn[:128].T,
        jnp.where(first, kept, came).T,
        jnp.where(first, came, kept).T,
        grad_attn[256:],
        mlp_grads[:384].T,
        mlp_grads[384:768].T,
        mlp_grads[768:],
        gain_sums[:256],
        gain_sums[256:512],
        gain_sums[512:528],
        gain_sums[528:544],
    )


def solution(mesh):
    fine = Mesh(mesh.devices.reshape(2, 4, 2, 4, 2), ("xl", "z", "xh", "y", "c"))
    rows = P(SPANS, None)
    by_both = P(SPANS, TENSOR)
    turned = P(TENSOR, SPANS)
    lone = P(SPANS)
    return jax.shard_map(
        body,
        mesh=fine,
        in_specs=(
            rows,
            rows,
            P(),
            P(),
            by_both,
            by_both,
            by_both,
            turned,
            by_both,
            by_both,
            turned,
            lone,
            lone,
            lone,
            lone,
        ),
        out_specs=(
            by_both,
            by_both,
            by_both,
            by_both,
            by_both,
            turned,
            by_both,
            by_both,
            turned,
            lone,
            lone,
            lone,
            lone,
        ),
        check_vma=False,
    )
```

```python
import jax
import jax.numpy as jnp
from jax import lax
from jax.experimental import pallas as pl
from jax.experimental.pallas import tpu as pltpu
from jax.sharding import Mesh, PartitionSpec as P

SPAN = 128
MICRO = 2
HD = 128
D = 2048
ROWS = 1024
KEYS = 4096
KEY_BLK = 512

epsilon = 1e-06
rope_base = 1000000.0
score_scale = HD ** (-0.5)
log2e = 1.4426950408889634
bf16 = jnp.bfloat16
f32 = jnp.float32
SPANS = ("xl", "z")
TENSOR = ("xh", "y", "c")
CHIPS = ("xh", "y")
MIB = 1024 * 1024
SMALL = pl.CostEstimate(flops=1024, bytes_accessed=1024, transcendentals=0)


def swap(block):
    return lax.ppermute(block, "c", [(0, 1), (1, 0)])


def far_span(block):
    return lax.ppermute(block, "xl", [(0, 1), (1, 0)])


def onward(block, by):
    return lax.ppermute(block, "z", [(i, i + by) for i in range(4) if i + by < 4])


def backward(block, by):
    return lax.ppermute(block, "z", [(i, i - by) for i in range(4) if i - by >= 0])


def exchange(block, axes):
    return lax.all_to_all(block, axes, 0, 0, tiled=True)


def spread(block, axes, count):
    return exchange(jnp.broadcast_to(block[None], (count,) + block.shape), axes)


def after(block, *earlier):
    return lax.optimization_barrier((block,) + earlier)[0]


def fence(block):
    return swap(block.reshape(-1, block.shape[-1])[:512, :256])


def ordered(kernel, inputs, earlier):
    return lambda *refs: kernel(*refs[:inputs], *refs[inputs + len(earlier) :])


def in_hbm(block):
    return pltpu.with_memory_space_constraint(block, pltpu.HBM)


def unread(earlier):
    return [pl.BlockSpec(memory_space=pl.ANY)] * len(earlier)


def plain_dot(first_op, second_op):
    return jnp.dot(first_op, second_op, preferred_element_type=f32)


def left_dot(first_op, second_op):
    return lax.dot_general(
        first_op, second_op, (((0,), (0,)), ((), ())), preferred_element_type=f32
    )


def right_dot(first_op, second_op):
    return lax.dot_general(
        first_op, second_op, (((1,), (1,)), ((), ())), preferred_element_type=f32
    )


def inverse_rms(values):
    return lax.rsqrt(jnp.mean(values * values, axis=-1, keepdims=True) + epsilon)


def norm_back(incoming, normal, inverse):
    return inverse * (incoming - normal * jnp.mean(incoming * normal, axis=-1, keepdims=True))


def block_mask(key_block, starts):
    key_at = key_block * KEY_BLK + lax.broadcasted_iota(jnp.int32, (KEY_BLK, ROWS), 0)
    query_at = (KEYS - ROWS) + lax.broadcasted_iota(jnp.int32, (KEY_BLK, ROWS), 1)
    return (key_at >= starts) & (key_at <= query_at)


def over_keys(range_ref, step, state):
    own = (KEYS - ROWS) // KEY_BLK
    seen = jnp.minimum(range_ref[1], own)
    state = lax.fori_loop(range_ref[0], seen, lambda at, state: step(at, state, True), state)
    state = lax.fori_loop(seen, own, lambda at, state: step(at, state, False), state)
    for at in range(own, KEYS // KEY_BLK):
        state = step(at, state, True)
    return state


def attend_kernel(range_ref, start_ref, q_ref, k_ref, v_ref, out_ref, full_ref, total_ref):
    queries = q_ref[...]
    starts = start_ref[...]

    def step(at, state, masked):
        acc, total = state
        rows = pl.ds(pl.multiple_of(at * KEY_BLK, KEY_BLK), KEY_BLK)
        weights = jnp.exp2(right_dot(k_ref[rows, :], queries) * (score_scale * log2e))
        if masked:
            weights = jnp.where(block_mask(at, starts), weights, 0.0)
        total = total + jnp.sum(weights, axis=0, keepdims=True)
        acc = acc + left_dot(v_ref[rows, :], weights.astype(bf16))
        return acc, total

    acc, total = over_keys(
        range_ref, step, (jnp.zeros((HD, ROWS), f32), jnp.zeros((1, ROWS), f32))
    )
    full = acc / total
    full_ref[...] = full
    total_ref[...] = jnp.log2(total)
    out_ref[...] = full.T.astype(bf16)


def attend(low, starts, queries, keys, values, earlier):
    vmem = pl.BlockSpec(memory_space=pltpu.VMEM)
    return pl.pallas_call(
        ordered(attend_kernel, 5, earlier),
        out_shape=(
            jax.ShapeDtypeStruct((ROWS, HD), bf16),
            pltpu.HBM((HD, ROWS), f32),
            jax.ShapeDtypeStruct((1, ROWS), f32),
        ),
        in_specs=[pl.BlockSpec(memory_space=pltpu.SMEM)] + [vmem] * 4 + unread(earlier),
        out_specs=(vmem,) * 3,
        compiler_params=pltpu.CompilerParams(vmem_limit_bytes=24 * MIB),
        cost_estimate=SMALL,
        name="attend",
    )(low, starts, queries, keys, values, *earlier)


def attend_back_kernel(
    range_ref,
    core_ref,
    start_ref,
    q_ref,
    k_ref,
    v_ref,
    do_ref,
    full_ref,
    total_ref,
    dq_ref,
    keep_ref,
    send_ref,
    dk_ref,
    dv_ref,
):
    dk_ref[...] = jnp.zeros_like(dk_ref)
    dv_ref[...] = jnp.zeros_like(dv_ref)
    queries = q_ref[...]
    starts = start_ref[...]
    incoming = do_ref[...]
    total = total_ref[...]
    delta = jnp.sum(incoming.astype(f32).T * full_ref[...], axis=0, keepdims=True)

    def step(at, acc, masked):
        rows = pl.ds(pl.multiple_of(at * KEY_BLK, KEY_BLK), KEY_BLK)
        keys = k_ref[rows, :]
        weights = jnp.exp2(right_dot(keys, queries) * (score_scale * log2e) - total)
        if masked:
            weights = jnp.where(block_mask(at, starts), weights, 0.0)
        grads = right_dot(v_ref[rows, :], incoming)
        grads = (weights * (grads - delta)).astype(bf16)
        dv_ref[rows, :] += plain_dot(weights.astype(bf16), incoming)
        dk_ref[rows, :] += plain_dot(grads, queries)
        return acc + left_dot(keys, grads)

    dq_ref[...] = over_keys(range_ref, step, jnp.zeros((HD, ROWS), f32)).T * score_scale

    @pl.when(core_ref[0] == 0)
    def _():
        keep_ref[...] = dk_ref[...] * score_scale
        send_ref[...] = dv_ref[...].astype(bf16)

    @pl.when(core_ref[0] == 1)
    def _():
        keep_ref[...] = dv_ref[...]
        send_ref[...] = (dk_ref[...] * score_scale).astype(bf16)


def attend_back(low, core, starts, queries, keys, values, incoming, full, total, earlier):
    vmem = pl.BlockSpec(memory_space=pltpu.VMEM)
    smem = pl.BlockSpec(memory_space=pltpu.SMEM)
    return pl.pallas_call(
        ordered(attend_back_kernel, 9, earlier),
        out_shape=(
            pltpu.HBM((ROWS, HD), f32),
            jax.ShapeDtypeStruct((KEYS, HD), f32),
            jax.ShapeDtypeStruct((KEYS, HD), bf16),
        ),
        in_specs=[smem, smem] + [vmem] * 7 + unread(earlier),
        out_specs=(vmem,) * 3,
        scratch_shapes=[pltpu.VMEM((KEYS, HD), f32), pltpu.VMEM((KEYS, HD), f32)],
        compiler_params=pltpu.CompilerParams(vmem_limit_bytes=32 * MIB),
        cost_estimate=SMALL,
        name="attend_back",
    )(low, core, starts, queries, keys, values, incoming, full, total, *earlier)


def colour_kernel(place_ref, lengths_ref, column_ref, row_ref, out_ref, start_ref, range_ref):
    micro, block = place_ref[1], place_ref[2]
    first_end = lengths_ref[micro, 0]
    second_end = first_end + lengths_ref[micro, 1]

    def begin(offset):
        begun = jnp.where(offset >= first_end, first_end, 0)
        begun = jnp.where(offset >= second_end, second_end, begun)
        return begun - (block - 3) * ROWS

    start_ref[...] = begin(block * ROWS + lax.broadcasted_iota(jnp.int32, (1, ROWS), 1))
    range_ref[0] = begin(block * ROWS) >> 9
    range_ref[1] = (begin(block * ROWS + ROWS - 1) + KEY_BLK - 1) >> 9
    down_at = lax.broadcasted_iota(jnp.int32, (64, 64), 0)
    across_at = lax.broadcasted_iota(jnp.int32, (64, 64), 1)
    same_slots = (down_at >> 3) == (across_at >> 3)
    same_spans = (column_ref[...] >> 3) == (row_ref[...] >> 3)
    colour = jnp.zeros((64, 1), jnp.int32)
    for _ in range(3):
        colour_row = jnp.sum(
            jnp.where(down_at == across_at, colour, 0).astype(f32), axis=0, keepdims=True
        ).astype(jnp.int32)
        alike = colour == colour_row

        def partner(group):
            near = group & alike
            rank_down = jnp.sum(
                jnp.where(near & (across_at < down_at), 1.0, 0.0), axis=1, keepdims=True
            ).astype(jnp.int32)
            rank_across = jnp.sum(
                jnp.where(near & (down_at < across_at), 1.0, 0.0), axis=0, keepdims=True
            ).astype(jnp.int32)
            return jnp.where(near & ((rank_down ^ 1) == rank_across), 1.0, 0.0)

        by_slot = partner(same_slots)
        jump = plain_dot(by_slot, partner(same_spans))
        label = lax.broadcasted_iota(jnp.int32, (64, 128), 0).astype(f32)
        for turn in range(5):
            label = jnp.minimum(label, plain_dot(jump, label))
            if turn < 4:
                jump = plain_dot(jump, jump)
        bit = jnp.where(label > plain_dot(by_slot, label), 1, 0)
        colour = colour * 2 + bit[:, :1]
    colour_row = jnp.sum(
        jnp.where(down_at == across_at, colour, 0).astype(f32), axis=0, keepdims=True
    )
    own = place_ref[0]
    same_row = (down_at & 7) == (across_at & 7)
    slot_colour = jnp.sum(
        jnp.where(down_at == own * 8 + (across_at >> 3), colour, 0).astype(f32),
        axis=0,
        keepdims=True,
    ).astype(jnp.int32)
    owner = jnp.sum(
        jnp.where(same_slots & (colour == own), column_ref[...] >> 3, 0).astype(f32),
        axis=0,
        keepdims=True,
    ).astype(jnp.int32)
    span_colour = jnp.sum(
        jnp.where(row_ref[...] == own * 8 + (down_at >> 3), colour_row, 0.0),
        axis=1,
        keepdims=True,
    ).astype(jnp.int32)
    for index, match in enumerate(
        (
            slot_colour == (down_at >> 3),
            owner == (down_at >> 3),
            span_colour == (across_at >> 3),
        )
    ):
        out_ref[index] = jnp.where(match & same_row, 1.0, 0.0).astype(bf16)


def routes(place, lengths, span_order):
    vmem = pl.BlockSpec(memory_space=pltpu.VMEM)
    smem = pl.BlockSpec(memory_space=pltpu.SMEM)
    return pl.pallas_call(
        colour_kernel,
        out_shape=(
            jax.ShapeDtypeStruct((3, 64, 64), bf16),
            jax.ShapeDtypeStruct((1, ROWS), jnp.int32),
            jax.ShapeDtypeStruct((2,), jnp.int32),
        ),
        in_specs=[smem, smem, vmem, vmem],
        out_specs=(vmem, vmem, smem),
        name="routes",
    )(place, lengths, span_order.reshape(64, 1), span_order.reshape(1, 64))


def project_kernel(
    place_ref,
    rows_ref,
    gain_ref,
    weight_ref,
    cos_ref,
    sin_ref,
    gain_query_ref,
    gain_key_ref,
    normed_ref,
    inverse_ref,
    query_out_ref,
    kv_out_ref,
    query_proj_ref,
    kv_proj_ref,
):
    rows = rows_ref[...].astype(f32)
    inverse = inverse_rms(rows)
    normed = (rows * inverse * gain_ref[...]).astype(bf16)
    inverse_ref[...] = inverse
    normed_ref[...] = normed
    cos, sin = cos_ref[...], sin_ref[...]

    def turned(values):
        return values * cos + pltpu.roll(values, 64, 1) * sin

    proj = plain_dot(normed, weight_ref[...])
    query, kv = proj[:, :HD], proj[:, HD:]
    kv_proj_ref[...] = kv
    key = turned(kv * inverse_rms(kv) * gain_key_ref[...])
    kv_out_ref[...] = jnp.where(place_ref[0] == 0, key, kv).astype(bf16)
    query_proj_ref[...] = query
    query = turned(query * inverse_rms(query) * gain_query_ref[...])
    query_out_ref[...] = query.astype(bf16)


def project(core, rows, gain, weights, cos, sin, gain_query, gain_key):
    wide = pl.BlockSpec((256, D), lambda i: (i, 0))
    head = pl.BlockSpec((256, HD), lambda i: (i, 0))
    one = pl.BlockSpec((256, 1), lambda i: (i, 0))
    weight = pl.BlockSpec((D, 256), lambda i: (0, 0))
    small = pl.BlockSpec((1, HD), lambda i: (0, 0))
    column = pltpu.HBM((ROWS, 1), f32)
    return pl.pallas_call(
        project_kernel,
        grid=(4,),
        out_shape=(
            pltpu.HBM((ROWS, D), bf16),
            column,
            jax.ShapeDtypeStruct((ROWS, HD), bf16),
            jax.ShapeDtypeStruct((ROWS, HD), bf16),
            pltpu.HBM((ROWS, HD), f32),
            pltpu.HBM((ROWS, HD), f32),
        ),
        in_specs=[
            pl.BlockSpec(memory_space=pltpu.SMEM),
            wide,
            pl.BlockSpec((1, D), lambda i: (0, 0)),
            weight,
            head,
            head,
            small,
            small,
        ],
        out_specs=(wide, one, head, head, head, head),
        compiler_params=pltpu.CompilerParams(vmem_limit_bytes=20 * MIB),
        cost_estimate=SMALL,
        name="project",
    )(core, rows, gain, weights, cos, sin, gain_query, gain_key)


def project_back_kernel(
    place_ref,
    query_grad_ref,
    own_ref,
    one_ref,
    two_ref,
    three_ref,
    cos_ref,
    sin_ref,
    query_proj_ref,
    kv_proj_ref,
    gain_query_ref,
    gain_key_ref,
    out_ref,
    sum_ref,
):
    cos, sin = cos_ref[...], sin_ref[...]

    def turned_back(values):
        return values * cos - pltpu.roll(values, 64, 1) * sin

    step = pl.program_id(0)
    grad = turned_back(query_grad_ref[...])
    query = query_proj_ref[...]
    inverse = inverse_rms(query)
    hat = query * inverse
    sums = jnp.sum(grad * hat, axis=0, keepdims=True)
    query = norm_back(grad * gain_query_ref[...], hat, inverse)
    out_ref[:, :HD] = query.astype(bf16)
    kv = own_ref[...] + one_ref[...].astype(f32)
    kv = kv + two_ref[...].astype(f32) + three_ref[...].astype(f32)
    grad = turned_back(kv)
    key = kv_proj_ref[...]
    inverse = inverse_rms(key)
    hat = key * inverse
    is_key = place_ref[0] == 0
    key_sums = jnp.where(is_key, jnp.sum(grad * hat, axis=0, keepdims=True), 0.0)
    key = norm_back(grad * gain_key_ref[...], hat, inverse)
    out_ref[:, HD:] = jnp.where(is_key, key, kv).astype(bf16)
    sums = jnp.concatenate([sums, key_sums], axis=1)

    @pl.when(step == 0)
    def _():
        sum_ref[...] = sums

    @pl.when(step > 0)
    def _():
        sum_ref[...] += sums


def project_back(core, query_grad, own, arrived, cos, sin, projections, gains, earlier):
    head = pl.BlockSpec((256, HD), lambda i: (i, 0))
    small = pl.BlockSpec((1, HD), lambda i: (0, 0))
    return pl.pallas_call(
        ordered(project_back_kernel, 12, earlier),
        grid=(4,),
        out_shape=(
            jax.ShapeDtypeStruct((ROWS, 256), bf16),
            jax.ShapeDtypeStruct((1, 256), f32),
        ),
        in_specs=[pl.BlockSpec(memory_space=pltpu.SMEM)]
        + [head] * 9
        + [small] * 2
        + unread(earlier),
        out_specs=(
            pl.BlockSpec((256, 256), lambda i: (i, 0)),
            pl.BlockSpec((1, 256), lambda i: (0, 0)),
        ),
        compiler_params=pltpu.CompilerParams(vmem_limit_bytes=12 * MIB),
        cost_estimate=SMALL,
        name="project_back",
    )(core, query_grad, own, *arrived, cos, sin, *projections, *gains, *earlier)


def pack_kernel(query_ref, key_ref, value_ref, gains_ref, out_ref):
    half = jnp.concatenate([key_ref[...], value_ref[...]], axis=0).T
    query = query_ref[...]
    gains = gains_ref[...]
    for index in range(8):
        out_ref[index, :256, :HD] = query
        out_ref[index, :256, HD:] = half
        out_ref[index, 256:, :] = gains


def pack(query, key, value, gains):
    vmem = pl.BlockSpec(memory_space=pltpu.VMEM)
    return pl.pallas_call(
        pack_kernel,
        out_shape=jax.ShapeDtypeStruct((8, 272, 256), bf16),
        in_specs=[vmem] * 4,
        out_specs=vmem,
        compiler_params=pltpu.CompilerParams(vmem_limit_bytes=8 * MIB),
        cost_estimate=SMALL,
        name="pack",
    )(query, key.T, value.T, gains)


def merge_kernel(keep_ref, came_ref, own_ref, one_ref, two_ref, three_ref):
    for block, out_ref in enumerate((three_ref, two_ref, one_ref, own_ref)):
        rows = pl.ds(block * ROWS, ROWS)
        total = keep_ref[rows, :] + came_ref[rows, :].astype(f32)
        out_ref[...] = total.astype(out_ref.dtype)


def merge(keep, came):
    vmem = pl.BlockSpec(memory_space=pltpu.VMEM)
    away = jax.ShapeDtypeStruct((ROWS, HD), bf16)
    return pl.pallas_call(
        merge_kernel,
        out_shape=(jax.ShapeDtypeStruct((ROWS, HD), f32), away, away, away),
        in_specs=[vmem] * 2,
        out_specs=(vmem,) * 4,
        compiler_params=pltpu.CompilerParams(vmem_limit_bytes=12 * MIB),
        cost_estimate=SMALL,
        name="merge",
    )(keep, came)


def norm_kernel(parts_ref, rows_ref, gain_ref, hidden_ref, out_ref):
    hidden = rows_ref[...].astype(f32)
    hidden = hidden + sum(parts_ref[index].astype(f32) for index in range(8))
    hidden_ref[...] = hidden
    normed = (hidden * inverse_rms(hidden) * gain_ref[...]).astype(bf16)
    for index in range(8):
        out_ref[index] = normed


def norm(parts, rows, gain):
    vmem = pl.BlockSpec(memory_space=pltpu.VMEM)
    return pl.pallas_call(
        norm_kernel,
        out_shape=(
            pltpu.HBM((64, D), f32),
            pltpu.HBM((8, 64, D), bf16),
        ),
        in_specs=[vmem] * 3,
        out_specs=(vmem, vmem),
        compiler_params=pltpu.CompilerParams(vmem_limit_bytes=12 * MIB),
        cost_estimate=SMALL,
        name="norm",
    )(in_hbm(parts), rows, gain)


def norm_grad_kernel(
    parts_ref, hidden_ref, gain_ref, grad_ref, hidden_grad_ref, gain_grad_ref, out_ref
):
    grad = sum(parts_ref[index].astype(f32) for index in range(8))
    hidden = hidden_ref[...]
    inverse = inverse_rms(hidden)
    normal = hidden * inverse
    gain_grad_ref[...] = jnp.sum(grad * normal, axis=0, keepdims=True)
    grad = grad_ref[...].astype(f32) + norm_back(grad * gain_ref[...], normal, inverse)
    hidden_grad_ref[...] = grad
    for index in range(8):
        out_ref[index] = grad.astype(bf16)


def norm_grad(parts, hidden, gain, grad):
    vmem = pl.BlockSpec(memory_space=pltpu.VMEM)
    return pl.pallas_call(
        norm_grad_kernel,
        out_shape=(
            pltpu.HBM((64, D), f32),
            jax.ShapeDtypeStruct((1, D), f32),
            pltpu.HBM((8, 64, D), bf16),
        ),
        in_specs=[vmem] * 4,
        out_specs=(vmem,) * 3,
        compiler_params=pltpu.CompilerParams(vmem_limit_bytes=12 * MIB),
        cost_estimate=SMALL,
        name="norm_grad",
    )(in_hbm(parts), hidden, gain, grad)


def turned_columns(block):
    return jnp.concatenate(
        [block[:, at * 256 : at * 256 + 256] for at in (0, 4, 1, 5, 2, 6, 3, 7)], axis=1
    )


def turned_place(index):
    return (index % 2) * 4 + index // 2


def feed_kernel(
    normed_ref,
    grad_ref,
    near_source_ref,
    far_source_ref,
    near_out_ref,
    far_out_ref,
    part_ref,
    near_ref,
    far_ref,
    sems,
):
    copies = [
        pltpu.make_async_copy(near_source_ref, near_ref, sems.at[0]),
        pltpu.make_async_copy(far_source_ref, far_ref, sems.at[1]),
    ]
    first = pl.program_id(0) == 0

    @pl.when(first)
    def _():
        for copy in copies:
            copy.start()

    def arrived(index):
        @pl.when(first)
        def _():
            copies[index].wait()

    normed = turned_columns(normed_ref[...].reshape(256, D))
    grad = turned_columns(grad_ref[...].reshape(256, D))
    for index, (weight_ref, out_ref) in enumerate(
        ((near_ref, near_out_ref), (far_ref, far_out_ref))
    ):
        arrived(index)
        wide = plain_dot(normed, weight_ref[:, :768])
        gate, up = wide[:, :384], wide[:, 384:]
        grad_act = plain_dot(grad, weight_ref[:, 768:])
        sigma = jax.nn.sigmoid(gate)
        silu = gate * sigma
        grad_gate = grad_act * up * sigma * (1.0 + gate * (1.0 - sigma))
        out_ref[:, :384] = grad_gate.astype(bf16)
        out_ref[:, 384:768] = (grad_act * silu).astype(bf16)
        out_ref[:, 768:] = (silu * up).astype(bf16)
    part = right_dot(near_out_ref[:, :768], near_ref[:, :768])
    part = part + right_dot(far_out_ref[:, :768], far_ref[:, :768])
    for index in range(8):
        at = turned_place(index) * 256
        part_ref[:, at : at + 256] = part[:, index * 256 : index * 256 + 256].astype(bf16)


def feed(normed, grad, near, far):
    rows = pl.BlockSpec((4, 64, D), lambda i: (i, 0, 0))
    tile = pl.BlockSpec((256, D), lambda i: (i, 0))
    weight = pl.BlockSpec(memory_space=pl.ANY)
    out = pl.BlockSpec((256, 1152), lambda i: (i, 0))
    return pl.pallas_call(
        feed_kernel,
        grid=(2,),
        out_shape=(
            pltpu.HBM((512, 1152), bf16),
            pltpu.HBM((512, 1152), bf16),
            pltpu.HBM((512, D), bf16),
        ),
        in_specs=[rows, rows, weight, weight],
        out_specs=(out, out, tile),
        scratch_shapes=[
            pltpu.VMEM((D, 1152), bf16),
            pltpu.VMEM((D, 1152), bf16),
            pltpu.SemaphoreType.DMA((2,)),
        ],
        compiler_params=pltpu.CompilerParams(vmem_limit_bytes=36 * MIB),
        cost_estimate=SMALL,
        name="feed",
    )(normed, grad, in_hbm(near), in_hbm(far))


def weights_grad_kernel(
    normed_near_ref,
    normed_far_ref,
    grad_near_ref,
    grad_far_ref,
    near_ref,
    far_ref,
    out_ref,
    near_turned_ref,
    far_turned_ref,
):
    @pl.when(pl.program_id(0) == 0)
    def _():
        near_turned_ref[...] = near_ref[...].T
        far_turned_ref[...] = far_ref[...].T

    wide = plain_dot(near_turned_ref[:768, :], normed_near_ref[...].reshape(512, 256))
    wide = wide + plain_dot(far_turned_ref[:768, :], normed_far_ref[...].reshape(512, 256))
    down = plain_dot(near_turned_ref[768:, :], grad_near_ref[...].reshape(512, 256))
    down = down + plain_dot(far_turned_ref[768:, :], grad_far_ref[...].reshape(512, 256))
    out_ref[0, :768, :] = wide.astype(bf16)
    out_ref[0, 768:, :] = down.astype(bf16)


def weights_grad(normed, grad, hidden, earlier):
    rows = pl.BlockSpec((8, 64, 256), lambda i: (0, 0, i))
    whole = pl.BlockSpec((512, 1152), lambda i: (0, 0))
    return pl.pallas_call(
        ordered(weights_grad_kernel, 6, earlier),
        grid=(8,),
        out_shape=pltpu.HBM((8, 1152, 256), bf16),
        in_specs=[rows] * 4 + [whole] * 2 + unread(earlier),
        out_specs=pl.BlockSpec((1, 1152, 256), lambda i: (i % 4 * 2 + i // 4, 0, 0)),
        scratch_shapes=[pltpu.VMEM((1152, 512), bf16)] * 2,
        compiler_params=pltpu.CompilerParams(vmem_limit_bytes=24 * MIB),
        cost_estimate=SMALL,
        name="weights_grad",
    )(*normed, *grad, *hidden, *earlier)


def down_kernel(
    place_ref,
    near_act_ref,
    far_act_ref,
    near_ref,
    far_ref,
    hidden_ref,
    out_ref,
    mark_ref,
    total_ref,
):
    chip = place_ref[0]
    total = right_dot(near_act_ref[...], near_ref[...])
    total_ref[...] = total + right_dot(far_act_ref[...], far_ref[...])

    @pl.when(pl.program_id(0) == chip // 4)
    def _():
        rows = pl.ds(pl.multiple_of((chip % 4) * 64, 64), 64)
        total_ref[rows, :] += turned_columns(hidden_ref[...])

    for index in range(8):
        cols = total_ref[:, index * 256 : index * 256 + 256]
        out_ref[turned_place(index)] = cols.astype(bf16)
    mark_ref[...] = total_ref[:, :256].astype(bf16)


def down(chip, near_act, far_act, near, far, hidden, earlier):
    weight = pl.BlockSpec((D, 384), lambda i: (0, 2))
    return pl.pallas_call(
        ordered(down_kernel, 6, earlier),
        grid=(2,),
        out_shape=(
            pltpu.HBM((8, 512, 256), bf16),
            jax.ShapeDtypeStruct((512, 256), bf16),
        ),
        in_specs=[
            pl.BlockSpec(memory_space=pltpu.SMEM),
            pl.BlockSpec((256, 384), lambda i: (i, 2)),
            pl.BlockSpec((256, 384), lambda i: (i, 2)),
            weight,
            weight,
            pl.BlockSpec((64, D), lambda i: (0, 0)),
            *unread(earlier),
        ],
        out_specs=(
            pl.BlockSpec((8, 256, 256), lambda i: (0, i, 0)),
            pl.BlockSpec((256, 256), lambda i: (i, 0)),
        ),
        scratch_shapes=[pltpu.VMEM((256, D), f32)],
        compiler_params=pltpu.CompilerParams(vmem_limit_bytes=24 * MIB),
        cost_estimate=SMALL,
        name="down",
    )(chip, near_act, far_act, near, far, hidden, *earlier)


def input_part_kernel(
    place_ref,
    near_ref,
    far_ref,
    near_weight_ref,
    far_weight_ref,
    rows_ref,
    gain_ref,
    hidden_ref,
    mlp_ref,
    head_ref,
    out_ref,
    mark_ref,
    total_ref,
    term_ref,
    sum_ref,
):
    step = pl.program_id(0)
    part = right_dot(near_ref[...], near_weight_ref[...])
    part = part + right_dot(far_ref[...], far_weight_ref[...])
    rows = rows_ref[...].astype(f32)
    inverse = inverse_rms(rows)
    gain = gain_ref[...]
    weighted = part * (rows * inverse)
    term = jnp.sum(weighted * gain, axis=1, keepdims=True) * (1.0 / D)
    term_ref[pl.ds(step, 1), :] = jnp.broadcast_to(term, (256, 128)).T[:1, :]
    sums = jnp.sum(weighted.reshape(32, 8, D), axis=0)

    @pl.when(step == 0)
    def _():
        sum_ref[...] = sums

    @pl.when(step > 0)
    def _():
        sum_ref[...] += sums

    total_ref[...] = part * (gain * inverse)
    hidden = hidden_ref[...]
    for span in range(2):
        own = pl.ds(pl.multiple_of(span * 128 + place_ref[0] * 16, 16), 16)
        total_ref[own, :] += hidden[span * 16 : span * 16 + 16, :]
    at = pl.ds(pl.multiple_of(step * 256, 256), 256)
    for index in range(8):
        cols = total_ref[:, index * 256 : index * 256 + 256]
        out_ref[index, at, :] = cols.astype(bf16)
    mark_ref[...] = total_ref[:, :256].astype(bf16)

    @pl.when(step == 1)
    def _():
        terms = term_ref[:2, :]
        coarse = terms.astype(bf16).astype(f32)
        totals = jnp.sum(sum_ref[...], axis=0, keepdims=True)
        extra = jnp.concatenate(
            [coarse, terms - coarse]
            + [totals[:, index * 256 : index * 256 + 256] for index in range(8)]
            + [mlp_ref[:, index * 256 : index * 256 + 256] for index in range(8)]
            + [head_ref[...], jnp.zeros((11, 256), f32)],
            axis=0,
        ).astype(bf16)
        for index in range(8):
            out_ref[index, 512:, :] = extra


def input_part(
    place, near, far, near_weight, far_weight, rows, gain, hidden, mlp, head, earlier
):
    def fixed(*shape):
        return pl.BlockSpec(shape, lambda i, place_ref: (0,) * len(shape))

    def tile(*shape):
        return pl.BlockSpec(shape, lambda i, place_ref: (i, 0))

    def own(*shape):
        return pl.BlockSpec(shape, lambda i, place_ref: (place_ref[1] * 2 + i, 0))

    return pl.pallas_call(
        ordered(input_part_kernel, 10, earlier),
        out_shape=(
            pltpu.HBM((8, 544, 256), bf16),
            jax.ShapeDtypeStruct((512, 256), bf16),
        ),
        grid_spec=pltpu.PrefetchScalarGridSpec(
            num_scalar_prefetch=1,
            grid=(2,),
            in_specs=[
                tile(256, 256),
                tile(256, 256),
                fixed(D, 256),
                fixed(D, 256),
                own(256, D),
                fixed(1, D),
                tile(32, D),
                fixed(1, D),
                fixed(1, 256),
                *unread(earlier),
            ],
            out_specs=(fixed(8, 544, 256), tile(256, 256)),
            scratch_shapes=[
                pltpu.VMEM((256, D), f32),
                pltpu.VMEM((8, 256), f32),
                pltpu.VMEM((8, D), f32),
            ],
        ),
        compiler_params=pltpu.CompilerParams(vmem_limit_bytes=28 * MIB),
        cost_estimate=SMALL,
        name="input_part",
    )(place, near, far, near_weight, far_weight, rows, gain, hidden, mlp, head, *earlier)


def attention_grads_kernel(normed_ref, grad_ref, grad_out_ref, out_ref, turned_ref):
    @pl.when(pl.program_id(0) == 0)
    def _():
        turned_ref[...] = grad_ref[...].T

    out_ref[0, :256, :] = plain_dot(turned_ref[...], normed_ref[...]).astype(bf16)
    out_ref[0, 256:, :] = grad_out_ref[...]


def attention_grads(normed, grad_proj, grad_out, earlier):
    return pl.pallas_call(
        ordered(attention_grads_kernel, 3, earlier),
        grid=(8,),
        out_shape=jax.ShapeDtypeStruct((8, 384, 256), bf16),
        in_specs=[
            pl.BlockSpec((ROWS, 256), lambda i: (0, i)),
            pl.BlockSpec((ROWS, 256), lambda i: (0, 0)),
            pl.BlockSpec((HD, 256), lambda i: (0, i)),
            *unread(earlier),
        ],
        out_specs=pl.BlockSpec((1, 384, 256), lambda i: (i % 4 * 2 + i // 4, 0, 0)),
        scratch_shapes=[pltpu.VMEM((256, ROWS), bf16)],
        compiler_params=pltpu.CompilerParams(vmem_limit_bytes=12 * MIB),
        cost_estimate=SMALL,
        name="attention_grads",
    )(normed, grad_proj, grad_out, *earlier)


def body(
    inputs,
    out_grad,
    lengths,
    span_order,
    w_query,
    w_key,
    w_value,
    w_out,
    w_gate,
    w_up,
    w_down,
    norm_attn,
    norm_mlp,
    norm_query,
    norm_key,
):
    xl, z, xh, y, core = (lax.axis_index(name) for name in ("xl", "z", "xh", "y", "c"))
    span_place = xl * 4 + z
    chip = xh * 4 + y
    first = core == 0

    def by_core(near, far, axis=0):
        join = jnp.stack if axis is None else lambda parts: jnp.concatenate(parts, axis=axis)
        return jnp.where(first, join([near, far]), join([far, near]))

    def split(block):
        near = lax.dynamic_slice_in_dim(block, core * 512, 512, 0)
        far = lax.dynamic_slice_in_dim(block, (1 - core) * 512, 512, 0)
        return near, far

    def chip_major(block):
        return block.reshape(4, 8, 16, -1).transpose(1, 0, 2, 3).reshape(512, -1)

    def span_major(block):
        return block.reshape(8, 4, 16, -1).transpose(1, 0, 2, 3).reshape(512, -1)

    gains = jnp.concatenate([norm_attn, norm_mlp, norm_query, norm_key])
    gains = jnp.pad(gains, (0, 16 * 256 - 544)).reshape(16, 256)
    spread_weights = exchange(pack(w_query, w_key, w_value, gains), SPANS)
    qkv_weights = spread_weights[:, :256].reshape(D, 256)
    gains = spread_weights[:, 256:259].reshape(8, 768).astype(f32)
    gain_attn = gains[:, :256].reshape(1, D)
    gain_mlp = gains[:, 256:512].reshape(1, D)
    gain_query = gains[:, 512:528].reshape(1, HD)
    gain_key = gains[:, 528:544].reshape(1, HD)
    key_half, value_half = qkv_weights[:, 128:192], qkv_weights[:, 192:256]
    other_half = swap(jnp.where(first, value_half, key_half))
    near_weight = jnp.where(
        first,
        jnp.concatenate([qkv_weights[:, :192], other_half], 1),
        jnp.concatenate([qkv_weights[:, :128], other_half, value_half], 1),
    )

    route, starts, low = routes(jnp.stack([span_place, xl, z]), lengths, span_order)

    def reorder(index, rows):
        return plain_dot(route[index], rows).astype(bf16)

    moving = lax.dynamic_index_in_dim(
        out_grad.reshape(8, 16, 8, D), chip * 2 + core, 1, keepdims=False
    ).reshape(64, D)
    moving = reorder(0, moving).reshape(8, 8, D)
    spread_out = jnp.broadcast_to(w_out.reshape(1, 16, D), (8, 16, D))
    moving = jnp.concatenate([moving, spread_out], axis=1)
    arrived = exchange(after(moving, qkv_weights), SPANS)
    out_weights = arrived[:, 8:].reshape(8, HD, 256)
    moving = arrived[:, :8].reshape(64, D)

    ends = jnp.cumsum(lax.dynamic_index_in_dim(lengths, xl, 0, keepdims=False))
    offset = z * ROWS + jnp.arange(ROWS, dtype=jnp.int32)
    doc_start = jnp.where(offset >= ends[1], ends[1], jnp.where(offset >= ends[0], ends[0], 0))
    frequency = jnp.power(rope_base, -2.0 * jnp.arange(HD // 2, dtype=f32) / HD)
    angles = (offset - doc_start).astype(f32)[:, None] * frequency[None, :]
    cos_table, sin_table = jnp.cos(angles), jnp.sin(angles)
    cos_table = jnp.concatenate([cos_table, cos_table], axis=1)
    sin_table = jnp.concatenate([-sin_table, sin_table], axis=1)

    normed, inverse_one, query_bf, own_kv, query_proj, kv_proj = project(
        core.reshape(1),
        in_hbm(inputs),
        gain_attn,
        near_weight,
        cos_table,
        sin_table,
        gain_query,
        gain_key,
    )
    ready_kv = after(own_kv, arrived)
    moving = after(reorder(1, moving), own_kv)
    moving = exchange(moving.reshape(8, 8, D), SPANS).reshape(64, D)
    moving = reorder(2, moving).reshape(8, 8, D)
    near = lax.dynamic_slice_in_dim(moving, core * 4, 4, 0)
    far = lax.dynamic_slice_in_dim(moving, (1 - core) * 4, 4, 0)
    own_grad = by_core(near, swap(far), 1).reshape(64, D)
    spread_grad = jnp.broadcast_to(own_grad[None], (8, 64, D))
    grad_mine = exchange(spread_grad, CHIPS)

    mine = jnp.concatenate(
        [onward(ready_kv, 3), onward(ready_kv, 2), onward(ready_kv, 1), own_kv], axis=0
    )
    mine = after(mine, spread_grad)
    other = swap(mine)
    all_keys = jnp.where(first, mine, other)
    all_values = jnp.where(first, other, mine)

    out_weights = out_weights.transpose(1, 0, 2).reshape(HD, D)
    out_two = jnp.concatenate([out_weights, swap(out_weights)], axis=0)

    mlp_shard = after(jnp.concatenate([w_gate, w_up, w_down.T], axis=1), qkv_weights)
    grad_fence = fence(spread_grad)
    far_shard = after(far_span(mlp_shard), mine, grad_fence)
    mlp_shard = jnp.where(
        xl == 0,
        jnp.concatenate([mlp_shard, far_shard]),
        jnp.concatenate([far_shard, mlp_shard]),
    )
    near_weights = lax.all_gather(mlp_shard, "z", axis=0, tiled=True)

    own_rows = lax.dynamic_slice_in_dim(inputs, core * 512, 512, 0).reshape(4, 8, 16, D)
    own_rows = lax.dynamic_index_in_dim(own_rows, chip, 1, keepdims=False).reshape(64, D)

    attended, attended_full, total = attend(
        low,
        starts,
        in_hbm(query_bf),
        in_hbm(all_keys),
        in_hbm(all_values),
        [grad_fence, out_two, mlp_shard, own_rows],
    )

    att_near, att_far = split(attended)
    att_near, att_far = after(chip_major(att_near), grad_mine), after(chip_major(att_far), grad_mine)
    att_two = jnp.concatenate([att_near, swap(att_far)], axis=1)
    branch = plain_dot(att_two, out_two).astype(bf16)
    branch = branch.reshape(8, 64, D)
    branch = exchange(branch, CHIPS)
    far_weights = swap(after(near_weights, branch))
    hidden, spread_normed = norm(branch, own_rows, gain_mlp)
    normed_mine = exchange(spread_normed, CHIPS)

    near_out, far_out, part = feed(normed_mine, grad_mine, near_weights, far_weights)
    mlp_grads = weights_grad(
        (normed_mine, swap(normed_mine)),
        (grad_mine, swap(grad_mine)),
        (near_out, swap(far_out)),
        [fence(part)],
    )
    part = exchange(part.reshape(8, 64, D), CHIPS)
    part, mlp_grads = lax.optimization_barrier((part, mlp_grads))
    def by_span(block):
        sent = lax.dynamic_index_in_dim(block, 1 - xl, 0, keepdims=False)
        return lax.dynamic_index_in_dim(block, xl, 0, keepdims=False), far_span(sent)

    mlp_grads = lax.psum_scatter(mlp_grads, "z", scatter_dimension=0, tiled=True)

    grad_hidden, gain_mlp_part, spread_branch = norm_grad(part, hidden, gain_mlp, own_grad)
    out_cols, out_mark = down(
        chip.reshape(1),
        near_out,
        far_out,
        near_weights,
        far_weights,
        hidden,
        [fence(spread_branch)],
    )
    far_weight = swap(near_weight)
    branch_mine = exchange(spread_branch, CHIPS).reshape(512, D)
    branch_mine = after(branch_mine, out_cols, far_weight)
    out_cols, out_mark = after(out_cols, branch_mine), after(out_mark, branch_mine)
    out_fence = swap(out_mark)
    out_cols = exchange(out_cols, CHIPS)
    grad_two = right_dot(branch_mine, out_two).astype(bf16)
    grad_att = by_core(span_major(grad_two[:, :HD]), span_major(swap(grad_two[:, HD:])))

    grad_query_rot, keep, send = attend_back(
        low,
        core.reshape(1),
        starts,
        in_hbm(query_bf),
        in_hbm(all_keys),
        in_hbm(all_values),
        grad_att,
        in_hbm(attended_full),
        total,
        [out_fence],
    )
    came = swap(send)
    own_kv_grad, *away = merge(keep, came)
    received = [backward(block, by + 1) for by, block in enumerate(away)]

    def unorder(index, rows):
        return left_dot(route[index], rows).astype(bf16)

    grad_out = left_dot(att_two, after(branch_mine, received[2])).astype(bf16)
    grad_out = (grad_out[:HD].astype(f32) + swap(grad_out[HD:]).astype(f32)).astype(bf16)
    grad_proj, head_gains = project_back(
        core.reshape(1),
        in_hbm(grad_query_rot),
        own_kv_grad,
        [in_hbm(block) for block in received],
        in_hbm(cos_table),
        in_hbm(sin_table),
        (in_hbm(query_proj), in_hbm(kv_proj)),
        (gain_query, gain_key),
        [in_hbm(mlp_grads), out_cols],
    )

    grad_near, grad_far = split(grad_proj)
    by_cols, mark = input_part(
        jnp.stack([chip, core]),
        grad_near,
        swap(grad_far),
        in_hbm(near_weight),
        in_hbm(far_weight),
        in_hbm(inputs),
        gain_attn,
        in_hbm(grad_hidden),
        gain_mlp_part,
        head_gains,
        [],
    )
    mlp_kept, mlp_came = by_span(after(mlp_grads, grad_proj))
    grad_attn = attention_grads(normed, grad_proj, grad_out, [swap(mark), mlp_came])
    out_cols = after(out_cols, grad_attn)
    grad_attn = grad_attn.reshape(4, 2, 384, 256)
    parts = [
        lax.dynamic_index_in_dim(grad_attn, (z + by) % 4, 0, keepdims=False) for by in range(4)
    ]
    parts = [parts[0]] + [
        lax.ppermute(parts[by], "z", [(i, (i + by) % 4) for i in range(4)]) for by in (1, 2, 3)
    ]
    out_cols = jnp.sum(out_cols.astype(f32), axis=0).astype(bf16)
    near = jnp.where(first, out_cols[:, :128], out_cols[:, 128:])
    far = jnp.where(first, out_cols[:, 128:], out_cols[:, :128])
    out_cols = by_core(near, swap(far), None).reshape(2, 8, 4, 2, 8, 128)
    out_rows = jnp.concatenate(
        [out_cols[:, index // 2, :, index % 2].reshape(64, 128) for index in range(16)], axis=1
    )

    by_cols = exchange(by_cols, CHIPS)

    class_rows = exchange(after(unorder(2, out_rows).reshape(8, 8, D), by_cols), SPANS)
    out_rows = class_rows
    parts = lax.optimization_barrier((*parts, by_cols))[:4]
    grad_attn = sum(part.astype(f32) for part in parts)
    attn_kept, attn_came = by_span(grad_attn.astype(bf16))
    by_cols = jnp.sum(by_cols.astype(f32), axis=0)
    row_term = (by_cols[512:514] + by_cols[514:516]).reshape(512, 1)
    own_inverse = lax.dynamic_slice_in_dim(inverse_one, core * 512, 512, 0)
    own_cols = lax.dynamic_slice(inputs, (core * 512, chip * 256), (512, 256)).astype(f32)
    in_grad = by_cols[:512] - own_cols * (own_inverse * own_inverse * row_term)
    near = jnp.where(first, in_grad[:, :128], in_grad[:, 128:])
    far = jnp.where(first, in_grad[:, 128:], in_grad[:, :128])
    in_grad = by_core(near, swap(far))
    gain_sums = jnp.concatenate(
        [
            by_cols[516:524],
            by_cols[524:532],
            by_cols[532, :128].reshape(8, 16),
            by_cols[532, 128:].reshape(8, 16),
        ],
        axis=1,
    )
    gain_sums = gain_sums + swap(gain_sums)
    coarse = gain_sums.astype(bf16)
    extra = jnp.concatenate(
        [coarse, (gain_sums - coarse.astype(f32)).astype(bf16), jnp.zeros((8, 960), bf16)], axis=1
    )
    extra = jnp.pad(extra[:, None], ((0, 0), (0, 7), (0, 0)))
    out_rows = unorder(1, out_rows.reshape(64, D)).reshape(8, 8, D)
    out_rows = after(jnp.concatenate([out_rows, extra], axis=1), attn_came)
    out_rows = exchange(out_rows, SPANS)
    gain_sums = jnp.sum(out_rows[:, 8].astype(f32), axis=0)
    gain_sums = gain_sums[:544] + gain_sums[544:1088]
    layer_out = unorder(0, out_rows[:, :8].reshape(64, D))
    layer_out = jnp.stack(
        [layer_out[:, at * 128 : at * 128 + 128].reshape(8, 8, 128) for at in range(16)],
        axis=1,
    )
    layer_out = layer_out.reshape(ROWS, 128).astype(f32)

    grad_attn = attn_kept.astype(f32) + attn_came.astype(f32)
    grad_kv_weight = grad_attn[128:256]
    low_half, high_half = grad_kv_weight[:64], grad_kv_weight[64:]
    came = swap(jnp.where(first, high_half, low_half))
    kept = jnp.where(first, low_half, high_half)
    mlp_kept, mlp_came = after(mlp_kept, class_rows), after(mlp_came, class_rows)
    mlp_grads = mlp_kept.astype(f32) + mlp_came.astype(f32)

    return (
        layer_out,
        in_grad,
        grad_attn[:128].T,
        jnp.where(first, kept, came).T,
        jnp.where(first, came, kept).T,
        grad_attn[256:],
        mlp_grads[:384].T,
        mlp_grads[384:768].T,
        mlp_grads[768:],
        gain_sums[:256],
        gain_sums[256:512],
        gain_sums[512:528],
        gain_sums[528:544],
    )


def solution(mesh):
    fine = Mesh(mesh.devices.reshape(2, 4, 2, 4, 2), ("xl", "z", "xh", "y", "c"))
    rows = P(SPANS, None)
    by_both = P(SPANS, TENSOR)
    turned = P(TENSOR, SPANS)
    lone = P(SPANS)
    return jax.shard_map(
        body,
        mesh=fine,
        in_specs=(
            rows,
            rows,
            P(),
            P(),
            by_both,
            by_both,
            by_both,
            turned,
            by_both,
            by_both,
            turned,
            lone,
            lone,
            lone,
            lone,
        ),
        out_specs=(
            by_both,
            by_both,
            by_both,
            by_both,
            by_both,
            turned,
            by_both,
            by_both,
            turned,
            lone,
            lone,
            lone,
            lone,
        ),
        check_vma=False,
    )
```
